32 devices in a mesh: tm: 8 (over z, x), stream: 2 (over core), head: 2 (over y).
Axes of the slice: x: 2, y: 2, z: 4, core: 2. Of those that a mesh axis runs over, the one named last changes fastest.
Arguments:
- residual_signal: bfloat16 [2, 8192, 1024], P('stream', 'tm', 'head'), may hold values from -12 to 12
- prescale_amplifier: float32 [2, 1024], P('stream'), may hold values from 0.1 to 1.9
- triple_projector: bfloat16 [2, 1024, 8, 384], P('stream', None, 'head'), may hold values from -0.1875 to 0.1875
- score_scaler: float32 [2, 8], P('stream', 'head'), may hold values from 2 to 5
- recall_retained_logshare: float32 [2, 8, 8192], P('stream', 'head', 'tm'), may hold values from -1.9 to 0
- tile_retain_grid: int32 [16, 2], P('tm'), may hold values 0 or 1
- recall_store_flags: int32 [16], P('tm'), may hold values 0 or 1
- emission_projector: bfloat16 [2, 8, 128, 1024], P('stream', 'head'), may hold values from -0.25 to 0.25
- sideways_coupling_coef: bfloat16 [2, 8, 128, 1024], P('stream', 'head'), may hold values from -0.25 to 0.25
Outputs:
- update: bfloat16 [2, 8192, 1024], P('stream', 'tm', 'head')
The draws below stay inside these ranges and needn't reach their ends.
All inputs are finite; a program needn't handle non-finite values. No bound on the sum of `tile_retain_grid` or of `recall_store_flags` on one device may be relied on, other than what follows from the above.
Results may differ from the reference program's by a relative error of at most 0.028.
Values may be sent and summed in bfloat16 or wider, within the bound.
No kernel may reach another device: no remote copies, remote signals or barrier semaphores. Data moves between devices by JAX's collectives and lax.ppermute only.
A program may use at most 64 MiB of HBM per device.

```python
import math
import jax
import jax.numpy as jnp
from jax import lax

BRANCH_FACETS = 8
HEAD_DIM = 128
D = 1024
TOK_DEV = 1024
BLOCK = 512
FRAME_TOKENS = 8192
NQB = 2
NBLK = 16
N_TM = 8
N_HEAD = 2


def draw_residual_signal(key, part):
    random_subkeys = jax.random.split(key, 2)
    row_scale = jnp.exp(jax.random.uniform(random_subkeys[0], (2, FRAME_TOKENS, 1), jnp.float32, math.log(0.3), math.log(3.0)))
    noise = jnp.clip(jax.random.normal(random_subkeys[1], (2, FRAME_TOKENS, D), jnp.float32), -3.0, 3.0)
    values = noise * row_scale
    return values.astype(jnp.bfloat16)


def draw_recall_retained_logshare(key, part):
    random_subkeys = jax.random.split(key, 5)
    odds = 2
    is_fast = jax.random.randint(random_subkeys[0], (2, BRANCH_FACETS, 1), 0, odds) == 0
    roughness = jax.random.uniform(random_subkeys[1], (2, BRANCH_FACETS, FRAME_TOKENS), jnp.float32, 0.5, 1.5)
    per_stretch = jnp.exp(jax.random.uniform(random_subkeys[2], (2, BRANCH_FACETS, FRAME_TOKENS // TOK_DEV, 1), jnp.float32, math.log(0.5), math.log(2.0)))
    per_stretch = jnp.broadcast_to(per_stretch, (2, BRANCH_FACETS, FRAME_TOKENS // TOK_DEV, TOK_DEV)).reshape(2, BRANCH_FACETS, FRAME_TOKENS)
    forget_rate = jnp.where(is_fast, 1.0 / 40.0, 0.2 / FRAME_TOKENS) * roughness * per_stretch
    flurry_places = jax.random.randint(random_subkeys[3], (2, BRANCH_FACETS, 3), 0, FRAME_TOKENS)
    flurry_depth = jax.random.uniform(random_subkeys[4], (2, BRANCH_FACETS, 3), jnp.float32, math.log(0.55), math.log(0.8))
    token_positions = jnp.arange(FRAME_TOKENS, dtype=jnp.int32)
    flurry_list = jnp.sum(jnp.where(token_positions[None, None, None, :] == flurry_places[..., None], flurry_depth[..., None], 0.0), axis=2)
    return (flurry_list - forget_rate).astype(jnp.float32)


def plant(result, rng, smallest, high):
    dims = result.shape
    spot = [jax.random.randint(jax.random.fold_in(rng, axis), (), 0, dims[axis]) for axis in range(len(dims))]
    result = result.at[tuple(spot)].set(smallest)
    longest = dims.index(max(dims))
    spot[longest] = (spot[longest] + 1) % dims[longest]
    return result.at[tuple(spot)].set(high)


def spiked(drawn, own_key, source, target, parts, factor):
    owner, partner = [(jnp.arange(drawn.shape[axis_at]) // (drawn.shape[axis_at] // parts)).reshape([-1 if axis == axis_at else 1 for axis in range(drawn.ndim)]) for axis_at in (source, target)]
    chosen = jax.random.permutation(own_key, parts)[partner]
    strong = (owner == chosen) | (owner == (partner + parts // 2) % parts)
    return jnp.where(strong, factor * drawn, drawn)


def shard_levels(own_key, dims, shards, least, high):
    loudness = 1.0
    for axis_at, shards_of in shards:
        steps = jax.random.uniform(jax.random.fold_in(jax.random.fold_in(own_key, 6), axis_at), (shards_of,), jnp.float32, least / len(shards), high / len(shards))
        loudness = loudness * jnp.repeat(jnp.exp(steps), dims[axis_at] // shards_of).reshape((-1,) + (1,) * (len(dims) - 1 - axis_at))
    return loudness


def centred(key, dims, spread, most, cuts=(), kind=jnp.bfloat16):
    entries = jax.random.normal(key, dims, jnp.float32) * spread
    if len(cuts) > 0:
        entries = shard_levels(key, dims, cuts, -0.22, 0.18) * entries
    return jnp.clip(entries, min=-most, max=most).astype(kind)


def noise_with(rng, extent, deviation, limit, cuts, heavy, kind=jnp.bfloat16):
    entries = deviation * jax.random.normal(rng, extent, jnp.float32)
    if cuts:
        entries = entries * shard_levels(rng, extent, cuts, -0.22, 0.18)
    return jnp.clip(spiked(entries, jax.random.fold_in(rng, 3), *heavy), -limit, limit).astype(kind)


def setup_inputs(seed: int = 0) -> dict:
    splits = jax.random.split(jax.random.key(seed), 10)
    return {
        "residual_signal": draw_residual_signal(jax.random.fold_in(splits[9], 71), 0),
        "prescale_amplifier": jnp.clip(1.0 + 0.18 * jax.random.normal(splits[1], (2, D), jnp.float32), 0.1, 1.9),
        "triple_projector": centred(splits[2], (2, D, BRANCH_FACETS, 3 * HEAD_DIM), D ** -0.5, 0.1875, ((0, 2), (2, 2))),
        "score_scaler": jnp.clip(jnp.exp(math.log(5.0) - 0.916290732 * jax.random.uniform(splits[3], (2, BRANCH_FACETS), jnp.float32) ** shard_levels(splits[3], (2, BRANCH_FACETS), ((0, 2), (1, 2)), -0.2, 0.2)), 2.0, 5.0),
        "recall_retained_logshare": draw_recall_retained_logshare(jax.random.fold_in(splits[9], 71), 0),
        "tile_retain_grid": plant((jax.random.randint(splits[5], (NBLK, NQB), 0, 4) < 3).astype(jnp.int32), jax.random.fold_in(splits[5], 1), 0, 1),
        "recall_store_flags": plant((jax.random.randint(splits[6], (NBLK,), 0, 4) < 3).astype(jnp.int32), jax.random.fold_in(splits[6], 1), 0, 1),
        "emission_projector": noise_with(splits[7], (2, BRANCH_FACETS, HEAD_DIM, D), D ** -0.5, 0.25, ((0, 2), (1, 2)), (1, 3, 2, 2.0)),
        "sideways_coupling_coef": noise_with(splits[8], (2, BRANCH_FACETS, HEAD_DIM, D), D ** -0.5, 0.25, ((0, 2), (1, 2)), (1, 3, 2, 2.0)),
    }


epsilon = 1e-06

def unit_rms(values):
    return values * lax.rsqrt(lax.optimization_barrier(jnp.mean(values * values, axis=-1, keepdims=True)) + epsilon)

def block_attention(asker_lines, probe_array_facets, content_array_facets, temper, keep_table):
    results = []
    for block_index in range(TOK_DEV // BLOCK):
        key_span = (block_index + 1) * BLOCK
        scores = jnp.einsum('qhd,khd->hqk', asker_lines[block_index * BLOCK:key_span].astype(jnp.float32), probe_array_facets[:key_span].astype(jnp.float32))
        scores = scores * (temper / math.sqrt(HEAD_DIM))[:, None, None]
        key_place = jnp.arange(key_span, dtype=jnp.int32)
        query_place = block_index * BLOCK + jnp.arange(BLOCK, dtype=jnp.int32)
        key_block = key_place // BLOCK
        earlier = (key_block < block_index) & (jnp.repeat(keep_table[block_index, :block_index + 1], BLOCK) == 1)
        diagonal = (key_block[None, :] == block_index) & (key_place[None, :] <= query_place[:, None])
        allowed = earlier[None, :] | diagonal
        powers = jnp.where(allowed[None], jnp.exp(scores), 0.0)
        totals = lax.optimization_barrier(jnp.sum(powers, axis=-1))
        weights = powers.astype(jnp.bfloat16)
        weighted = jnp.einsum('hqk,khd->qhd', weights.astype(jnp.float32), content_array_facets[:key_span].astype(jnp.float32))
        results.append(weighted / jnp.transpose(totals)[:, :, None])
    return jnp.concatenate(results, axis=0)

def branch_evaluate(frames_one, gain_one, weights_one, temper, keep_one, tile_retain_grid, recall_store_flags):
    stretch_rows = frames_one.reshape(N_TM, TOK_DEV, D)
    stretch_logs = jnp.transpose(keep_one.reshape(BRANCH_FACETS, N_TM, TOK_DEV), (1, 0, 2))
    stretch_keeps = tile_retain_grid.reshape(N_TM, TOK_DEV // BLOCK, TOK_DEV // BLOCK)
    stretch_picks = recall_store_flags.reshape(N_TM, TOK_DEV // BLOCK)
    matrix = weights_one.reshape(D, BRANCH_FACETS * 3 * HEAD_DIM)

    def one_stretch(item):
        rows_here, logs_here, keeps_here, picks_here = item
        inputs = rows_here.astype(jnp.float32)
        normed = (unit_rms(inputs) * gain_one).astype(jnp.bfloat16)
        projected = jnp.dot(normed, matrix, preferred_element_type=jnp.float32).reshape(TOK_DEV, BRANCH_FACETS, 3, HEAD_DIM)
        asker_lines = unit_rms(projected[:, :, 0]).astype(jnp.bfloat16)
        probe_array_facets = unit_rms(projected[:, :, 1]).astype(jnp.bfloat16)
        content_array_facets = projected[:, :, 2].astype(jnp.bfloat16)
        local_portion = block_attention(asker_lines, probe_array_facets, content_array_facets, temper, keeps_here)
        running = jnp.cumsum(logs_here, axis=1)
        chosen = jnp.repeat(picks_here, BLOCK).astype(jnp.float32)
        fading = jnp.exp(running[:, -1:] - running) * chosen[None, :]
        weighted_keys = jnp.transpose(probe_array_facets.astype(jnp.float32), (1, 0, 2)) * fading[:, :, None]
        summary = jnp.einsum('htd,the->hde', weighted_keys, content_array_facets.astype(jnp.float32), precision=lax.Precision.HIGHEST)
        return (asker_lines, local_portion, running, summary, jnp.exp(running[:, -1]))
    asker_lines, local_portion, running, summary, stretch_decay = lax.map(one_stretch, (stretch_rows, stretch_logs, stretch_keeps, stretch_picks))

    def advance(memory_state, item):
        summary_here, decay_here = item
        return (decay_here[:, None, None] * memory_state + summary_here, memory_state)
    _, memory = lax.scan(advance, jnp.zeros((BRANCH_FACETS, HEAD_DIM, HEAD_DIM), jnp.float32), (summary, stretch_decay))
    reading = jnp.einsum('cthd,chde->cthe', asker_lines.astype(jnp.float32), memory, precision=lax.Precision.HIGHEST)
    recalled = jnp.transpose(jnp.exp(running), (0, 2, 1))[..., None] * reading * (1.0 / math.sqrt(HEAD_DIM * FRAME_TOKENS))
    return (local_portion + recalled).astype(jnp.bfloat16).reshape(FRAME_TOKENS, BRANCH_FACETS, HEAD_DIM)

def grouped(head_out, weight_one):
    per_group = BRANCH_FACETS // N_HEAD
    summed = jnp.zeros((FRAME_TOKENS, D), jnp.float32)
    for group in range(N_HEAD):
        left_rows = head_out[:, group * per_group:(group + 1) * per_group].reshape(FRAME_TOKENS, per_group * HEAD_DIM)
        right_mat = weight_one[group * per_group:(group + 1) * per_group].reshape(per_group * HEAD_DIM, D)
        partial_sum = jnp.dot(left_rows, right_mat, preferred_element_type=jnp.float32)
        summed = summed + lax.optimization_barrier(partial_sum.astype(jnp.bfloat16)).astype(jnp.float32)
    return summed

def reference(residual_signal, prescale_amplifier, triple_projector, score_scaler, recall_retained_logshare, tile_retain_grid, recall_store_flags, emission_projector, sideways_coupling_coef):
    facet_result_lines = [branch_evaluate(residual_signal[branch_ordinal], prescale_amplifier[branch_ordinal], triple_projector[branch_ordinal], score_scaler[branch_ordinal], recall_retained_logshare[branch_ordinal], tile_retain_grid, recall_store_flags) for branch_ordinal in range(2)]
    updates = []
    for branch_ordinal in range(2):
        summed = grouped(facet_result_lines[branch_ordinal], emission_projector[branch_ordinal]) + grouped(facet_result_lines[1 - branch_ordinal], sideways_coupling_coef[1 - branch_ordinal])
        updates.append(summed.astype(jnp.bfloat16))
    return jnp.stack(updates)
```

```python
import functools
import math

import jax
import jax.numpy as jnp
from jax import lax
from jax.experimental import pallas as pl
from jax.experimental.pallas import tpu as pltpu
from jax.sharding import PartitionSpec as P

BLOCK = 512
TILE = 256
TAIL = 16
IN_CHUNKS = 2
OUT_CHUNKS = 4
EPSILON = 1e-06
F32 = jnp.float32
BF16 = jnp.bfloat16
SMEM = pl.BlockSpec(memory_space=pltpu.SMEM)


def params(mib):
    return pltpu.CompilerParams(vmem_limit_bytes=mib * 1024 * 1024)


def dot(a, b):
    return lax.dot_general(a, b, (((1,), (0,)), ((), ())), preferred_element_type=F32)


def dot_nt(a, b):
    return lax.dot_general(a, b, (((1,), (1,)), ((), ())), preferred_element_type=F32)


def dot_tn(a, b):
    return lax.dot_general(a, b, (((0,), (0,)), ((), ())), preferred_element_type=F32)


def unit(values):
    return values * lax.rsqrt(jnp.mean(values * values, axis=-1, keepdims=True) + EPSILON)


def whole(shape):
    return pl.BlockSpec(shape, lambda i: (0,) * len(shape))


def qkv_kernel(shards, heads, dim, first, last, *refs):
    me_ref, gain_ref, w_ref, fade_ref, tail_ref, prev_ref = refs[:6]
    x_refs = refs[6 : 6 + shards]
    q_ref, k_ref, v_ref, sum_ref = refs[6 + shards : 10 + shards]
    width = x_refs[0].shape[1]
    step = pl.program_id(0)

    @pl.when(step == 0)
    def _():
        if first:
            sum_ref[...] = jnp.zeros_like(sum_ref)
        else:
            sum_ref[...] = prev_ref[...]

    me = me_ref[0]
    parts = [x[...].astype(F32) for x in x_refs]
    squares = sum(jnp.sum(p * p, axis=-1, keepdims=True) for p in parts)
    scale = lax.rsqrt(squares * (1.0 / (width * shards)) + EPSILON)
    total = None
    for k in range(shards):
        owner = lax.rem(me + k, shards)
        rows = pl.ds(pl.multiple_of(owner * width, width), width)
        normed = (parts[k] * scale * gain_ref[:, rows]).astype(BF16)
        term = dot(normed, w_ref[rows, :])
        total = term if total is None else total + term
    for h in range(heads):
        base = h * 3 * dim
        cols = slice(h * dim, (h + 1) * dim)
        q_ref[:, cols] = unit(total[:, base : base + dim]).astype(BF16)
        key = unit(total[:, base + dim : base + 2 * dim]).astype(BF16)
        value = total[:, base + 2 * dim : base + 3 * dim].astype(BF16)
        k_ref[:, cols] = key
        v_ref[:, cols] = value
        faded = (key.astype(F32) * fade_ref[:, h : h + 1]).astype(BF16)
        sum_ref[h] += dot_tn(faded, value)
    if last:
        load_ref = refs[10 + shards]

        @pl.when(step == pl.num_programs(0) - 1)
        def _():
            for h in range(heads):
                load_ref[h, :dim, :] = sum_ref[h].astype(BF16)
                load_ref[h, dim:, :] = tail_ref[h]


def qkv(me, gain, w, fade, tail, prev, xs, heads, dim, first, last):
    shards = len(xs)
    rows, width = xs[0].shape
    tile = min(TILE, rows)
    by_rows = lambda cols: pl.BlockSpec((tile, cols), lambda i: (i, 0))
    out_shape = [jax.ShapeDtypeStruct((rows, heads * dim), BF16)] * 3
    out_shape.append(jax.ShapeDtypeStruct((heads, dim, dim), F32))
    out_specs = [by_rows(heads * dim)] * 3 + [whole((heads, dim, dim))]
    if last:
        out_shape.append(jax.ShapeDtypeStruct((heads, dim + TAIL, dim), BF16))
        out_specs.append(whole((heads, dim + TAIL, dim)))
    return pl.pallas_call(
        functools.partial(qkv_kernel, shards, heads, dim, first, last),
        grid=(rows // tile,),
        in_specs=[
            SMEM,
            whole(gain.shape),
            whole(w.shape),
            by_rows(heads),
            whole(tail.shape),
            whole(prev.shape),
        ]
        + [by_rows(width)] * shards,
        out_specs=out_specs,
        out_shape=out_shape,
        compiler_params=params(40),
        cost_estimate=pl.CostEstimate(
            flops=2 * rows * w.shape[0] * w.shape[1], bytes_accessed=w.size * 2, transcendentals=0
        ),
        name="qkv",
    )(me, gain, w, fade, tail, prev, *xs)


def attention_kernel(pieces, head0, keep_ref, scale_ref, *refs):
    q_refs, k_refs, v_refs = refs[:pieces], refs[pieces : 2 * pieces], refs[2 * pieces : 3 * pieces]
    out_ref = refs[3 * pieces]
    scale = scale_ref[0, head0 + pl.program_id(0)]
    dim = out_ref.shape[1]
    joined = lambda rs: jnp.concatenate([r[...] for r in rs], axis=0)
    q, k, v = joined(q_refs), joined(k_refs), joined(v_refs)
    v = jnp.concatenate([v, jnp.ones_like(v)], axis=1)
    length = q.shape[0]
    per = BLOCK // TILE
    row = lax.broadcasted_iota(jnp.int32, (TILE, TILE), 0)
    col = lax.broadcasted_iota(jnp.int32, (TILE, TILE), 1)
    causal = col <= row
    for t in range(length // TILE):
        block = t // per
        mine = q[t * TILE : (t + 1) * TILE]
        span = slice(t * TILE, (t + 1) * TILE)
        powers = jnp.where(causal, jnp.exp(dot_nt(mine, k[span]) * scale), 0.0)
        total = dot(powers.astype(BF16), v[span])
        if t > block * per:
            span = slice(block * BLOCK, t * TILE)
            powers = jnp.exp(dot_nt(mine, k[span]) * scale)
            total += dot(powers.astype(BF16), v[span])
        for j in range(block):
            span = slice(j * BLOCK, (j + 1) * BLOCK)
            powers = jnp.exp(dot_nt(mine, k[span]) * scale)
            part = dot(powers.astype(BF16), v[span])
            total += jnp.where(keep_ref[block, j] == 1, part, 0.0)
        out_ref[t * TILE : (t + 1) * TILE, :] = (total[:, :dim] / total[:, dim:]).astype(BF16)


def attention(keep, scale, qs, ks, vs, head0, heads, dim):
    pieces = len(qs)
    length = sum(q.shape[0] for q in qs)
    spec = lambda rows: pl.BlockSpec((rows, dim), lambda h: (0, head0 + h))
    return pl.pallas_call(
        functools.partial(attention_kernel, pieces, head0),
        grid=(heads,),
        in_specs=[SMEM, SMEM] + [spec(a.shape[0]) for a in (*qs, *ks, *vs)],
        out_specs=pl.BlockSpec((length, dim), lambda h: (0, h)),
        out_shape=jax.ShapeDtypeStruct((length, heads * dim), BF16),
        compiler_params=params(40),
        cost_estimate=pl.CostEstimate(
            flops=heads * 3 * length * length * dim,
            bytes_accessed=heads * length * dim * 8,
            transcendentals=heads * length * length,
        ),
        name="attention",
    )(keep, scale, *qs, *ks, *vs)


def opened(ref, h, dim):
    body = ref[h, :dim, :].astype(F32)
    decay = ref[h, dim : dim + 1, :].astype(F32) + ref[h, dim + TAIL // 2 : dim + TAIL // 2 + 1, :].astype(F32)
    return body, decay


def pair_kernel(heads, dim, odd_ref, mine_ref, other_ref, out_ref):
    odd = odd_ref[0] == 1
    for h in range(heads):
        own, own_decay = opened(mine_ref, h, dim)
        far, far_decay = opened(other_ref, h, dim)
        early, late = jnp.where(odd, far, own), jnp.where(odd, own, far)
        late_decay = jnp.where(odd, own_decay, far_decay)
        both = own_decay * far_decay
        out_ref[h, :dim, :] = (late_decay * early + late).astype(BF16)
        high = both.astype(BF16)
        low = (both - high.astype(F32)).astype(BF16)
        out_ref[h, dim : dim + TAIL // 2, :] = jnp.broadcast_to(high, (TAIL // 2, dim))
        out_ref[h, dim + TAIL // 2 :, :] = jnp.broadcast_to(low, (TAIL // 2, dim))


def pair(odd, mine, other):
    heads, _, dim = mine.shape
    return pl.pallas_call(
        functools.partial(pair_kernel, heads, dim),
        in_specs=[SMEM] + [pl.BlockSpec(memory_space=pltpu.VMEM)] * 2,
        out_specs=pl.BlockSpec(memory_space=pltpu.VMEM),
        out_shape=jax.ShapeDtypeStruct(mine.shape, BF16),
        cost_estimate=pl.CostEstimate(flops=mine.size, bytes_accessed=mine.size * 6, transcendentals=0),
        name="pair",
    )(odd, mine, other)


def recall_kernel(count, groups, heads, dim, paired, odd_ref, gain_ref, q_ref, *refs):
    local_refs, refs = refs[:groups], refs[groups:]
    other_ref, far_refs = refs[0], refs[1 : 1 + count]
    out_ref = refs[1 + count]
    per = heads // groups
    for h in range(heads):
        state = None
        for ref in reversed(far_refs):
            body, decay = opened(ref, h, dim)
            state = body if state is None else body + decay * state
        if paired:
            body, decay = opened(other_ref, h, dim)
            later = body if state is None else decay * state + body
            first = jnp.zeros_like(body) if state is None else state
            state = jnp.where(odd_ref[0] == 1, later, first)
        if state is None:
            state = jnp.zeros((dim, dim), F32)
        cols = slice(h * dim, (h + 1) * dim)
        recalled = dot(q_ref[:, cols], state.astype(BF16)) * gain_ref[:, h : h + 1]
        local = local_refs[h // per][:, h % per * dim : (h % per + 1) * dim]
        out_ref[:, cols] = (local.astype(F32) + recalled).astype(BF16)


def recall(odd, gain, q, locals_, other, fars, index, chunk, q_index, paired):
    heads, _, dim = other.shape
    groups = len(locals_)
    rows = lambda cols, at: pl.BlockSpec((chunk, cols), lambda i: (at, 0))
    load = whole(other.shape)
    return pl.pallas_call(
        functools.partial(recall_kernel, len(fars), groups, heads, dim, paired),
        grid=(1,),
        in_specs=[SMEM, rows(heads, index), rows(heads * dim, q_index)]
        + [rows(heads // groups * dim, index)] * groups
        + [load] * (1 + len(fars)),
        out_specs=pl.BlockSpec((chunk, heads * dim), lambda i: (0, 0)),
        out_shape=jax.ShapeDtypeStruct((chunk, heads * dim), BF16),
        compiler_params=params(40),
        cost_estimate=pl.CostEstimate(
            flops=2 * chunk * heads * dim * dim, bytes_accessed=chunk * heads * dim * 6, transcendentals=0
        ),
        name="recall",
    )(odd, gain, q, *locals_, other, *fars)


def project_kernel(shards, me_ref, own_ref, side_ref, own_w_ref, side_w_ref, *out_refs):
    width = out_refs[0].shape[1]
    own, side = own_ref[...], side_ref[...]
    for k in reversed(range(shards)):
        owner = lax.rem(me_ref[0] + k, shards)
        cols = pl.ds(pl.multiple_of(owner * width, width), width)
        out = dot(own, own_w_ref[:, cols]) + dot(side, side_w_ref[:, cols])
        out_refs[k][...] = out.astype(out_refs[k].dtype)


def project(me, own, side, own_w, side_w, shards):
    rows = own.shape[0]
    width = own_w.shape[1] // shards
    vmem = pl.BlockSpec(memory_space=pltpu.VMEM)
    return pl.pallas_call(
        functools.partial(project_kernel, shards),
        in_specs=[SMEM] + [vmem] * 4,
        out_specs=[vmem] * shards,
        out_shape=[jax.ShapeDtypeStruct((rows, width), BF16)] * shards,
        compiler_params=params(40),
        cost_estimate=pl.CostEstimate(
            flops=4 * rows * own_w.size, bytes_accessed=own_w.size * 4, transcendentals=0
        ),
        name="project",
    )(me, own, side, own_w, side_w)


def per_device(
    residual_signal,
    prescale_amplifier,
    triple_projector,
    score_scaler,
    recall_retained_logshare,
    tile_retain_grid,
    recall_store_flags,
    emission_projector,
    sideways_coupling_coef,
):
    x = residual_signal[0]
    length = x.shape[0]
    shards = lax.axis_size("head")
    blocks = lax.axis_size("tm")
    heads = triple_projector.shape[2]
    dim = emission_projector.shape[2]
    me = lax.axis_index("head").astype(jnp.int32).reshape(1)
    place = lax.axis_index("tm")
    paired = blocks % 2 == 0
    odd = (place % 2 if paired else place * 0).astype(jnp.int32).reshape(1)
    swap_streams = [(0, 1), (1, 0)]

    in_rows = length // IN_CHUNKS
    received = []
    for c in range(IN_CHUNKS):
        piece = x[c * in_rows : (c + 1) * in_rows]
        xs = [piece]
        for k in range(1, shards):
            xs.append(lax.ppermute(piece, "head", [((d + k) % shards, d) for d in range(shards)]))
        received.append(xs)

    own_w = emission_projector[0].reshape(heads * dim, -1)
    side_mine = sideways_coupling_coef[0].reshape(heads * dim, -1)
    side_w = lax.ppermute(side_mine, "stream", swap_streams)

    running = jnp.cumsum(recall_retained_logshare[0], axis=1)
    flags = jnp.repeat(recall_store_flags, BLOCK).astype(F32)
    fade = jnp.transpose(jnp.exp(running[:, -1:] - running) * flags[None, :])
    reading = jnp.transpose(jnp.exp(running)) * (1.0 / math.sqrt(dim * length * blocks))
    decay = jnp.exp(running[:, -1])
    high = decay.astype(BF16)
    low = (decay - high.astype(F32)).astype(BF16)
    tail = jnp.concatenate(
        [jnp.broadcast_to(part[:, None, None], (heads, TAIL // 2, dim)) for part in (high, low)], axis=1
    )
    scale = score_scaler * (1.0 / math.sqrt(dim))
    gain = prescale_amplifier
    w = triple_projector[0].reshape(triple_projector.shape[1], -1)

    qs, ks, vs = [], [], []
    summary = jnp.zeros((heads, dim, dim), F32)
    for c in range(IN_CHUNKS):
        last = c == IN_CHUNKS - 1
        results = qkv(
            me,
            gain,
            w,
            fade[c * in_rows : (c + 1) * in_rows],
            tail,
            summary,
            received[c],
            heads,
            dim,
            c == 0,
            last,
        )
        qs.append(results[0])
        ks.append(results[1])
        vs.append(results[2])
        summary = results[3]
    mine = results[4]

    other, joint, step = mine, mine, 1
    if paired:
        step = 2
        other = lax.ppermute(mine, "tm", [(d, d ^ 1) for d in range(blocks)])
        joint = pair(odd, mine, other)
    fars = [
        lax.ppermute(joint, "tm", [(d, d + k) for d in range(blocks - k)])
        for k in range(step, blocks, step)
    ]

    groups = 2 if heads % 2 == 0 else 1
    per = heads // groups
    locals_ = [
        attention(tile_retain_grid, scale, qs, ks, vs, g * per, per, dim) for g in range(groups)
    ]

    chunk = length // OUT_CHUNKS
    per_piece = in_rows // chunk
    done = []
    for c in range(OUT_CHUNKS):
        head_out = recall(
            odd, reading, qs[c // per_piece], locals_, other, fars, c, chunk, c % per_piece, paired
        )
        side = lax.ppermute(head_out, "stream", swap_streams)
        outs = project(me, head_out, side, own_w, side_w, shards)
        total = outs[0].astype(F32)
        for k in range(1, shards):
            total += lax.ppermute(
                outs[k], "head", [(d, (d + k) % shards) for d in range(shards)]
            ).astype(F32)
        done.append(total.astype(BF16))
    return jnp.concatenate(done, axis=0)[None]


def solution(mesh):
    placed = (
        P("stream", "tm", "head"),
        P("stream", None),
        P("stream", None, "head", None),
        P("stream", "head"),
        P("stream", "head", "tm"),
        P("tm", None),
        P("tm"),
        P("stream", "head", None, None),
        P("stream", "head", None, None),
    )
    return jax.shard_map(
        per_device, mesh=mesh, in_specs=placed, out_specs=P("stream", "tm", "head"), check_vma=False
    )
```

```python
import functools
import math

import jax
import jax.numpy as jnp
from jax import lax
from jax.experimental import pallas as pl
from jax.experimental.pallas import tpu as pltpu
from jax.sharding import PartitionSpec as P

BLOCK = 512
CHUNK = 256
TAIL = 16
EPSILON = 1e-06
F32 = jnp.float32
BF16 = jnp.bfloat16
SMEM = pl.BlockSpec(memory_space=pltpu.SMEM)
VMEM = pl.BlockSpec(memory_space=pltpu.VMEM)


def params():
    return pltpu.CompilerParams(vmem_limit_bytes=16 * 1024 * 1024)


def cost(flops, bytes_accessed, transcendentals=0):
    return pl.CostEstimate(
        flops=int(flops), bytes_accessed=int(bytes_accessed), transcendentals=int(transcendentals)
    )


def struct(shape, dtype=BF16):
    return jax.ShapeDtypeStruct(shape, dtype)


def dot(a, b):
    return lax.dot_general(a, b, (((1,), (0,)), ((), ())), preferred_element_type=F32)


def dot_nt(a, b):
    return lax.dot_general(a, b, (((1,), (1,)), ((), ())), preferred_element_type=F32)


def dot_tn(a, b):
    return lax.dot_general(a, b, (((0,), (0,)), ((), ())), preferred_element_type=F32)


def unit(values):
    return values * lax.rsqrt(jnp.mean(values * values, axis=-1, keepdims=True) + EPSILON)


def normed_parts(me, gain_ref, x_refs):
    shards, width = len(x_refs), x_refs[0].shape[1]
    parts = [x[...].astype(F32) for x in x_refs]
    squares = sum(jnp.sum(p * p, axis=-1, keepdims=True) for p in parts)
    scale = lax.rsqrt(squares * (1.0 / (width * shards)) + EPSILON)
    out = []
    for k, part in enumerate(parts):
        owner = lax.rem(me + k, shards)
        rows = pl.ds(pl.multiple_of(owner * width, width), width)
        out.append(((part * scale * gain_ref[:, rows]).astype(BF16), rows))
    return out


def projected(parts, w_ref, cols):
    total = None
    for part, rows in parts:
        term = dot(part, w_ref[rows, cols])
        total = term if total is None else total + term
    return total


def write_queries(parts, w_ref, q_ref, heads, dim):
    total = projected(parts, w_ref, slice(0, heads * dim))
    for h in range(heads):
        cols = slice(h * dim, (h + 1) * dim)
        q_ref[:, cols] = unit(total[:, cols]).astype(BF16)


def write_keys_values(parts, w_ref, fade_ref, k_ref, v_ref, sum_ref, heads, dim):
    keys = projected(parts, w_ref, slice(heads * dim, 2 * heads * dim))
    values = projected(parts, w_ref, slice(2 * heads * dim, 3 * heads * dim))
    for h in range(heads):
        cols = slice(h * dim, (h + 1) * dim)
        key = unit(keys[:, cols]).astype(BF16)
        value = values[:, cols].astype(BF16)
        k_ref[:, cols] = key
        v_ref[:, cols] = value
        faded = (key.astype(F32) * fade_ref[:, h : h + 1]).astype(BF16)
        sum_ref[h] += dot_tn(faded, value)


def qkv_kernel(heads, dim, me_ref, gain_ref, w_ref, fade_ref, prev_ref, *refs):
    x_refs, (q_ref, k_ref, v_ref, sum_ref) = refs[:-4], refs[-4:]
    sum_ref[...] = prev_ref[...]
    parts = normed_parts(me_ref[0], gain_ref, x_refs)
    write_keys_values(parts, w_ref, fade_ref, k_ref, v_ref, sum_ref, heads, dim)
    write_queries(parts, w_ref, q_ref, heads, dim)


def qkv(me, gain, w, fade, prev, xs, heads, dim):
    rows = xs[0].shape[0]
    return pl.pallas_call(
        functools.partial(qkv_kernel, heads, dim),
        in_specs=[SMEM] + [VMEM] * (4 + len(xs)),
        out_specs=[VMEM] * 4,
        out_shape=[struct((rows, heads * dim))] * 3 + [struct((heads, dim, dim), F32)],
        compiler_params=params(),
        cost_estimate=cost(4 * rows * w.size, 0),
        name="qkv",
    )(me, gain, w, fade, prev, *xs)


def last_kernel(heads, dim, me_ref, odd_ref, gain_ref, w_ref, fade_ref, prev_ref, tail_ref, *refs):
    x_refs, (k_ref, v_ref, keep_ref, send_ref, sum_ref) = refs[:-5], refs[-5:]
    half = dim // 2
    sum_ref[...] = prev_ref[...]
    parts = normed_parts(me_ref[0], gain_ref, x_refs)
    write_keys_values(parts, w_ref, fade_ref, k_ref, v_ref, sum_ref, heads, dim)
    odd = odd_ref[0]
    kept = pl.ds(pl.multiple_of(odd * half, half), half)
    sent = pl.ds(pl.multiple_of((1 - odd) * half, half), half)
    for h in range(heads):
        rows = slice(h * half, (h + 1) * half)
        keep_ref[rows, :] = sum_ref[h, kept, :]
        send_ref[rows, :] = sum_ref[h, sent, :].astype(BF16)
    send_ref[heads * half :, :] = tail_ref[...]


def last_keys_values(me, odd, gain, w, fade, prev, tail, xs, heads, dim):
    rows = xs[0].shape[0]
    size = heads * dim // 2
    return pl.pallas_call(
        functools.partial(last_kernel, heads, dim),
        in_specs=[SMEM, SMEM] + [VMEM] * (5 + len(xs)),
        out_specs=[VMEM] * 4,
        out_shape=[struct((rows, heads * dim))] * 2 + [struct((size, dim), F32), struct((size + TAIL, dim))],
        scratch_shapes=[pltpu.VMEM((heads, dim, dim), F32)],
        compiler_params=params(),
        cost_estimate=cost(3 * rows * w.size, 0),
        name="last_keys_values",
    )(me, odd, gain, w, fade, prev, tail, *xs)


def queries_kernel(heads, dim, me_ref, gain_ref, w_ref, *refs):
    parts = normed_parts(me_ref[0], gain_ref, refs[:-1])
    write_queries(parts, w_ref, refs[-1], heads, dim)


def last_queries(me, gain, w, xs, heads, dim):
    rows = xs[0].shape[0]
    return pl.pallas_call(
        functools.partial(queries_kernel, heads, dim),
        in_specs=[SMEM] + [VMEM] * (2 + len(xs)),
        out_specs=VMEM,
        out_shape=struct((rows, heads * dim)),
        compiler_params=params(),
        cost_estimate=cost(2 * rows * w.size, 0),
        name="last_queries",
    )(me, gain, w, *xs)


def attention_kernel(chunk, heads, dim, keep_ref, scale_ref, q_ref, *refs):
    k_refs, v_refs, out_ref = refs[: chunk + 1], refs[chunk + 1 : -1], refs[-1]
    rows = q_ref.shape[0]
    per = BLOCK // rows
    block = chunk // per
    causal = lax.broadcasted_iota(jnp.int32, (rows, rows), 1) <= lax.broadcasted_iota(
        jnp.int32, (rows, rows), 0
    )
    ones = jnp.ones((rows, dim), BF16)
    for h in range(heads):
        cols = slice(h * dim, (h + 1) * dim)
        query = q_ref[:, cols]
        total = None
        for j in range(chunk + 1):
            powers = jnp.exp(dot_nt(query, k_refs[j][:, cols]) * scale_ref[0, h])
            if j == chunk:
                powers = jnp.where(causal, powers, 0.0)
            part = dot(powers.astype(BF16), jnp.concatenate([v_refs[j][:, cols], ones], axis=1))
            if j // per < block:
                part = jnp.where(keep_ref[block, j // per] == 1, part, 0.0)
            total = part if total is None else total + part
        out_ref[:, cols] = (total[:, :dim] / total[:, dim:]).astype(BF16)


def attention(chunk, keep, scale, q, ks, vs, heads, dim):
    rows = q.shape[0]
    return pl.pallas_call(
        functools.partial(attention_kernel, chunk, heads, dim),
        in_specs=[SMEM, SMEM] + [VMEM] * (1 + len(ks) + len(vs)),
        out_specs=VMEM,
        out_shape=struct(q.shape),
        compiler_params=params(),
        cost_estimate=cost(
            (chunk + 1) * heads * 8 * rows * rows * dim, 0, (chunk + 1) * heads * rows * rows
        ),
        name="attention",
    )(keep, scale, q, *ks, *vs)


def decays_of(ref, size, h):
    high = ref[size + h : size + h + 1, :].astype(F32)
    low = ref[size + TAIL // 2 + h : size + TAIL // 2 + h + 1, :].astype(F32)
    return high + low


def pair_kernel(heads, odd_ref, tail_ref, keep_ref, came_ref, out_ref):
    size = keep_ref.shape[0]
    half = size // heads
    odd = odd_ref[0] == 1
    out_ref[size:, :] = jnp.zeros_like(tail_ref)
    for h in range(heads):
        rows = slice(h * half, (h + 1) * half)
        own, far = keep_ref[rows, :], came_ref[rows, :].astype(F32)
        own_decay, far_decay = decays_of(tail_ref, 0, h), decays_of(came_ref, size, h)
        late_decay = jnp.where(odd, own_decay, far_decay)
        early, late = jnp.where(odd, far, own), jnp.where(odd, own, far)
        out_ref[rows, :] = (late_decay * early + late).astype(BF16)
        both = own_decay * far_decay
        high = both.astype(BF16)
        out_ref[size + h : size + h + 1, :] = high
        out_ref[size + TAIL // 2 + h : size + TAIL // 2 + h + 1, :] = (both - high.astype(F32)).astype(BF16)


def pair(odd, tail, keep, came, heads):
    return pl.pallas_call(
        functools.partial(pair_kernel, heads),
        in_specs=[SMEM] + [VMEM] * 3,
        out_specs=VMEM,
        out_shape=struct(came.shape),
        compiler_params=params(),
        cost_estimate=cost(came.size * 8, 0),
        name="pair",
    )(odd, tail, keep, came)


def entering_kernel(heads, odd_ref, tail_ref, keep_ref, came_ref, *refs):
    far_refs, (stay_ref, send_ref) = refs[:-2], refs[-2:]
    size = keep_ref.shape[0]
    half = size // heads
    odd = odd_ref[0] == 1
    for h in range(heads):
        rows = slice(h * half, (h + 1) * half)
        state = jnp.zeros((half, keep_ref.shape[1]), F32)
        for ref in reversed(far_refs):
            state = ref[rows, :].astype(F32) + decays_of(ref, size, h) * state
        own, far = keep_ref[rows, :], came_ref[rows, :].astype(F32)
        decay = jnp.where(odd, decays_of(came_ref, size, h), decays_of(tail_ref, 0, h))
        later = decay * state + jnp.where(odd, far, own)
        stay_ref[rows, :] = jnp.where(odd, later, state).astype(BF16)
        send_ref[rows, :] = jnp.where(odd, state, later).astype(BF16)


def entering(odd, tail, keep, came, fars, heads):
    return pl.pallas_call(
        functools.partial(entering_kernel, heads),
        in_specs=[SMEM] + [VMEM] * (3 + len(fars)),
        out_specs=[VMEM] * 2,
        out_shape=[struct(keep.shape)] * 2,
        compiler_params=params(),
        cost_estimate=cost(came.size * 16, 0),
        name="entering",
    )(odd, tail, keep, came, *fars)


def recall_kernel(heads, dim, odd_ref, reading_ref, q_ref, local_ref, stay_ref, came_ref, out_ref):
    half = dim // 2
    odd = odd_ref[0] == 1
    for h in range(heads):
        rows = slice(h * half, (h + 1) * half)
        cols = slice(h * dim, (h + 1) * dim)
        stay, came = stay_ref[rows, :].astype(F32), came_ref[rows, :].astype(F32)
        state = jnp.concatenate([jnp.where(odd, came, stay), jnp.where(odd, stay, came)], axis=0)
        recalled = dot(q_ref[:, cols], state.astype(BF16)) * reading_ref[:, h : h + 1]
        out_ref[:, cols] = (local_ref[:, cols].astype(F32) + recalled).astype(BF16)


def recall(odd, reading, q, local, stay, came, heads, dim):
    return pl.pallas_call(
        functools.partial(recall_kernel, heads, dim),
        in_specs=[SMEM] + [VMEM] * 5,
        out_specs=VMEM,
        out_shape=struct(q.shape),
        compiler_params=params(),
        cost_estimate=cost(4 * q.size * dim, 0),
        name="recall",
    )(odd, reading, q, local, stay, came)


def project_kernel(shards, me_ref, own_ref, side_ref, own_w_ref, side_w_ref, *out_refs):
    width = out_refs[0].shape[1]
    own, side = own_ref[...], side_ref[...]
    for k in reversed(range(shards)):
        owner = lax.rem(me_ref[0] + k, shards)
        cols = pl.ds(pl.multiple_of(owner * width, width), width)
        out = dot(own, own_w_ref[:, cols]) + dot(side, side_w_ref[:, cols])
        out_refs[k][...] = out.astype(out_refs[k].dtype)


def project(me, own, side, own_w, side_w, shards):
    rows = own.shape[0]
    width = own_w.shape[1] // shards
    return pl.pallas_call(
        functools.partial(project_kernel, shards),
        in_specs=[SMEM] + [VMEM] * 4,
        out_specs=[VMEM] * shards,
        out_shape=[struct((rows, width))] * shards,
        compiler_params=params(),
        cost_estimate=cost(4 * rows * own_w.size, 0),
        name="project",
    )(me, own, side, own_w, side_w)


def finish_kernel(count, *refs):
    total = refs[0][...].astype(F32)
    for ref in refs[1:count]:
        total += ref[...].astype(F32)
    refs[-1][...] = total.astype(BF16)


def finish(parts, result, chunk, length):
    rows, width = parts[0].shape
    whole = pl.BlockSpec((rows, width), lambda i: (0, 0))
    more = [] if result is None else [result]
    return pl.pallas_call(
        functools.partial(finish_kernel, len(parts)),
        grid=(1,),
        in_specs=[whole] * len(parts) + [pl.BlockSpec(memory_space=pl.ANY)] * len(more),
        out_specs=pl.BlockSpec((rows, width), lambda i: (chunk, 0)),
        out_shape=struct((length, width)),
        input_output_aliases={len(parts): 0} if more else {},
        compiler_params=params(),
        cost_estimate=cost(rows * width * 2, rows * width * 6),
        name="finish",
    )(*parts, *more)


def per_device(
    residual_signal,
    prescale_amplifier,
    triple_projector,
    score_scaler,
    recall_retained_logshare,
    tile_retain_grid,
    recall_store_flags,
    emission_projector,
    sideways_coupling_coef,
):
    x = residual_signal[0]
    length = x.shape[0]
    chunks = length // CHUNK
    shards = lax.axis_size("head")
    blocks = lax.axis_size("tm")
    heads = triple_projector.shape[2]
    dim = emission_projector.shape[2]
    me = lax.axis_index("head").astype(jnp.int32).reshape(1)
    odd = lax.rem(lax.axis_index("tm"), 2).astype(jnp.int32).reshape(1)
    swap_streams = [(0, 1), (1, 0)]
    swap_pairs = [(d, d ^ 1) for d in range(blocks)]

    received = []
    for c in range(chunks):
        piece = x[c * CHUNK : (c + 1) * CHUNK]
        piece, x = lax.optimization_barrier((piece, x))
        xs = [piece]
        for k in range(1, shards):
            xs.append(lax.ppermute(piece, "head", [((d + k) % shards, d) for d in range(shards)]))
        received.append(xs)

    own_w = emission_projector[0].reshape(heads * dim, -1)
    side_w = lax.ppermute(
        sideways_coupling_coef[0].reshape(heads * dim, -1), "stream", swap_streams
    )

    running = jnp.cumsum(recall_retained_logshare[0], axis=1)
    flags = jnp.repeat(recall_store_flags, BLOCK).astype(F32)
    fade = jnp.transpose(jnp.exp(running[:, -1:] - running) * flags[None, :])
    reading = jnp.transpose(jnp.exp(running)) * (1.0 / math.sqrt(dim * length * blocks))
    decay = jnp.exp(running[:, -1])
    high = decay.astype(BF16)
    low = (decay - high.astype(F32)).astype(BF16)
    tail = jnp.concatenate(
        [
            jnp.broadcast_to(jnp.pad(part, (0, TAIL // 2 - heads))[:, None], (TAIL // 2, dim))
            for part in (high, low)
        ],
        axis=0,
    )
    scale = score_scaler * (1.0 / math.sqrt(dim))
    gain = prescale_amplifier
    w = triple_projector[0].reshape(-1, heads, 3, dim)
    w = jnp.transpose(w, (0, 2, 1, 3)).reshape(-1, 3 * heads * dim)
    rows_of = lambda array, c: array[c * CHUNK : (c + 1) * CHUNK]

    qs, ks, vs, locals_ = [], [], [], []
    summary = jnp.zeros((heads, dim, dim), F32)
    for c in range(chunks - 1):
        q, k, v, summary = qkv(me, gain, w, rows_of(fade, c), summary, received[c], heads, dim)
        qs.append(q)
        ks.append(k)
        vs.append(v)
        locals_.append(attention(c, tile_retain_grid, scale, q, ks, vs, heads, dim))
    k, v, keep, sent = last_keys_values(
        me, odd, gain, w, rows_of(fade, chunks - 1), summary, tail, received[-1], heads, dim
    )
    ks.append(k)
    vs.append(v)

    came = lax.ppermute(sent, "tm", swap_pairs)
    joint = pair(odd, tail, keep, came, heads)
    fars = [
        lax.ppermute(joint, "tm", [(d, d + 2 * k) for d in range(blocks - 2 * k)])
        for k in range(1, blocks // 2)
    ]
    stay, sent = entering(odd, tail, keep, came, fars, heads)
    state = lax.ppermute(sent, "tm", swap_pairs)

    qs.append(last_queries(me, gain, w, received[-1], heads, dim))
    locals_.append(attention(chunks - 1, tile_retain_grid, scale, qs[-1], ks, vs, heads, dim))

    result = None
    for c in range(chunks):
        head_out = recall(odd, rows_of(reading, c), qs[c], locals_[c], stay, state, heads, dim)
        side = lax.ppermute(head_out, "stream", swap_streams)
        outs = project(me, head_out, side, own_w, side_w, shards)
        parts = [outs[0]]
        for k in range(1, shards):
            parts.append(
                lax.ppermute(outs[k], "head", [(d, (d + k) % shards) for d in range(shards)])
            )
        result = finish(parts, result, c, length)
    return result[None]


def solution(mesh):
    placed = (
        P("stream", "tm", "head"),
        P("stream", None),
        P("stream", None, "head", None),
        P("stream", "head"),
        P("stream", "head", "tm"),
        P("tm", None),
        P("tm"),
        P("stream", "head", None, None),
        P("stream", "head", None, None),
    )
    return jax.shard_map(
        per_device, mesh=mesh, in_specs=placed, out_specs=P("stream", "tm", "head"), check_vma=False
    )
```

```python
import functools
import math

import jax
import jax.numpy as jnp
from jax import lax
from jax.experimental import pallas as pl
from jax.experimental.pallas import tpu as pltpu
from jax.sharding import PartitionSpec as P

BLOCK = 512
CHUNK = 256
TAIL = 16
EPSILON = 1e-06
F32 = jnp.float32
BF16 = jnp.bfloat16
SMEM = pl.BlockSpec(memory_space=pltpu.SMEM)
VMEM = pl.BlockSpec(memory_space=pltpu.VMEM)


def params():
    return pltpu.CompilerParams(vmem_limit_bytes=16 * 1024 * 1024)


def cost(flops, bytes_accessed, transcendentals=0):
    return pl.CostEstimate(
        flops=int(flops), bytes_accessed=int(bytes_accessed), transcendentals=int(transcendentals)
    )


def struct(shape, dtype=BF16):
    return jax.ShapeDtypeStruct(shape, dtype)


def dot(a, b):
    return lax.dot_general(a, b, (((1,), (0,)), ((), ())), preferred_element_type=F32)


def dot_nt(a, b):
    return lax.dot_general(a, b, (((1,), (1,)), ((), ())), preferred_element_type=F32)


def dot_tn(a, b):
    return lax.dot_general(a, b, (((0,), (0,)), ((), ())), preferred_element_type=F32)


def unit(values):
    return values * lax.rsqrt(jnp.mean(values * values, axis=-1, keepdims=True) + EPSILON)


def prepare_kernel(heads, factor, logs_ref, flags_ref, fade_ref, reading_ref, tail_ref, rows_ref):
    length = logs_ref.shape[1]
    rows_ref[...] = jnp.zeros_like(rows_ref)
    rows_ref[:heads, :] = logs_ref[...]
    running = rows_ref[...]
    place = lax.broadcasted_iota(jnp.int32, running.shape, 1)
    step = 1
    while step < length:
        running += jnp.where(place >= step, pltpu.roll(running, step, 1), 0.0)
        step *= 2
    last = running[:, length - 1 :]
    chosen = jnp.zeros_like(running)
    for block in range(length // BLOCK):
        inside = (place >= block * BLOCK) & (place < (block + 1) * BLOCK)
        chosen = jnp.where(inside, flags_ref[block].astype(F32), chosen)
    fade_ref[...] = jnp.transpose(jnp.exp(last - running) * chosen)
    reading_ref[...] = jnp.transpose(jnp.exp(running) * factor)
    decay = jnp.exp(last)
    high = decay.astype(BF16).astype(F32)
    both = jnp.concatenate([high, decay - high], axis=0)
    tail_ref[...] = jnp.broadcast_to(both, tail_ref.shape).astype(BF16)


def prepare(logs, flags, dim, factor):
    heads, length = logs.shape
    lines = TAIL // 2
    return pl.pallas_call(
        functools.partial(prepare_kernel, heads, factor),
        in_specs=[VMEM, SMEM],
        out_specs=[VMEM] * 3,
        out_shape=[struct((length, lines), F32)] * 2 + [struct((TAIL, dim))],
        scratch_shapes=[pltpu.VMEM((lines, length), F32)],
        compiler_params=params(),
        cost_estimate=cost(40 * lines * length, 0),
        name="prepare",
    )(logs, flags)


def normed_parts(me, gain_ref, x_refs):
    shards, width = len(x_refs), x_refs[0].shape[1]
    parts = [x[...].astype(F32) for x in x_refs]
    squares = sum(jnp.sum(p * p, axis=-1, keepdims=True) for p in parts)
    scale = lax.rsqrt(squares * (1.0 / (width * shards)) + EPSILON)
    out = []
    for k, part in enumerate(parts):
        owner = lax.rem(me + k, shards)
        rows = pl.ds(pl.multiple_of(owner * width, width), width)
        out.append(((part * scale * gain_ref[:, rows]).astype(BF16), rows))
    return out


def projected(parts, w_ref, cols):
    total = None
    for part, rows in parts:
        term = dot(part, w_ref[rows, cols])
        total = term if total is None else total + term
    return total


def add_summary(sum_ref, h, key, value, fade_ref, first):
    fade = fade_ref[first : first + key.shape[0], h : h + 1]
    sum_ref[h] += dot_tn((key.astype(F32) * fade).astype(BF16), value)


def qkv_kernel(heads, dim, first, me_ref, gain_ref, w_ref, fade_ref, *refs):
    refs, (q_ref, k_ref, v_ref, sum_ref) = refs[:-4], refs[-4:]
    if first == 0:
        sum_ref[...] = jnp.zeros_like(sum_ref)
        x_refs = refs
    else:
        sum_ref[...] = refs[0][...]
        x_refs = refs[1:]
    parts = normed_parts(me_ref[0], gain_ref, x_refs)
    total = projected(parts, w_ref, slice(None))
    for h in range(heads):
        base = 3 * h * dim
        cols = slice(h * dim, (h + 1) * dim)
        q_ref[:, cols] = unit(total[:, base : base + dim]).astype(BF16)
        key = unit(total[:, base + dim : base + 2 * dim]).astype(BF16)
        value = total[:, base + 2 * dim : base + 3 * dim].astype(BF16)
        k_ref[:, cols] = key
        v_ref[:, cols] = value
        add_summary(sum_ref, h, key, value, fade_ref, first)


def qkv(me, gain, w, fade, prev, xs, heads, dim, first):
    rows = xs[0].shape[0]
    before = [prev] if first else []
    return pl.pallas_call(
        functools.partial(qkv_kernel, heads, dim, first),
        in_specs=[SMEM] + [VMEM] * (3 + len(before) + len(xs)),
        out_specs=[VMEM] * 4,
        out_shape=[struct((rows, heads * dim))] * 3 + [struct((heads, dim, dim), F32)],
        compiler_params=params(),
        cost_estimate=cost(4 * rows * w.size, 0),
        name="qkv",
    )(me, gain, w, fade, *before, *xs)


def last_kernel(heads, dim, first, me_ref, gain_ref, w_ref, fade_ref, prev_ref, tail_ref, *refs):
    x_refs, (k_ref, v_ref, send_ref, sum_ref) = refs[:-4], refs[-4:]
    sum_ref[...] = prev_ref[...]
    parts = normed_parts(me_ref[0], gain_ref, x_refs)
    for h in range(heads):
        base = 3 * h * dim
        cols = slice(h * dim, (h + 1) * dim)
        both = projected(parts, w_ref, slice(base + dim, base + 3 * dim))
        key = unit(both[:, :dim]).astype(BF16)
        value = both[:, dim:].astype(BF16)
        k_ref[:, cols] = key
        v_ref[:, cols] = value
        add_summary(sum_ref, h, key, value, fade_ref, first)
        send_ref[cols, :] = sum_ref[h].astype(BF16)
    send_ref[heads * dim :, :] = tail_ref[...]


def last_keys_values(me, gain, w, fade, prev, tail, xs, heads, dim, first):
    rows = xs[0].shape[0]
    return pl.pallas_call(
        functools.partial(last_kernel, heads, dim, first),
        in_specs=[SMEM] + [VMEM] * (5 + len(xs)),
        out_specs=[VMEM] * 3,
        out_shape=[struct((rows, heads * dim))] * 2 + [struct((heads * dim + TAIL, dim))],
        scratch_shapes=[pltpu.VMEM((heads, dim, dim), F32)],
        compiler_params=params(),
        cost_estimate=cost(3 * rows * w.size, 0),
        name="last_keys_values",
    )(me, gain, w, fade, prev, tail, *xs)


def queries_kernel(heads, dim, me_ref, gain_ref, w_ref, *refs):
    q_ref = refs[-1]
    parts = normed_parts(me_ref[0], gain_ref, refs[:-1])
    for h in range(heads):
        base = 3 * h * dim
        cols = slice(h * dim, (h + 1) * dim)
        q_ref[:, cols] = unit(projected(parts, w_ref, slice(base, base + dim))).astype(BF16)


def last_queries(me, gain, w, xs, heads, dim):
    rows = xs[0].shape[0]
    return pl.pallas_call(
        functools.partial(queries_kernel, heads, dim),
        in_specs=[SMEM] + [VMEM] * (2 + len(xs)),
        out_specs=VMEM,
        out_shape=struct((rows, heads * dim)),
        compiler_params=params(),
        cost_estimate=cost(2 * rows * w.size, 0),
        name="last_queries",
    )(me, gain, w, *xs)


def attention_kernel(chunk, heads, dim, keep_ref, scale_ref, q_ref, *refs):
    k_refs, v_refs, out_ref = refs[: chunk + 1], refs[chunk + 1 : -1], refs[-1]
    rows = q_ref.shape[0]
    per = BLOCK // rows
    block = chunk // per
    causal = lax.broadcasted_iota(jnp.int32, (rows, rows), 1) <= lax.broadcasted_iota(
        jnp.int32, (rows, rows), 0
    )
    ones = jnp.ones((rows, dim), BF16)
    for h in range(heads):
        cols = slice(h * dim, (h + 1) * dim)
        query = q_ref[:, cols]
        total = None
        for j in range(chunk + 1):
            powers = jnp.exp(dot_nt(query, k_refs[j][:, cols]) * scale_ref[0, h])
            if j == chunk:
                powers = jnp.where(causal, powers, 0.0)
            part = dot(powers.astype(BF16), jnp.concatenate([v_refs[j][:, cols], ones], axis=1))
            if j // per < block:
                part = jnp.where(keep_ref[block, j // per] == 1, part, 0.0)
            total = part if total is None else total + part
        out_ref[:, cols] = (total[:, :dim] / total[:, dim:]).astype(BF16)


def attention(chunk, keep, scale, q, ks, vs, heads, dim):
    rows = q.shape[0]
    return pl.pallas_call(
        functools.partial(attention_kernel, chunk, heads, dim),
        in_specs=[SMEM, SMEM] + [VMEM] * (1 + len(ks) + len(vs)),
        out_specs=VMEM,
        out_shape=struct(q.shape),
        compiler_params=params(),
        cost_estimate=cost(
            (chunk + 1) * heads * 8 * rows * rows * dim, 0, (chunk + 1) * heads * rows * rows
        ),
        name="attention",
    )(keep, scale, q, *ks, *vs)


def body_and_decay(ref, h, dim):
    size = ref.shape[0] - TAIL
    high = ref[size + h : size + h + 1, :].astype(F32)
    low = ref[size + TAIL // 2 + h : size + TAIL // 2 + h + 1, :].astype(F32)
    return ref[h * dim : (h + 1) * dim, :].astype(F32), high + low


def scanned(place, refs, h, dim):
    count = len(refs)
    loaded = [body_and_decay(ref, h, dim) for ref in refs]
    state, since = jnp.zeros((dim, refs[0].shape[1]), F32), jnp.ones((1, refs[0].shape[1]), F32)
    before, before_decay = state, since
    for j in range(count):
        before = jnp.where(place == j, state, before)
        before_decay = jnp.where(place == j, since, before_decay)
        body, decay = loaded[0]
        for k in range(1, count):
            here = place == (j ^ k)
            body = jnp.where(here, loaded[k][0], body)
            decay = jnp.where(here, loaded[k][1], decay)
        state = decay * state + body
        since = since * decay
    return before, before_decay, state, since


def quad_kernel(heads, dim, place_ref, *refs):
    refs, (before_ref, decay_ref, total_ref) = refs[:-3], refs[-3:]
    size = heads * dim
    total_ref[size:, :] = jnp.zeros((TAIL, total_ref.shape[1]), BF16)
    for h in range(heads):
        rows = slice(h * dim, (h + 1) * dim)
        before, before_decay, state, since = scanned(place_ref[0], refs, h, dim)
        before_ref[rows, :] = before
        decay_ref[h : h + 1, :] = before_decay
        total_ref[rows, :] = state.astype(BF16)
        high = since.astype(BF16)
        total_ref[size + h : size + h + 1, :] = high
        low = (since - high.astype(F32)).astype(BF16)
        total_ref[size + TAIL // 2 + h : size + TAIL // 2 + h + 1, :] = low


def quad(place, loads, heads, dim):
    shape = loads[0].shape
    return pl.pallas_call(
        functools.partial(quad_kernel, heads, dim),
        in_specs=[SMEM] + [VMEM] * len(loads),
        out_specs=[VMEM] * 3,
        out_shape=[
            struct((heads * dim, shape[1]), F32),
            struct((TAIL // 2, shape[1]), F32),
            struct(shape),
        ],
        compiler_params=params(),
        cost_estimate=cost(loads[0].size * 40, 0),
        name="quad",
    )(place, *loads)


def entering_kernel(heads, dim, place_ref, before_ref, decay_ref, *refs):
    refs, out_ref = refs[:-1], refs[-1]
    for h in range(heads):
        rows = slice(h * dim, (h + 1) * dim)
        earlier = scanned(place_ref[0], refs, h, dim)[0]
        out_ref[rows, :] = (before_ref[rows, :] + decay_ref[h : h + 1, :] * earlier).astype(BF16)


def entering(place, before, decay, totals, heads, dim):
    return pl.pallas_call(
        functools.partial(entering_kernel, heads, dim),
        in_specs=[SMEM] + [VMEM] * (2 + len(totals)),
        out_specs=VMEM,
        out_shape=struct(before.shape),
        compiler_params=params(),
        cost_estimate=cost(before.size * 20, 0),
        name="entering",
    )(place, before, decay, *totals)


def recall_kernel(heads, dim, first, reading_ref, q_ref, local_ref, state_ref, out_ref):
    for h in range(heads):
        cols = slice(h * dim, (h + 1) * dim)
        reading = reading_ref[first : first + q_ref.shape[0], h : h + 1]
        recalled = dot(q_ref[:, cols], state_ref[cols, :]) * reading
        out_ref[:, cols] = (local_ref[:, cols].astype(F32) + recalled).astype(BF16)


def recall(reading, q, local, state, heads, dim, first):
    return pl.pallas_call(
        functools.partial(recall_kernel, heads, dim, first),
        in_specs=[VMEM] * 4,
        out_specs=VMEM,
        out_shape=struct(q.shape),
        compiler_params=params(),
        cost_estimate=cost(4 * q.size * dim, 0),
        name="recall",
    )(reading, q, local, state)


def project_kernel(shards, me_ref, own_ref, side_ref, own_w_ref, side_w_ref, *out_refs):
    width = out_refs[0].shape[1]
    own, side = own_ref[...], side_ref[...]
    for k in reversed(range(shards)):
        owner = lax.rem(me_ref[0] + k, shards)
        cols = pl.ds(pl.multiple_of(owner * width, width), width)
        out = dot(own, own_w_ref[:, cols]) + dot(side, side_w_ref[:, cols])
        out_refs[k][...] = out.astype(out_refs[k].dtype)


def project(me, own, side, own_w, side_w, shards):
    rows = own.shape[0]
    width = own_w.shape[1] // shards
    return pl.pallas_call(
        functools.partial(project_kernel, shards),
        in_specs=[SMEM] + [VMEM] * 4,
        out_specs=[VMEM] * shards,
        out_shape=[struct((rows, width))] * shards,
        compiler_params=params(),
        cost_estimate=cost(4 * rows * own_w.size, 0),
        name="project",
    )(me, own, side, own_w, side_w)


def finish_kernel(count, *refs):
    total = refs[0][...].astype(F32)
    for ref in refs[1:count]:
        total += ref[...].astype(F32)
    refs[-1][...] = total.astype(BF16)


def finish(parts, result, chunk, length):
    rows, width = parts[0].shape
    whole = pl.BlockSpec((rows, width), lambda i: (0, 0))
    more = [] if result is None else [result]
    return pl.pallas_call(
        functools.partial(finish_kernel, len(parts)),
        grid=(1,),
        in_specs=[whole] * len(parts) + [pl.BlockSpec(memory_space=pl.ANY)] * len(more),
        out_specs=pl.BlockSpec((rows, width), lambda i: (chunk, 0)),
        out_shape=struct((length, width)),
        input_output_aliases={len(parts): 0} if more else {},
        compiler_params=params(),
        cost_estimate=cost(rows * width * 2, rows * width * 6),
        name="finish",
    )(*parts, *more)


def per_device(
    residual_signal,
    prescale_amplifier,
    triple_projector,
    score_scaler,
    recall_retained_logshare,
    tile_retain_grid,
    recall_store_flags,
    emission_projector,
    sideways_coupling_coef,
):
    x = residual_signal[0]
    length = x.shape[0]
    chunks = length // CHUNK
    shards = lax.axis_size("head")
    blocks = lax.axis_size("tm")
    heads = triple_projector.shape[2]
    dim = emission_projector.shape[2]
    me = lax.axis_index("head").astype(jnp.int32).reshape(1)
    place = lax.axis_index("tm").astype(jnp.int32).reshape(1)
    swap_streams = [(0, 1), (1, 0)]
    tied = lambda *arrays: lax.optimization_barrier(arrays)

    received = []
    for c in range(chunks):
        piece = x[c * CHUNK : (c + 1) * CHUNK]
        xs = [piece]
        for k in range(1, shards):
            xs.append(lax.ppermute(piece, "head", [((d + k) % shards, d) for d in range(shards)]))
        received.append(xs)

    own_w = emission_projector[0].reshape(heads * dim, -1)
    side_w = lax.ppermute(
        sideways_coupling_coef[0].reshape(heads * dim, -1), "stream", swap_streams
    )
    fade, reading, tail = prepare(
        recall_retained_logshare[0],
        recall_store_flags,
        dim,
        1.0 / math.sqrt(dim * length * blocks),
    )
    scale = score_scaler * (1.0 / math.sqrt(dim))
    gain = prescale_amplifier
    w = triple_projector[0].reshape(-1, 3 * heads * dim)

    qs, ks, vs, locals_ = [], [], [], []
    summary = None
    for c in range(chunks - 1):
        q, k, v, summary = qkv(
            me, gain, w, fade, summary, received[c], heads, dim, c * CHUNK
        )
        qs.append(q)
        ks.append(k)
        vs.append(v)
        locals_.append(attention(c, tile_retain_grid, scale, q, ks, vs, heads, dim))
    summary, *locals_ = tied(summary, *locals_)
    k, v, sent = last_keys_values(
        me, gain, w, fade, summary, tail, received[-1], heads, dim, (chunks - 1) * CHUNK
    )
    ks.append(k)
    vs.append(v)

    quad_size = min(4, blocks)
    loads = [sent] + [
        lax.ppermute(sent, "tm", [(d, d ^ k) for d in range(blocks)]) for k in range(1, quad_size)
    ]
    qs.append(last_queries(me, gain, w, received[-1], heads, dim))
    locals_.append(attention(chunks - 1, tile_retain_grid, scale, qs[-1], ks, vs, heads, dim))
    *loads, locals_[-1] = tied(*loads, locals_[-1])
    before, decay, total = quad(lax.rem(place, quad_size), loads, heads, dim)
    totals = [total] + [
        lax.ppermute(total, "tm", [(d, d ^ (quad_size * k)) for d in range(blocks)])
        for k in range(1, blocks // quad_size)
    ]
    state = entering(lax.div(place, quad_size), before, decay, totals, heads, dim)

    result = None
    for c in range(chunks):
        head_out = recall(reading, qs[c], locals_[c], state, heads, dim, c * CHUNK)
        side = lax.ppermute(head_out, "stream", swap_streams)
        outs = project(me, head_out, side, own_w, side_w, shards)
        parts = [outs[0]]
        for k in range(1, shards):
            parts.append(
                lax.ppermute(outs[k], "head", [(d, (d + k) % shards) for d in range(shards)])
            )
        result = finish(parts, result, c, length)
    return result[None]


def solution(mesh):
    placed = (
        P("stream", "tm", "head"),
        P("stream", None),
        P("stream", None, "head", None),
        P("stream", "head"),
        P("stream", "head", "tm"),
        P("tm", None),
        P("tm"),
        P("stream", "head", None, None),
        P("stream", "head", None, None),
    )
    return jax.shard_map(
        per_device, mesh=mesh, in_specs=placed, out_specs=P("stream", "tm", "head"), check_vma=False
    )
```

```python
import functools
import math

import jax
import jax.numpy as jnp
from jax import lax
from jax.experimental import pallas as pl
from jax.experimental.pallas import tpu as pltpu
from jax.sharding import PartitionSpec as P

BLOCK = 512
CHUNK = 256
TAIL = 16
EPSILON = 1e-06
F32 = jnp.float32
BF16 = jnp.bfloat16
SMEM = pl.BlockSpec(memory_space=pltpu.SMEM)
VMEM = pl.BlockSpec(memory_space=pltpu.VMEM)


def params():
    return pltpu.CompilerParams(vmem_limit_bytes=16 * 1024 * 1024)


def cost(flops, bytes_accessed, transcendentals=0):
    return pl.CostEstimate(
        flops=int(flops), bytes_accessed=int(bytes_accessed), transcendentals=int(transcendentals)
    )


def struct(shape, dtype=BF16):
    return jax.ShapeDtypeStruct(shape, dtype)


def dot(a, b):
    return lax.dot_general(a, b, (((1,), (0,)), ((), ())), preferred_element_type=F32)


def dot_nt(a, b):
    return lax.dot_general(a, b, (((1,), (1,)), ((), ())), preferred_element_type=F32)


def dot_tn(a, b):
    return lax.dot_general(a, b, (((0,), (0,)), ((), ())), preferred_element_type=F32)


def unit(values):
    return values * lax.rsqrt(jnp.mean(values * values, axis=-1, keepdims=True) + EPSILON)


def prepare_kernel(heads, factor, logs_ref, flags_ref, fade_ref, reading_ref, tail_ref, rows_ref):
    length = logs_ref.shape[1]
    rows_ref[...] = jnp.zeros_like(rows_ref)
    rows_ref[:heads, :] = logs_ref[...]
    running = rows_ref[...]
    place = lax.broadcasted_iota(jnp.int32, running.shape, 1)
    step = 1
    while step < length:
        running += jnp.where(place >= step, pltpu.roll(running, step, 1), 0.0)
        step *= 2
    last = running[:, length - 1 :]
    chosen = jnp.zeros_like(running)
    for block in range(length // BLOCK):
        inside = (place >= block * BLOCK) & (place < (block + 1) * BLOCK)
        chosen = jnp.where(inside, flags_ref[block].astype(F32), chosen)
    fade_ref[...] = jnp.transpose(jnp.exp(last - running) * chosen)
    reading_ref[...] = jnp.transpose(jnp.exp(running) * factor)
    decay = jnp.exp(last)
    high = decay.astype(BF16).astype(F32)
    both = jnp.concatenate([high, decay - high], axis=0)
    tail_ref[...] = jnp.broadcast_to(both, tail_ref.shape).astype(BF16)


def prepare(logs, flags, dim, factor):
    heads, length = logs.shape
    lines = TAIL // 2
    return pl.pallas_call(
        functools.partial(prepare_kernel, heads, factor),
        in_specs=[VMEM, SMEM],
        out_specs=[VMEM] * 3,
        out_shape=[struct((length, lines), F32)] * 2 + [struct((TAIL, dim))],
        scratch_shapes=[pltpu.VMEM((lines, length), F32)],
        compiler_params=params(),
        cost_estimate=cost(40 * lines * length, 0),
        name="prepare",
    )(logs, flags)


def normed_parts(me, gain_ref, x_refs):
    shards, width = len(x_refs), x_refs[0].shape[1]
    parts = [x[...].astype(F32) for x in x_refs]
    squares = sum(jnp.sum(p * p, axis=-1, keepdims=True) for p in parts)
    scale = lax.rsqrt(squares * (1.0 / (width * shards)) + EPSILON)
    out = []
    for k, part in enumerate(parts):
        owner = lax.rem(me + k, shards)
        rows = pl.ds(pl.multiple_of(owner * width, width), width)
        out.append(((part * scale * gain_ref[:, rows]).astype(BF16), rows))
    return out


def projected(parts, w_ref, cols):
    total = None
    for part, rows in parts:
        term = dot(part, w_ref[rows, cols])
        total = term if total is None else total + term
    return total


def add_summary(sum_ref, h, key, value, fade_ref, first):
    fade = fade_ref[first : first + key.shape[0], h : h + 1]
    sum_ref[h] += dot_tn((key.astype(F32) * fade).astype(BF16), value)


def qkv_kernel(heads, dim, first, me_ref, gain_ref, w_ref, fade_ref, *refs):
    refs, (q_ref, k_ref, v_ref, sum_ref) = refs[:-4], refs[-4:]
    if first == 0:
        sum_ref[...] = jnp.zeros_like(sum_ref)
        x_refs = refs
    else:
        sum_ref[...] = refs[0][...]
        x_refs = refs[1:]
    parts = normed_parts(me_ref[0], gain_ref, x_refs)
    wide = heads * dim
    thirds = [projected(parts, w_ref, slice(i * wide, (i + 1) * wide)) for i in range(3)]
    taken = lambda at: thirds[at * dim // wide][:, at * dim % wide : at * dim % wide + dim]
    for h in range(heads):
        cols = slice(h * dim, (h + 1) * dim)
        q_ref[:, cols] = unit(taken(3 * h)).astype(BF16)
        key = unit(taken(3 * h + 1)).astype(BF16)
        value = taken(3 * h + 2).astype(BF16)
        k_ref[:, cols] = key
        v_ref[:, cols] = value
        add_summary(sum_ref, h, key, value, fade_ref, first)


def qkv(me, gain, w, fade, prev, xs, heads, dim, first):
    rows = xs[0].shape[0]
    before = [prev] if first else []
    return pl.pallas_call(
        functools.partial(qkv_kernel, heads, dim, first),
        in_specs=[SMEM] + [VMEM] * (3 + len(before) + len(xs)),
        out_specs=[VMEM] * 4,
        out_shape=[struct((rows, heads * dim))] * 3 + [struct((heads, dim, dim), F32)],
        compiler_params=params(),
        cost_estimate=cost(4 * rows * w.size, 0),
        name="qkv",
    )(me, gain, w, fade, *before, *xs)


def last_kernel(heads, dim, first, me_ref, gain_ref, w_ref, fade_ref, prev_ref, tail_ref, *refs):
    x_refs, (k_ref, v_ref, send_ref, sum_ref) = refs[:-4], refs[-4:]
    sum_ref[...] = prev_ref[...]
    parts = normed_parts(me_ref[0], gain_ref, x_refs)
    pairs = [
        projected(parts, w_ref, slice((3 * h + 1) * dim, (3 * h + 3) * dim)) for h in range(heads)
    ]
    for h in range(heads):
        cols = slice(h * dim, (h + 1) * dim)
        key = unit(pairs[h][:, :dim]).astype(BF16)
        value = pairs[h][:, dim:].astype(BF16)
        k_ref[:, cols] = key
        v_ref[:, cols] = value
        add_summary(sum_ref, h, key, value, fade_ref, first)
        send_ref[cols, :] = sum_ref[h].astype(BF16)
    send_ref[heads * dim :, :] = tail_ref[...]


def last_keys_values(me, gain, w, fade, prev, tail, xs, heads, dim, first):
    rows = xs[0].shape[0]
    return pl.pallas_call(
        functools.partial(last_kernel, heads, dim, first),
        in_specs=[SMEM] + [VMEM] * (5 + len(xs)),
        out_specs=[VMEM] * 3,
        out_shape=[struct((rows, heads * dim))] * 2 + [struct((heads * dim + TAIL, dim))],
        scratch_shapes=[pltpu.VMEM((heads, dim, dim), F32)],
        compiler_params=params(),
        cost_estimate=cost(3 * rows * w.size, 0),
        name="last_keys_values",
    )(me, gain, w, fade, prev, tail, *xs)


def queries_kernel(heads, dim, me_ref, gain_ref, w_ref, *refs):
    q_ref = refs[-1]
    parts = normed_parts(me_ref[0], gain_ref, refs[:-1])
    for h in range(heads):
        base = 3 * h * dim
        cols = slice(h * dim, (h + 1) * dim)
        q_ref[:, cols] = unit(projected(parts, w_ref, slice(base, base + dim))).astype(BF16)


def last_queries(me, gain, w, xs, heads, dim):
    rows = xs[0].shape[0]
    return pl.pallas_call(
        functools.partial(queries_kernel, heads, dim),
        in_specs=[SMEM] + [VMEM] * (2 + len(xs)),
        out_specs=VMEM,
        out_shape=struct((rows, heads * dim)),
        compiler_params=params(),
        cost_estimate=cost(2 * rows * w.size, 0),
        name="last_queries",
    )(me, gain, w, *xs)


def attention_kernel(chunk, heads, dim, keep_ref, scale_ref, q_ref, *refs):
    k_refs, v_refs, out_ref = refs[: chunk + 1], refs[chunk + 1 : -1], refs[-1]
    rows = q_ref.shape[0]
    per = BLOCK // rows
    block = chunk // per
    causal = lax.broadcasted_iota(jnp.int32, (rows, rows), 1) <= lax.broadcasted_iota(
        jnp.int32, (rows, rows), 0
    )
    ones = jnp.ones((rows, dim), BF16)
    for h in range(heads):
        cols = slice(h * dim, (h + 1) * dim)
        query = q_ref[:, cols]
        scale = scale_ref[0, h] * (1.0 / math.sqrt(dim))
        total = None
        for j in range(chunk + 1):
            powers = jnp.exp(dot_nt(query, k_refs[j][:, cols]) * scale)
            if j == chunk:
                powers = jnp.where(causal, powers, 0.0)
            part = dot(powers.astype(BF16), jnp.concatenate([v_refs[j][:, cols], ones], axis=1))
            if j // per < block:
                part = jnp.where(keep_ref[block, j // per] == 1, part, 0.0)
            total = part if total is None else total + part
        out_ref[:, cols] = (total[:, :dim] / total[:, dim:]).astype(BF16)


def attention(chunk, keep, scale, q, ks, vs, heads, dim):
    rows = q.shape[0]
    return pl.pallas_call(
        functools.partial(attention_kernel, chunk, heads, dim),
        in_specs=[SMEM, SMEM] + [VMEM] * (1 + len(ks) + len(vs)),
        out_specs=VMEM,
        out_shape=struct(q.shape),
        compiler_params=params(),
        cost_estimate=cost(
            (chunk + 1) * heads * 8 * rows * rows * dim, 0, (chunk + 1) * heads * rows * rows
        ),
        name="attention",
    )(keep, scale, q, *ks, *vs)


def body_and_decay(ref, h, dim):
    size = ref.shape[0] - TAIL
    high = ref[size + h : size + h + 1, :].astype(F32)
    low = ref[size + TAIL // 2 + h : size + TAIL // 2 + h + 1, :].astype(F32)
    return ref[h * dim : (h + 1) * dim, :].astype(F32), high + low


def scanned(place, refs, h, dim):
    count = len(refs)
    loaded = [body_and_decay(ref, h, dim) for ref in refs]
    state, since = jnp.zeros((dim, refs[0].shape[1]), F32), jnp.ones((1, refs[0].shape[1]), F32)
    before, before_decay = state, since
    for j in range(count):
        before = jnp.where(place == j, state, before)
        before_decay = jnp.where(place == j, since, before_decay)
        body, decay = loaded[0]
        for k in range(1, count):
            here = place == (j ^ k)
            body = jnp.where(here, loaded[k][0], body)
            decay = jnp.where(here, loaded[k][1], decay)
        state = decay * state + body
        since = since * decay
    return before, before_decay, state, since


def quad_kernel(heads, dim, place_ref, *refs):
    refs, (before_ref, decay_ref, total_ref) = refs[:-3], refs[-3:]
    size = heads * dim
    total_ref[size:, :] = jnp.zeros((TAIL, total_ref.shape[1]), BF16)
    for h in range(heads):
        rows = slice(h * dim, (h + 1) * dim)
        before, before_decay, state, since = scanned(place_ref[0], refs, h, dim)
        before_ref[rows, :] = before
        decay_ref[h : h + 1, :] = before_decay
        total_ref[rows, :] = state.astype(BF16)
        high = since.astype(BF16)
        total_ref[size + h : size + h + 1, :] = high
        low = (since - high.astype(F32)).astype(BF16)
        total_ref[size + TAIL // 2 + h : size + TAIL // 2 + h + 1, :] = low


def quad(place, loads, heads, dim):
    shape = loads[0].shape
    return pl.pallas_call(
        functools.partial(quad_kernel, heads, dim),
        in_specs=[SMEM] + [VMEM] * len(loads),
        out_specs=[VMEM] * 3,
        out_shape=[
            struct((heads * dim, shape[1]), F32),
            struct((TAIL // 2, shape[1]), F32),
            struct(shape),
        ],
        compiler_params=params(),
        cost_estimate=cost(loads[0].size * 40, 0),
        name="quad",
    )(place, *loads)


def entering_kernel(heads, dim, place_ref, before_ref, decay_ref, *refs):
    refs, out_ref = refs[:-1], refs[-1]
    for h in range(heads):
        rows = slice(h * dim, (h + 1) * dim)
        earlier = scanned(place_ref[0], refs, h, dim)[0]
        out_ref[rows, :] = (before_ref[rows, :] + decay_ref[h : h + 1, :] * earlier).astype(BF16)


def entering(place, before, decay, totals, heads, dim):
    return pl.pallas_call(
        functools.partial(entering_kernel, heads, dim),
        in_specs=[SMEM] + [VMEM] * (2 + len(totals)),
        out_specs=VMEM,
        out_shape=struct(before.shape),
        compiler_params=params(),
        cost_estimate=cost(before.size * 20, 0),
        name="entering",
    )(place, before, decay, *totals)


def recall_kernel(heads, dim, first, reading_ref, q_ref, local_ref, state_ref, out_ref):
    for h in range(heads):
        cols = slice(h * dim, (h + 1) * dim)
        reading = reading_ref[first : first + q_ref.shape[0], h : h + 1]
        recalled = dot(q_ref[:, cols], state_ref[cols, :]) * reading
        out_ref[:, cols] = (local_ref[:, cols].astype(F32) + recalled).astype(BF16)


def recall(reading, q, local, state, heads, dim, first):
    return pl.pallas_call(
        functools.partial(recall_kernel, heads, dim, first),
        in_specs=[VMEM] * 4,
        out_specs=VMEM,
        out_shape=struct(q.shape),
        compiler_params=params(),
        cost_estimate=cost(4 * q.size * dim, 0),
        name="recall",
    )(reading, q, local, state)


def project_kernel(shards, me_ref, own_ref, side_ref, own_w_ref, side_w_ref, *out_refs):
    width = out_refs[0].shape[1]
    own, side = own_ref[...], side_ref[...]
    for k in reversed(range(shards)):
        owner = lax.rem(me_ref[0] + k, shards)
        cols = pl.ds(pl.multiple_of(owner * width, width), width)
        out = dot(own, own_w_ref[:, cols]) + dot(side, side_w_ref[:, cols])
        out_refs[k][...] = out.astype(out_refs[k].dtype)


def project(me, own, side, own_w, side_w, shards):
    rows = own.shape[0]
    width = own_w.shape[1] // shards
    return pl.pallas_call(
        functools.partial(project_kernel, shards),
        in_specs=[SMEM] + [VMEM] * 4,
        out_specs=[VMEM] * shards,
        out_shape=[struct((rows, width))] * shards,
        compiler_params=params(),
        cost_estimate=cost(4 * rows * own_w.size, 0),
        name="project",
    )(me, own, side, own_w, side_w)


def finish_kernel(count, *refs):
    total = refs[0][...].astype(F32)
    for ref in refs[1:count]:
        total += ref[...].astype(F32)
    refs[-1][...] = total.astype(BF16)


def finish(parts, result, chunk, length):
    rows, width = parts[0].shape
    whole = pl.BlockSpec((rows, width), lambda i: (0, 0))
    more = [] if result is None else [result]
    return pl.pallas_call(
        functools.partial(finish_kernel, len(parts)),
        grid=(1,),
        in_specs=[whole] * len(parts) + [pl.BlockSpec(memory_space=pl.ANY)] * len(more),
        out_specs=pl.BlockSpec((rows, width), lambda i: (chunk, 0)),
        out_shape=struct((length, width)),
        input_output_aliases={len(parts): 0} if more else {},
        compiler_params=params(),
        cost_estimate=cost(rows * width * 2, rows * width * 6),
        name="finish",
    )(*parts, *more)


def per_device(
    residual_signal,
    prescale_amplifier,
    triple_projector,
    score_scaler,
    recall_retained_logshare,
    tile_retain_grid,
    recall_store_flags,
    emission_projector,
    sideways_coupling_coef,
):
    x = residual_signal[0]
    length = x.shape[0]
    chunks = length // CHUNK
    shards = lax.axis_size("head")
    blocks = lax.axis_size("tm")
    heads = triple_projector.shape[2]
    dim = emission_projector.shape[2]
    me = lax.axis_index("head").astype(jnp.int32).reshape(1)
    place = lax.axis_index("tm").astype(jnp.int32).reshape(1)
    swap_streams = [(0, 1), (1, 0)]
    tied = lambda *arrays: lax.optimization_barrier(arrays)

    received = []
    for c in range(chunks):
        piece = x[c * CHUNK : (c + 1) * CHUNK]
        xs = [piece]
        for k in range(1, shards):
            xs.append(lax.ppermute(piece, "head", [((d + k) % shards, d) for d in range(shards)]))
        received.append(xs)

    own_w = emission_projector[0].reshape(heads * dim, -1)
    side_w = lax.ppermute(
        sideways_coupling_coef[0].reshape(heads * dim, -1), "stream", swap_streams
    )
    fade, reading, tail = prepare(
        recall_retained_logshare[0],
        recall_store_flags,
        dim,
        1.0 / math.sqrt(dim * length * blocks),
    )
    gain = prescale_amplifier
    w = triple_projector[0].reshape(-1, 3 * heads * dim)

    qs, ks, vs, locals_ = [], [], [], []
    summary = None
    for c in range(chunks - 1):
        q, k, v, summary = qkv(
            me, gain, w, fade, summary, received[c], heads, dim, c * CHUNK
        )
        qs.append(q)
        ks.append(k)
        vs.append(v)
        locals_.append(attention(c, tile_retain_grid, score_scaler, q, ks, vs, heads, dim))
    summary, *locals_ = tied(summary, *locals_)
    k, v, sent = last_keys_values(
        me, gain, w, fade, summary, tail, received[-1], heads, dim, (chunks - 1) * CHUNK
    )
    ks.append(k)
    vs.append(v)

    quad_size = min(4, blocks)
    loads = [sent] + [
        lax.ppermute(sent, "tm", [(d, d ^ k) for d in range(blocks)]) for k in range(1, quad_size)
    ]
    qs.append(last_queries(me, gain, w, received[-1], heads, dim))
    locals_.append(attention(chunks - 1, tile_retain_grid, score_scaler, qs[-1], ks, vs, heads, dim))
    *loads, locals_[-1] = tied(*loads, locals_[-1])
    before, decay, total = quad(lax.rem(place, quad_size), loads, heads, dim)
    totals = [total] + [
        lax.ppermute(total, "tm", [(d, d ^ (quad_size * k)) for d in range(blocks)])
        for k in range(1, blocks // quad_size)
    ]
    state = entering(lax.div(place, quad_size), before, decay, totals, heads, dim)

    result = None
    for c in range(chunks):
        head_out = recall(reading, qs[c], locals_[c], state, heads, dim, c * CHUNK)
        side = lax.ppermute(head_out, "stream", swap_streams)
        outs = project(me, head_out, side, own_w, side_w, shards)
        parts = [outs[0]]
        for k in range(1, shards):
            parts.append(
                lax.ppermute(outs[k], "head", [(d, (d + k) % shards) for d in range(shards)])
            )
        result = finish(parts, result, c, length)
    return result[None]


def solution(mesh):
    placed = (
        P("stream", "tm", "head"),
        P("stream", None),
        P("stream", None, "head", None),
        P("stream", "head"),
        P("stream", "head", "tm"),
        P("tm", None),
        P("tm"),
        P("stream", "head", None, None),
        P("stream", "head", None, None),
    )
    return jax.shard_map(
        per_device, mesh=mesh, in_specs=placed, out_specs=P("stream", "tm", "head"), check_vma=False
    )
```

```python
import functools
import math

import jax
import jax.numpy as jnp
from jax import lax
from jax.experimental import pallas as pl
from jax.experimental.pallas import tpu as pltpu
from jax.sharding import PartitionSpec as P

BLOCK = 512
CHUNK = 256
TAIL = 16
EPSILON = 1e-06
F32 = jnp.float32
BF16 = jnp.bfloat16
SMEM = pl.BlockSpec(memory_space=pltpu.SMEM)
VMEM = pl.BlockSpec(memory_space=pltpu.VMEM)


def params():
    return pltpu.CompilerParams(vmem_limit_bytes=16 * 1024 * 1024)


def cost(flops, bytes_accessed, transcendentals=0):
    return pl.CostEstimate(
        flops=int(flops), bytes_accessed=int(bytes_accessed), transcendentals=int(transcendentals)
    )


def struct(shape, dtype=BF16):
    return jax.ShapeDtypeStruct(shape, dtype)


def dot(a, b):
    return lax.dot_general(a, b, (((1,), (0,)), ((), ())), preferred_element_type=F32)


def dot_nt(a, b):
    return lax.dot_general(a, b, (((1,), (1,)), ((), ())), preferred_element_type=F32)


def dot_tn(a, b):
    return lax.dot_general(a, b, (((0,), (0,)), ((), ())), preferred_element_type=F32)


def unit(values):
    return values * lax.rsqrt(jnp.mean(values * values, axis=-1, keepdims=True) + EPSILON)


def prepare_kernel(heads, factor, logs_ref, flags_ref, fade_ref, reading_ref, tail_ref, rows_ref):
    length = logs_ref.shape[1]
    rows_ref[...] = jnp.zeros_like(rows_ref)
    rows_ref[:heads, :] = logs_ref[...]
    running = rows_ref[...]
    place = lax.broadcasted_iota(jnp.int32, running.shape, 1)
    step = 1
    while step < length:
        running += jnp.where(place >= step, pltpu.roll(running, step, 1), 0.0)
        step *= 2
    last = running[:, length - 1 :]
    chosen = jnp.zeros_like(running)
    for block in range(length // BLOCK):
        inside = (place >= block * BLOCK) & (place < (block + 1) * BLOCK)
        chosen = jnp.where(inside, flags_ref[block].astype(F32), chosen)
    fade_ref[...] = jnp.transpose(jnp.exp(last - running) * chosen)
    reading_ref[...] = jnp.transpose(jnp.exp(running) * factor)
    decay = jnp.exp(last)
    high = decay.astype(BF16).astype(F32)
    low = decay - high
    size = (TAIL // 2, tail_ref.shape[2])
    for h in range(heads):
        parts = [jnp.broadcast_to(part[h : h + 1, :], size) for part in (high, low)]
        tail_ref[h] = jnp.concatenate(parts, axis=0).astype(BF16)


def prepare(logs, flags, dim, factor):
    heads, length = logs.shape
    lines = TAIL // 2
    return pl.pallas_call(
        functools.partial(prepare_kernel, heads, factor),
        in_specs=[VMEM, SMEM],
        out_specs=[VMEM] * 3,
        out_shape=[struct((length, lines), F32)] * 2 + [struct((heads, TAIL, dim))],
        scratch_shapes=[pltpu.VMEM((lines, length), F32)],
        compiler_params=params(),
        cost_estimate=cost(40 * lines * length, 0),
        name="prepare",
    )(logs, flags)


def normed_parts(me, gain_ref, x_refs):
    shards, width = len(x_refs), x_refs[0].shape[1]
    parts = [x[...].astype(F32) for x in x_refs]
    squares = sum(jnp.sum(p * p, axis=-1, keepdims=True) for p in parts)
    scale = lax.rsqrt(squares * (1.0 / (width * shards)) + EPSILON)
    out = []
    for k, part in enumerate(parts):
        owner = lax.rem(me + k, shards)
        rows = pl.ds(pl.multiple_of(owner * width, width), width)
        out.append(((part * scale * gain_ref[:, rows]).astype(BF16), rows))
    return out


def projected(parts, w_ref, cols):
    total = None
    for part, rows in parts:
        term = dot(part, w_ref[rows, cols])
        total = term if total is None else total + term
    return total


def add_summary(sum_ref, h, key, value, fade_ref, first):
    fade = fade_ref[first : first + key.shape[0], h : h + 1]
    sum_ref[h] += dot_tn((key.astype(F32) * fade).astype(BF16), value)


def qkv_kernel(heads, dim, first, me_ref, gain_ref, w_ref, fade_ref, *refs):
    refs, (q_ref, k_ref, v_ref, sum_ref) = refs[:-4], refs[-4:]
    if first == 0:
        sum_ref[...] = jnp.zeros_like(sum_ref)
        x_refs = refs
    else:
        sum_ref[...] = refs[0][...]
        x_refs = refs[1:]
    parts = normed_parts(me_ref[0], gain_ref, x_refs)
    wide = heads * dim
    thirds = [projected(parts, w_ref, slice(i * wide, (i + 1) * wide)) for i in range(3)]
    taken = lambda at: thirds[at * dim // wide][:, at * dim % wide : at * dim % wide + dim]
    for h in range(heads):
        cols = slice(h * dim, (h + 1) * dim)
        q_ref[:, cols] = unit(taken(3 * h)).astype(BF16)
        key = unit(taken(3 * h + 1)).astype(BF16)
        value = taken(3 * h + 2).astype(BF16)
        k_ref[:, cols] = key
        v_ref[:, cols] = value
        add_summary(sum_ref, h, key, value, fade_ref, first)


def qkv(me, gain, w, fade, prev, xs, heads, dim, first):
    rows = xs[0].shape[0]
    before = [prev] if first else []
    return pl.pallas_call(
        functools.partial(qkv_kernel, heads, dim, first),
        in_specs=[SMEM] + [VMEM] * (3 + len(before) + len(xs)),
        out_specs=[VMEM] * 4,
        out_shape=[struct((rows, heads * dim))] * 3 + [struct((heads, dim, dim), F32)],
        compiler_params=params(),
        cost_estimate=cost(4 * rows * w.size, 0),
        name="qkv",
    )(me, gain, w, fade, *before, *xs)


def last_kernel(heads, dim, first, me_ref, gain_ref, w_ref, fade_ref, prev_ref, tail_ref, *refs):
    x_refs, (k_ref, v_ref, send_ref, sum_ref) = refs[:-4], refs[-4:]
    sum_ref[...] = prev_ref[...]
    parts = normed_parts(me_ref[0], gain_ref, x_refs)
    pairs = [
        projected(parts, w_ref, slice((3 * h + 1) * dim, (3 * h + 3) * dim)) for h in range(heads)
    ]
    for h in range(heads):
        cols = slice(h * dim, (h + 1) * dim)
        key = unit(pairs[h][:, :dim]).astype(BF16)
        value = pairs[h][:, dim:].astype(BF16)
        k_ref[:, cols] = key
        v_ref[:, cols] = value
        add_summary(sum_ref, h, key, value, fade_ref, first)
    blocks, part = send_ref.shape[0], send_ref.shape[1] - TAIL
    for j in range(blocks):
        h, row = divmod(j * part, dim)
        send_ref[j, :part, :] = sum_ref[h, row : row + part, :].astype(BF16)
        send_ref[j, part:, :] = tail_ref[h]


def last_keys_values(me, gain, w, fade, prev, tail, xs, heads, dim, first, blocks):
    rows = xs[0].shape[0]
    return pl.pallas_call(
        functools.partial(last_kernel, heads, dim, first),
        in_specs=[SMEM] + [VMEM] * (5 + len(xs)),
        out_specs=[VMEM] * 3,
        out_shape=[struct((rows, heads * dim))] * 2
        + [struct((blocks, heads * dim // blocks + TAIL, dim))],
        scratch_shapes=[pltpu.VMEM((heads, dim, dim), F32)],
        compiler_params=params(),
        cost_estimate=cost(3 * rows * w.size, 0),
        name="last_keys_values",
    )(me, gain, w, fade, prev, tail, *xs)


def queries_kernel(heads, dim, me_ref, gain_ref, w_ref, *refs):
    q_ref = refs[-1]
    parts = normed_parts(me_ref[0], gain_ref, refs[:-1])
    for h in range(heads):
        base = 3 * h * dim
        cols = slice(h * dim, (h + 1) * dim)
        q_ref[:, cols] = unit(projected(parts, w_ref, slice(base, base + dim))).astype(BF16)


def last_queries(me, gain, w, xs, heads, dim):
    rows = xs[0].shape[0]
    return pl.pallas_call(
        functools.partial(queries_kernel, heads, dim),
        in_specs=[SMEM] + [VMEM] * (2 + len(xs)),
        out_specs=VMEM,
        out_shape=struct((rows, heads * dim)),
        compiler_params=params(),
        cost_estimate=cost(2 * rows * w.size, 0),
        name="last_queries",
    )(me, gain, w, *xs)


def attention_kernel(chunk, heads, dim, keep_ref, scale_ref, q_ref, *refs):
    k_refs, v_refs, out_ref = refs[: chunk + 1], refs[chunk + 1 : -1], refs[-1]
    rows = q_ref.shape[0]
    per = BLOCK // rows
    block = chunk // per
    causal = lax.broadcasted_iota(jnp.int32, (rows, rows), 1) <= lax.broadcasted_iota(
        jnp.int32, (rows, rows), 0
    )
    ones = jnp.ones((rows, dim), BF16)
    for h in range(heads):
        cols = slice(h * dim, (h + 1) * dim)
        query = q_ref[:, cols]
        scale = scale_ref[0, h] * (1.0 / math.sqrt(dim))
        total = None
        for j in range(chunk + 1):
            powers = jnp.exp(dot_nt(query, k_refs[j][:, cols]) * scale)
            if j == chunk:
                powers = jnp.where(causal, powers, 0.0)
            part = dot(powers.astype(BF16), jnp.concatenate([v_refs[j][:, cols], ones], axis=1))
            if j // per < block:
                part = jnp.where(keep_ref[block, j // per] == 1, part, 0.0)
            total = part if total is None else total + part
        out_ref[:, cols] = (total[:, :dim] / total[:, dim:]).astype(BF16)


def attention(chunk, keep, scale, q, ks, vs, heads, dim):
    rows = q.shape[0]
    return pl.pallas_call(
        functools.partial(attention_kernel, chunk, heads, dim),
        in_specs=[SMEM, SMEM] + [VMEM] * (1 + len(ks) + len(vs)),
        out_specs=VMEM,
        out_shape=struct(q.shape),
        compiler_params=params(),
        cost_estimate=cost(
            (chunk + 1) * heads * 8 * rows * rows * dim, 0, (chunk + 1) * heads * rows * rows
        ),
        name="attention",
    )(keep, scale, q, *ks, *vs)


def scan_kernel(came_ref, out_ref):
    blocks, part, dim = out_ref.shape
    state = jnp.zeros((part, dim), F32)
    for c in range(blocks):
        out_ref[c] = state.astype(BF16)
        if c < blocks - 1:
            half = part + TAIL // 2
            decay = came_ref[c, part : part + 1, :].astype(F32) + came_ref[c, half : half + 1, :].astype(F32)
            state = decay * state + came_ref[c, :part, :].astype(F32)


def scan(came):
    blocks, rows, dim = came.shape
    return pl.pallas_call(
        scan_kernel,
        in_specs=[VMEM],
        out_specs=VMEM,
        out_shape=struct((blocks, rows - TAIL, dim)),
        compiler_params=params(),
        cost_estimate=cost(came.size * 10, 0),
        name="scan",
    )(came)


def recall_kernel(heads, dim, first, reading_ref, q_ref, local_ref, state_ref, out_ref):
    for h in range(heads):
        cols = slice(h * dim, (h + 1) * dim)
        reading = reading_ref[first : first + q_ref.shape[0], h : h + 1]
        recalled = dot(q_ref[:, cols], state_ref[cols, :]) * reading
        out_ref[:, cols] = (local_ref[:, cols].astype(F32) + recalled).astype(BF16)


def recall(reading, q, local, state, heads, dim, first):
    return pl.pallas_call(
        functools.partial(recall_kernel, heads, dim, first),
        in_specs=[VMEM] * 4,
        out_specs=VMEM,
        out_shape=struct(q.shape),
        compiler_params=params(),
        cost_estimate=cost(4 * q.size * dim, 0),
        name="recall",
    )(reading, q, local, state)


def project_kernel(shards, me_ref, own_ref, side_ref, own_w_ref, side_w_ref, *out_refs):
    width = out_refs[0].shape[1]
    own, side = own_ref[...], side_ref[...]
    for k in reversed(range(shards)):
        owner = lax.rem(me_ref[0] + k, shards)
        cols = pl.ds(pl.multiple_of(owner * width, width), width)
        out = dot(own, own_w_ref[:, cols]) + dot(side, side_w_ref[:, cols])
        out_refs[k][...] = out.astype(out_refs[k].dtype)


def project(me, own, side, own_w, side_w, shards):
    rows = own.shape[0]
    width = own_w.shape[1] // shards
    return pl.pallas_call(
        functools.partial(project_kernel, shards),
        in_specs=[SMEM] + [VMEM] * 4,
        out_specs=[VMEM] * shards,
        out_shape=[struct((rows, width))] * shards,
        compiler_params=params(),
        cost_estimate=cost(4 * rows * own_w.size, 0),
        name="project",
    )(me, own, side, own_w, side_w)


def finish_kernel(count, *refs):
    total = refs[0][...].astype(F32)
    for ref in refs[1:count]:
        total += ref[...].astype(F32)
    refs[-1][...] = total.astype(BF16)


def finish(parts, result, chunk, length):
    rows, width = parts[0].shape
    whole = pl.BlockSpec((rows, width), lambda i: (0, 0))
    more = [] if result is None else [result]
    return pl.pallas_call(
        functools.partial(finish_kernel, len(parts)),
        grid=(1,),
        in_specs=[whole] * len(parts) + [pl.BlockSpec(memory_space=pl.ANY)] * len(more),
        out_specs=pl.BlockSpec((rows, width), lambda i: (chunk, 0)),
        out_shape=struct((length, width)),
        input_output_aliases={len(parts): 0} if more else {},
        compiler_params=params(),
        cost_estimate=cost(rows * width * 2, rows * width * 6),
        name="finish",
    )(*parts, *more)


def per_device(
    residual_signal,
    prescale_amplifier,
    triple_projector,
    score_scaler,
    recall_retained_logshare,
    tile_retain_grid,
    recall_store_flags,
    emission_projector,
    sideways_coupling_coef,
):
    x = residual_signal[0]
    length = x.shape[0]
    chunks = length // CHUNK
    shards = lax.axis_size("head")
    blocks = lax.axis_size("tm")
    heads = triple_projector.shape[2]
    dim = emission_projector.shape[2]
    me = lax.axis_index("head").astype(jnp.int32).reshape(1)
    swap_streams = [(0, 1), (1, 0)]
    tied = lambda *arrays: lax.optimization_barrier(arrays)

    received = []
    for c in range(chunks):
        piece = x[c * CHUNK : (c + 1) * CHUNK]
        xs = [piece]
        for k in range(1, shards):
            xs.append(lax.ppermute(piece, "head", [((d + k) % shards, d) for d in range(shards)]))
        received.append(xs)

    own_w = emission_projector[0].reshape(heads * dim, -1)
    side_w = lax.ppermute(
        sideways_coupling_coef[0].reshape(heads * dim, -1), "stream", swap_streams
    )
    fade, reading, tail = prepare(
        recall_retained_logshare[0],
        recall_store_flags,
        dim,
        1.0 / math.sqrt(dim * length * blocks),
    )
    gain = prescale_amplifier
    w = triple_projector[0].reshape(-1, 3 * heads * dim)

    qs, ks, vs, locals_ = [], [], [], []
    summary = None
    for c in range(chunks - 1):
        q, k, v, summary = qkv(
            me, gain, w, fade, summary, received[c], heads, dim, c * CHUNK
        )
        qs.append(q)
        ks.append(k)
        vs.append(v)
        locals_.append(attention(c, tile_retain_grid, score_scaler, q, ks, vs, heads, dim))
    summary, *locals_ = tied(summary, *locals_)
    k, v, sent = last_keys_values(
        me, gain, w, fade, summary, tail, received[-1], heads, dim, (chunks - 1) * CHUNK, blocks
    )
    ks.append(k)
    vs.append(v)

    came = lax.all_to_all(sent, "tm", 0, 0)
    state = lax.all_to_all(scan(came), "tm", 0, 0).reshape(heads * dim, dim)

    result, finished = None, []
    for c in range(chunks):
        if c == chunks - 1:
            xs, finished[0] = tied(received[-1], finished[0])
            qs.append(last_queries(me, gain, w, xs, heads, dim))
            locals_.append(
                attention(c, tile_retain_grid, score_scaler, qs[-1], ks, vs, heads, dim)
            )
        head_out = recall(reading, qs[c], locals_[c], state, heads, dim, c * CHUNK)
        side = lax.ppermute(head_out, "stream", swap_streams)
        outs = project(me, head_out, side, own_w, side_w, shards)
        parts = [outs[0]]
        for k in range(1, shards):
            parts.append(
                lax.ppermute(outs[k], "head", [(d, (d + k) % shards) for d in range(shards)])
            )
        finished.append(parts)
    for c in range(chunks):
        result = finish(finished[c], result, c, length)
    return result[None]


def solution(mesh):
    placed = (
        P("stream", "tm", "head"),
        P("stream", None),
        P("stream", None, "head", None),
        P("stream", "head"),
        P("stream", "head", "tm"),
        P("tm", None),
        P("tm"),
        P("stream", "head", None, None),
        P("stream", "head", None, None),
    )
    return jax.shard_map(
        per_device, mesh=mesh, in_specs=placed, out_specs=P("stream", "tm", "head"), check_vma=False
    )
```

```python
import functools
import math

import jax
import jax.numpy as jnp
from jax import lax
from jax.experimental import pallas as pl
from jax.experimental.pallas import tpu as pltpu
from jax.sharding import PartitionSpec as P

BLOCK = 512
CHUNK = 256
TAIL = 16
EPSILON = 1e-06
F32 = jnp.float32
BF16 = jnp.bfloat16
SMEM = pl.BlockSpec(memory_space=pltpu.SMEM)
VMEM = pl.BlockSpec(memory_space=pltpu.VMEM)


def params():
    return pltpu.CompilerParams(vmem_limit_bytes=16 * 1024 * 1024)


def cost(flops, bytes_accessed, transcendentals=0):
    return pl.CostEstimate(
        flops=int(flops), bytes_accessed=int(bytes_accessed), transcendentals=int(transcendentals)
    )


def struct(shape, dtype=BF16):
    return jax.ShapeDtypeStruct(shape, dtype)


def dot(a, b):
    return lax.dot_general(a, b, (((1,), (0,)), ((), ())), preferred_element_type=F32)


def dot_nt(a, b):
    return lax.dot_general(a, b, (((1,), (1,)), ((), ())), preferred_element_type=F32)


def dot_tn(a, b):
    return lax.dot_general(a, b, (((0,), (0,)), ((), ())), preferred_element_type=F32)


def unit(values):
    return values * lax.rsqrt(jnp.mean(values * values, axis=-1, keepdims=True) + EPSILON)


def prepare_kernel(heads, factor, logs_ref, flags_ref, fade_ref, tail_ref, *refs):
    reading_refs, rows_ref = refs[:-1], refs[-1]
    length = logs_ref.shape[1]
    rows_ref[...] = jnp.zeros_like(rows_ref)
    rows_ref[:heads, :] = logs_ref[...]
    running = rows_ref[...]
    place = lax.broadcasted_iota(jnp.int32, running.shape, 1)
    step = 1
    while step < length:
        running += jnp.where(place >= step, pltpu.roll(running, step, 1), 0.0)
        step *= 2
    last = running[:, length - 1 :]
    chosen = jnp.zeros_like(running)
    for block in range(length // BLOCK):
        inside = (place >= block * BLOCK) & (place < (block + 1) * BLOCK)
        chosen = jnp.where(inside, flags_ref[block].astype(F32), chosen)
    fade_ref[...] = jnp.transpose(jnp.exp(last - running) * chosen)
    reading = jnp.transpose(jnp.exp(running) * factor)
    for c, ref in enumerate(reading_refs):
        ref[...] = reading[c * CHUNK : (c + 1) * CHUNK]
    decay = jnp.exp(last)
    high = decay.astype(BF16).astype(F32)
    lines, groups = running.shape[0], tail_ref.shape[0]
    for g in range(groups):
        both = [jnp.broadcast_to(part, (lines, tail_ref.shape[2])) for part in (high, decay - high)]
        if g > 0:
            both = [pltpu.roll(part, lines - g * (heads // groups), 0) for part in both]
        tail_ref[g] = jnp.concatenate(both, axis=0).astype(BF16)


def prepare(logs, flags, dim, factor, groups):
    heads, length = logs.shape
    lines = TAIL // 2
    return pl.pallas_call(
        functools.partial(prepare_kernel, heads, factor),
        in_specs=[VMEM, SMEM],
        out_specs=[VMEM] * (2 + length // CHUNK),
        out_shape=[struct((length, lines), F32), struct((groups, TAIL, dim))]
        + [struct((CHUNK, lines), F32)] * (length // CHUNK),
        scratch_shapes=[pltpu.VMEM((lines, length), F32)],
        compiler_params=params(),
        cost_estimate=cost(40 * lines * length, 0),
        name="prepare",
    )(logs, flags)


def normed_parts(me, gain_ref, x_refs):
    shards, width = len(x_refs), x_refs[0].shape[1]
    parts = [x[...].astype(F32) for x in x_refs]
    squares = sum(jnp.sum(p * p, axis=-1, keepdims=True) for p in parts)
    scale = lax.rsqrt(squares * (1.0 / (width * shards)) + EPSILON)
    out = []
    for k, part in enumerate(parts):
        owner = lax.rem(me + k, shards)
        rows = pl.ds(pl.multiple_of(owner * width, width), width)
        out.append(((part * scale * gain_ref[:, rows]).astype(BF16), rows))
    return out


def projected(parts, w_ref, cols):
    total = None
    for part, rows in parts:
        term = dot(part, w_ref[rows, cols])
        total = term if total is None else total + term
    return total


def add_summary(sum_ref, h, key, value, fade_ref, first):
    fade = fade_ref[first : first + key.shape[0], h : h + 1]
    sum_ref[h] += dot_tn((key.astype(F32) * fade).astype(BF16), value)


def qkv_kernel(heads, dim, first, me_ref, gain_ref, w_ref, fade_ref, *refs):
    refs, (q_ref, k_ref, v_ref, sum_ref) = refs[:-4], refs[-4:]
    if first == 0:
        sum_ref[...] = jnp.zeros_like(sum_ref)
        x_refs = refs
    else:
        sum_ref[...] = refs[0][...]
        x_refs = refs[1:]
    parts = normed_parts(me_ref[0], gain_ref, x_refs)
    wide = heads * dim
    thirds = [projected(parts, w_ref, slice(i * wide, (i + 1) * wide)) for i in range(3)]
    taken = lambda at: thirds[at * dim // wide][:, at * dim % wide : at * dim % wide + dim]
    for h in range(heads):
        cols = slice(h * dim, (h + 1) * dim)
        q_ref[:, cols] = unit(taken(3 * h)).astype(BF16)
        key = unit(taken(3 * h + 1)).astype(BF16)
        value = taken(3 * h + 2).astype(BF16)
        k_ref[:, cols] = key
        v_ref[:, cols] = value
        add_summary(sum_ref, h, key, value, fade_ref, first)


def qkv(me, gain, w, fade, prev, xs, heads, dim, first):
    rows = xs[0].shape[0]
    before = [prev] if first else []
    return pl.pallas_call(
        functools.partial(qkv_kernel, heads, dim, first),
        in_specs=[SMEM] + [VMEM] * (3 + len(before) + len(xs)),
        out_specs=[VMEM] * 4,
        out_shape=[struct((rows, heads * dim))] * 3 + [struct((heads, dim, dim), F32)],
        compiler_params=params(),
        cost_estimate=cost(4 * rows * w.size, 0),
        name="qkv",
    )(me, gain, w, fade, *before, *xs)


def last_kernel(shards, heads, dim, first, me_ref, gain_ref, w_ref, fade_ref, prev_ref, tail_ref, *refs):
    x_refs, (k_ref, v_ref, *send_refs, sum_ref) = refs[:shards], refs[shards:]
    per = heads // len(send_refs)
    sum_ref[...] = prev_ref[...]
    parts = normed_parts(me_ref[0], gain_ref, x_refs)
    pairs = [
        projected(parts, w_ref, slice((3 * h + 1) * dim, (3 * h + 3) * dim)) for h in range(heads)
    ]
    for h in range(heads):
        cols = slice(h * dim, (h + 1) * dim)
        key = unit(pairs[h][:, :dim]).astype(BF16)
        value = pairs[h][:, dim:].astype(BF16)
        k_ref[:, cols] = key
        v_ref[:, cols] = value
        add_summary(sum_ref, h, key, value, fade_ref, first)
        g, at = divmod(h, per)
        send_refs[g][at * dim : (at + 1) * dim, :] = sum_ref[h].astype(BF16)
    for g, send_ref in enumerate(send_refs):
        send_ref[per * dim :, :] = tail_ref[g]


def last_keys_values(me, gain, w, fade, prev, tail, xs, heads, dim, first):
    rows = xs[0].shape[0]
    groups = tail.shape[0]
    return pl.pallas_call(
        functools.partial(last_kernel, len(xs), heads, dim, first),
        in_specs=[SMEM] + [VMEM] * (5 + len(xs)),
        out_specs=[VMEM] * (2 + groups),
        out_shape=[struct((rows, heads * dim))] * 2
        + [struct((heads // groups * dim + TAIL, dim))] * groups,
        scratch_shapes=[pltpu.VMEM((heads, dim, dim), F32)],
        compiler_params=params(),
        cost_estimate=cost(3 * rows * w.size, 0),
        name="last_keys_values",
    )(me, gain, w, fade, prev, tail, *xs)


def queries_kernel(heads, dim, me_ref, gain_ref, w_ref, *refs):
    q_ref = refs[-1]
    parts = normed_parts(me_ref[0], gain_ref, refs[:-1])
    for h in range(heads):
        base = 3 * h * dim
        cols = slice(h * dim, (h + 1) * dim)
        q_ref[:, cols] = unit(projected(parts, w_ref, slice(base, base + dim))).astype(BF16)


def last_queries(me, gain, w, xs, heads, dim):
    rows = xs[0].shape[0]
    return pl.pallas_call(
        functools.partial(queries_kernel, heads, dim),
        in_specs=[SMEM] + [VMEM] * (2 + len(xs)),
        out_specs=VMEM,
        out_shape=struct((rows, heads * dim)),
        compiler_params=params(),
        cost_estimate=cost(2 * rows * w.size, 0),
        name="last_queries",
    )(me, gain, w, *xs)


def attention_kernel(chunk, heads, dim, keep_ref, scale_ref, q_ref, *refs):
    k_refs, v_refs, out_ref = refs[: chunk + 1], refs[chunk + 1 : -1], refs[-1]
    rows = q_ref.shape[0]
    per = BLOCK // rows
    block = chunk // per
    causal = lax.broadcasted_iota(jnp.int32, (rows, rows), 1) <= lax.broadcasted_iota(
        jnp.int32, (rows, rows), 0
    )
    ones = jnp.ones((rows, dim), BF16)
    for h in range(heads):
        cols = slice(h * dim, (h + 1) * dim)
        query = q_ref[:, cols]
        scale = scale_ref[0, h] * (1.0 / math.sqrt(dim))
        total = None
        for j in range(chunk + 1):
            powers = jnp.exp(dot_nt(query, k_refs[j][:, cols]) * scale)
            if j == chunk:
                powers = jnp.where(causal, powers, 0.0)
            part = dot(powers.astype(BF16), jnp.concatenate([v_refs[j][:, cols], ones], axis=1))
            if j // per < block:
                part = jnp.where(keep_ref[block, j // per] == 1, part, 0.0)
            total = part if total is None else total + part
        out_ref[:, cols] = (total[:, :dim] / total[:, dim:]).astype(BF16)


def attention(chunk, keep, scale, q, ks, vs, heads, dim):
    rows = q.shape[0]
    return pl.pallas_call(
        functools.partial(attention_kernel, chunk, heads, dim),
        in_specs=[SMEM, SMEM] + [VMEM] * (1 + len(ks) + len(vs)),
        out_specs=VMEM,
        out_shape=struct(q.shape),
        compiler_params=params(),
        cost_estimate=cost(
            (chunk + 1) * heads * 8 * rows * rows * dim, 0, (chunk + 1) * heads * rows * rows
        ),
        name="attention",
    )(keep, scale, q, *ks, *vs)


def body_and_decay(ref, h, dim):
    size = ref.shape[0] - TAIL
    high = ref[size + h : size + h + 1, :].astype(F32)
    low = ref[size + TAIL // 2 + h : size + TAIL // 2 + h + 1, :].astype(F32)
    return ref[h * dim : (h + 1) * dim, :].astype(F32), high + low


def scanned(place, refs, h, dim):
    count = len(refs)
    loaded = [body_and_decay(ref, h, dim) for ref in refs]
    state, since = jnp.zeros((dim, refs[0].shape[1]), F32), jnp.ones((1, refs[0].shape[1]), F32)
    before, before_decay = state, since
    for j in range(count):
        before = jnp.where(place == j, state, before)
        before_decay = jnp.where(place == j, since, before_decay)
        body, decay = loaded[0]
        for k in range(1, count):
            here = place == (j ^ k)
            body = jnp.where(here, loaded[k][0], body)
            decay = jnp.where(here, loaded[k][1], decay)
        state = decay * state + body
        since = since * decay
    return before, before_decay, state, since


def quad_kernel(heads, dim, place_ref, *refs):
    refs, (before_ref, decay_ref, total_ref) = refs[:-3], refs[-3:]
    size = heads * dim
    total_ref[size:, :] = jnp.zeros((TAIL, total_ref.shape[1]), BF16)
    for h in range(heads):
        rows = slice(h * dim, (h + 1) * dim)
        before, before_decay, state, since = scanned(place_ref[0], refs, h, dim)
        before_ref[rows, :] = before
        decay_ref[h : h + 1, :] = before_decay
        total_ref[rows, :] = state.astype(BF16)
        high = since.astype(BF16)
        total_ref[size + h : size + h + 1, :] = high
        low = (since - high.astype(F32)).astype(BF16)
        total_ref[size + TAIL // 2 + h : size + TAIL // 2 + h + 1, :] = low


def quad(place, loads, heads, dim):
    shape = loads[0].shape
    return pl.pallas_call(
        functools.partial(quad_kernel, heads, dim),
        in_specs=[SMEM] + [VMEM] * len(loads),
        out_specs=[VMEM] * 3,
        out_shape=[
            struct((heads * dim, shape[1]), F32),
            struct((TAIL // 2, shape[1]), F32),
            struct(shape),
        ],
        compiler_params=params(),
        cost_estimate=cost(loads[0].size * 40, 0),
        name="quad",
    )(place, *loads)


def entering_kernel(heads, dim, place_ref, before_ref, decay_ref, *refs):
    refs, out_ref = refs[:-1], refs[-1]
    for h in range(heads):
        rows = slice(h * dim, (h + 1) * dim)
        earlier = scanned(place_ref[0], refs, h, dim)[0]
        out_ref[rows, :] = (before_ref[rows, :] + decay_ref[h : h + 1, :] * earlier).astype(BF16)


def entering(place, before, decay, totals, heads, dim):
    return pl.pallas_call(
        functools.partial(entering_kernel, heads, dim),
        in_specs=[SMEM] + [VMEM] * (2 + len(totals)),
        out_specs=VMEM,
        out_shape=struct(before.shape),
        compiler_params=params(),
        cost_estimate=cost(before.size * 20, 0),
        name="entering",
    )(place, before, decay, *totals)


def recall_kernel(heads, dim, reading_ref, q_ref, local_ref, *refs):
    state_refs, out_ref = refs[:-1], refs[-1]
    per = heads // len(state_refs)
    for h in range(heads):
        cols = slice(h * dim, (h + 1) * dim)
        g, at = divmod(h, per)
        state = state_refs[g][at * dim : (at + 1) * dim, :]
        recalled = dot(q_ref[:, cols], state) * reading_ref[:, h : h + 1]
        out_ref[:, cols] = (local_ref[:, cols].astype(F32) + recalled).astype(BF16)


def recall(reading, q, local, states, heads, dim):
    return pl.pallas_call(
        functools.partial(recall_kernel, heads, dim),
        in_specs=[VMEM] * (3 + len(states)),
        out_specs=VMEM,
        out_shape=struct(q.shape),
        compiler_params=params(),
        cost_estimate=cost(4 * q.size * dim, 0),
        name="recall",
    )(reading, q, local, *states)


def project_kernel(shards, me_ref, own_ref, side_ref, own_w_ref, side_w_ref, *out_refs):
    width = out_refs[0].shape[1]
    own, side = own_ref[...], side_ref[...]
    for k in reversed(range(shards)):
        owner = lax.rem(me_ref[0] + k, shards)
        cols = pl.ds(pl.multiple_of(owner * width, width), width)
        out = dot(own, own_w_ref[:, cols]) + dot(side, side_w_ref[:, cols])
        out_refs[k][...] = out.astype(out_refs[k].dtype)


def project(me, own, side, own_w, side_w, shards):
    rows = own.shape[0]
    width = own_w.shape[1] // shards
    return pl.pallas_call(
        functools.partial(project_kernel, shards),
        in_specs=[SMEM] + [VMEM] * 4,
        out_specs=[VMEM] * shards,
        out_shape=[struct((rows, width))] * shards,
        compiler_params=params(),
        cost_estimate=cost(4 * rows * own_w.size, 0),
        name="project",
    )(me, own, side, own_w, side_w)


def finish_kernel(count, *refs):
    total = refs[0][...].astype(F32)
    for ref in refs[1:count]:
        total += ref[...].astype(F32)
    refs[-1][...] = total.astype(BF16)


def finish(parts, result, chunk, length):
    rows, width = parts[0].shape
    whole = pl.BlockSpec((rows, width), lambda i: (0, 0))
    more = [] if result is None else [result]
    return pl.pallas_call(
        functools.partial(finish_kernel, len(parts)),
        grid=(1,),
        in_specs=[whole] * len(parts) + [pl.BlockSpec(memory_space=pl.ANY)] * len(more),
        out_specs=pl.BlockSpec((rows, width), lambda i: (chunk, 0)),
        out_shape=struct((length, width)),
        input_output_aliases={len(parts): 0} if more else {},
        compiler_params=params(),
        cost_estimate=cost(rows * width * 2, rows * width * 6),
        name="finish",
    )(*parts, *more)


def per_device(
    residual_signal,
    prescale_amplifier,
    triple_projector,
    score_scaler,
    recall_retained_logshare,
    tile_retain_grid,
    recall_store_flags,
    emission_projector,
    sideways_coupling_coef,
):
    x = residual_signal[0]
    length = x.shape[0]
    chunks = length // CHUNK
    shards = lax.axis_size("head")
    blocks = lax.axis_size("tm")
    heads = triple_projector.shape[2]
    dim = emission_projector.shape[2]
    me = lax.axis_index("head").astype(jnp.int32).reshape(1)
    place = lax.axis_index("tm").astype(jnp.int32).reshape(1)
    swap_streams = [(0, 1), (1, 0)]
    tied = lambda *arrays: lax.optimization_barrier(arrays)

    received = []
    for c in range(chunks):
        piece = x[c * CHUNK : (c + 1) * CHUNK]
        if c > 2:
            piece, received[c - 3] = tied(piece, received[c - 3])
        xs = [piece]
        for k in range(1, shards):
            xs.append(lax.ppermute(piece, "head", [((d + k) % shards, d) for d in range(shards)]))
        received.append(xs)

    own_w = emission_projector[0].reshape(heads * dim, -1)
    side_w = lax.ppermute(
        sideways_coupling_coef[0].reshape(heads * dim, -1), "stream", swap_streams
    )
    groups = 2 if heads % 2 == 0 else 1
    fade, tail, *readings = prepare(
        recall_retained_logshare[0],
        recall_store_flags,
        dim,
        1.0 / math.sqrt(dim * length * blocks),
        groups,
    )
    gain = prescale_amplifier
    w = triple_projector[0].reshape(-1, 3 * heads * dim)

    qs, ks, vs, locals_ = [], [], [], []
    summary = None
    for c in range(chunks - 1):
        q, k, v, summary = qkv(
            me, gain, w, fade, summary, received[c], heads, dim, c * CHUNK
        )
        qs.append(q)
        ks.append(k)
        vs.append(v)
        locals_.append(attention(c, tile_retain_grid, score_scaler, q, ks, vs, heads, dim))
    summary, side_w, *locals_ = tied(summary, side_w, *locals_)
    k, v, *sents = last_keys_values(
        me, gain, w, fade, summary, tail, received[-1], heads, dim, (chunks - 1) * CHUNK
    )
    ks.append(k)
    vs.append(v)

    quad_size, per = min(4, blocks), heads // groups
    loads, befores, decays, totals, far, states = [], [], [], [], [], []
    for sent in sents:
        loads.append(
            [sent]
            + [
                lax.ppermute(sent, "tm", [(d, d ^ k) for d in range(blocks)])
                for k in range(1, quad_size)
            ]
        )
    for g in range(groups):
        before, decay, total = quad(lax.rem(place, quad_size), loads[g], per, dim)
        befores.append(before)
        decays.append(decay)
        totals.append(total)
        far.append(
            [
                lax.ppermute(total, "tm", [(d, d ^ (quad_size * k)) for d in range(blocks)])
                for k in range(1, blocks // quad_size)
            ]
        )
    qs.append(last_queries(me, gain, w, received[-1], heads, dim))
    locals_.append(attention(chunks - 1, tile_retain_grid, score_scaler, qs[-1], ks, vs, heads, dim))
    far, locals_[-1] = tied(far, locals_[-1])
    for g in range(groups):
        states.append(
            entering(
                lax.div(place, quad_size), befores[g], decays[g], [totals[g], *far[g]], per, dim
            )
        )

    result, finished = None, []
    for c in range(chunks):
        head_out = recall(readings[c], qs[c], locals_[c], states, heads, dim)
        side = lax.ppermute(head_out, "stream", swap_streams)
        outs = project(me, head_out, side, own_w, side_w, shards)
        parts = [outs[0]]
        for k in range(1, shards):
            parts.append(
                lax.ppermute(outs[k], "head", [(d, (d + k) % shards) for d in range(shards)])
            )
        finished.append(parts)
    for c in range(chunks):
        result = finish(finished[c], result, c, length)
    return result[None]


def solution(mesh):
    placed = (
        P("stream", "tm", "head"),
        P("stream", None),
        P("stream", None, "head", None),
        P("stream", "head"),
        P("stream", "head", "tm"),
        P("tm", None),
        P("tm"),
        P("stream", "head", None, None),
        P("stream", "head", None, None),
    )
    return jax.shard_map(
        per_device, mesh=mesh, in_specs=placed, out_specs=P("stream", "tm", "head"), check_vma=False
    )
```

```python
import functools
import math

import jax
import jax.numpy as jnp
from jax import lax
from jax.experimental import pallas as pl
from jax.experimental.pallas import tpu as pltpu
from jax.sharding import PartitionSpec as P

BLOCK = 512
CHUNK = 256
LAST = 128
TAIL = 16
EPSILON = 1e-06
F32 = jnp.float32
BF16 = jnp.bfloat16
SMEM = pl.BlockSpec(memory_space=pltpu.SMEM)
VMEM = pl.BlockSpec(memory_space=pltpu.VMEM)


def params():
    return pltpu.CompilerParams(vmem_limit_bytes=16 * 1024 * 1024)


def cost(flops, bytes_accessed, transcendentals=0):
    return pl.CostEstimate(
        flops=int(flops), bytes_accessed=int(bytes_accessed), transcendentals=int(transcendentals)
    )


def struct(shape, dtype=BF16):
    return jax.ShapeDtypeStruct(shape, dtype)


def dot(a, b):
    return lax.dot_general(a, b, (((1,), (0,)), ((), ())), preferred_element_type=F32)


def dot_nt(a, b):
    return lax.dot_general(a, b, (((1,), (1,)), ((), ())), preferred_element_type=F32)


def dot_tn(a, b):
    return lax.dot_general(a, b, (((0,), (0,)), ((), ())), preferred_element_type=F32)


def unit(values):
    return values * lax.rsqrt(jnp.mean(values * values, axis=-1, keepdims=True) + EPSILON)


def prepare_kernel(heads, factor, logs_ref, flags_ref, fade_ref, tail_ref, *refs):
    reading_refs, rows_ref = refs[:-1], refs[-1]
    length = logs_ref.shape[1]
    rows_ref[...] = jnp.zeros_like(rows_ref)
    rows_ref[:heads, :] = logs_ref[...]
    running = rows_ref[...]
    place = lax.broadcasted_iota(jnp.int32, running.shape, 1)
    step = 1
    while step < length:
        running += jnp.where(place >= step, pltpu.roll(running, step, 1), 0.0)
        step *= 2
    last = running[:, length - 1 :]
    chosen = jnp.zeros_like(running)
    for block in range(length // BLOCK):
        inside = (place >= block * BLOCK) & (place < (block + 1) * BLOCK)
        chosen = jnp.where(inside, flags_ref[block].astype(F32), chosen)
    fade_ref[...] = jnp.transpose(jnp.exp(last - running) * chosen)
    reading = jnp.transpose(jnp.exp(running) * factor)
    first = 0
    for ref in reading_refs:
        ref[...] = reading[first : first + ref.shape[0]]
        first += ref.shape[0]
    decay = jnp.exp(last)
    high = decay.astype(BF16).astype(F32)
    both = jnp.concatenate([high, decay - high], axis=0)
    tail_ref[...] = jnp.broadcast_to(both, tail_ref.shape).astype(BF16)


def prepare(logs, flags, dim, factor, sizes):
    heads, length = logs.shape
    lines = TAIL // 2
    return pl.pallas_call(
        functools.partial(prepare_kernel, heads, factor),
        in_specs=[VMEM, SMEM],
        out_specs=[VMEM] * (2 + len(sizes)),
        out_shape=[struct((length, lines), F32), struct((TAIL, dim))]
        + [struct((size, lines), F32) for size in sizes],
        scratch_shapes=[pltpu.VMEM((lines, length), F32)],
        compiler_params=params(),
        cost_estimate=cost(40 * lines * length, 0),
        name="prepare",
    )(logs, flags)


def normed_parts(me, gain_ref, x_refs):
    shards, width = len(x_refs), x_refs[0].shape[1]
    parts = [x[...].astype(F32) for x in x_refs]
    squares = sum(jnp.sum(p * p, axis=-1, keepdims=True) for p in parts)
    scale = lax.rsqrt(squares * (1.0 / (width * shards)) + EPSILON)
    out = []
    for k, part in enumerate(parts):
        owner = lax.rem(me + k, shards)
        rows = pl.ds(pl.multiple_of(owner * width, width), width)
        out.append(((part * scale * gain_ref[:, rows]).astype(BF16), rows))
    return out


def projected(parts, w_ref, cols):
    total = None
    for part, rows in parts:
        term = dot(part, w_ref[rows, cols])
        total = term if total is None else total + term
    return total


def add_summary(sum_ref, h, key, value, fade_ref, first):
    fade = fade_ref[first : first + key.shape[0], h : h + 1]
    sum_ref[h] += dot_tn((key.astype(F32) * fade).astype(BF16), value)


def qkv_kernel(heads, dim, first, me_ref, gain_ref, w_ref, fade_ref, *refs):
    refs, (q_ref, k_ref, v_ref, sum_ref) = refs[:-4], refs[-4:]
    if first == 0:
        sum_ref[...] = jnp.zeros_like(sum_ref)
        x_refs = refs
    else:
        sum_ref[...] = refs[0][...]
        x_refs = refs[1:]
    parts = normed_parts(me_ref[0], gain_ref, x_refs)
    wide = heads * dim
    thirds = [projected(parts, w_ref, slice(i * wide, (i + 1) * wide)) for i in range(3)]
    taken = lambda at: thirds[at * dim // wide][:, at * dim % wide : at * dim % wide + dim]
    for h in range(heads):
        cols = slice(h * dim, (h + 1) * dim)
        q_ref[:, cols] = unit(taken(3 * h)).astype(BF16)
        key = unit(taken(3 * h + 1)).astype(BF16)
        value = taken(3 * h + 2).astype(BF16)
        k_ref[:, cols] = key
        v_ref[:, cols] = value
        add_summary(sum_ref, h, key, value, fade_ref, first)


def qkv(me, gain, w, fade, prev, xs, heads, dim, first):
    rows = xs[0].shape[0]
    before = [prev] if first else []
    return pl.pallas_call(
        functools.partial(qkv_kernel, heads, dim, first),
        in_specs=[SMEM] + [VMEM] * (3 + len(before) + len(xs)),
        out_specs=[VMEM] * 4,
        out_shape=[struct((rows, heads * dim))] * 3 + [struct((heads, dim, dim), F32)],
        compiler_params=params(),
        cost_estimate=cost(4 * rows * w.size, 0),
        name="qkv",
    )(me, gain, w, fade, *before, *xs)


def last_kernel(heads, dim, first, me_ref, gain_ref, w_ref, fade_ref, prev_ref, tail_ref, *refs):
    x_refs, (k_ref, v_ref, send_ref, sum_ref) = refs[:-4], refs[-4:]
    sum_ref[...] = prev_ref[...]
    parts = normed_parts(me_ref[0], gain_ref, x_refs)
    pairs = [
        projected(parts, w_ref, slice((3 * h + 1) * dim, (3 * h + 3) * dim)) for h in range(heads)
    ]
    for h in range(heads):
        cols = slice(h * dim, (h + 1) * dim)
        key = unit(pairs[h][:, :dim]).astype(BF16)
        value = pairs[h][:, dim:].astype(BF16)
        k_ref[:, cols] = key
        v_ref[:, cols] = value
        add_summary(sum_ref, h, key, value, fade_ref, first)
        send_ref[cols, :] = sum_ref[h].astype(BF16)
    send_ref[heads * dim :, :] = tail_ref[...]


def last_keys_values(me, gain, w, fade, prev, tail, xs, heads, dim, first):
    rows = xs[0].shape[0]
    return pl.pallas_call(
        functools.partial(last_kernel, heads, dim, first),
        in_specs=[SMEM] + [VMEM] * (5 + len(xs)),
        out_specs=[VMEM] * 3,
        out_shape=[struct((rows, heads * dim))] * 2 + [struct((heads * dim + TAIL, dim))],
        scratch_shapes=[pltpu.VMEM((heads, dim, dim), F32)],
        compiler_params=params(),
        cost_estimate=cost(3 * rows * w.size, 0),
        name="last_keys_values",
    )(me, gain, w, fade, prev, tail, *xs)


def queries_kernel(heads, dim, me_ref, gain_ref, w_ref, *refs):
    q_ref = refs[-1]
    parts = normed_parts(me_ref[0], gain_ref, refs[:-1])
    for h in range(heads):
        base = 3 * h * dim
        cols = slice(h * dim, (h + 1) * dim)
        q_ref[:, cols] = unit(projected(parts, w_ref, slice(base, base + dim))).astype(BF16)


def last_queries(me, gain, w, xs, heads, dim):
    rows = xs[0].shape[0]
    return pl.pallas_call(
        functools.partial(queries_kernel, heads, dim),
        in_specs=[SMEM] + [VMEM] * (2 + len(xs)),
        out_specs=VMEM,
        out_shape=struct((rows, heads * dim)),
        compiler_params=params(),
        cost_estimate=cost(2 * rows * w.size, 0),
        name="last_queries",
    )(me, gain, w, *xs)


def attention_kernel(first, heads, dim, keep_ref, scale_ref, q_ref, *refs):
    count = len(refs) // 2
    k_refs, v_refs, out_ref = refs[:count], refs[count:-1], refs[-1]
    rows = q_ref.shape[0]
    block = first // BLOCK
    causal = lax.broadcasted_iota(jnp.int32, (rows, rows), 1) <= lax.broadcasted_iota(
        jnp.int32, (rows, rows), 0
    )
    for h in range(heads):
        cols = slice(h * dim, (h + 1) * dim)
        query = q_ref[:, cols]
        scale = scale_ref[0, h] * (1.0 / math.sqrt(dim))
        total, at = None, 0
        for j in range(count):
            keys = k_refs[j].shape[0]
            powers = jnp.exp(dot_nt(query, k_refs[j][:, cols]) * scale)
            if at == first:
                powers = jnp.where(causal, powers, 0.0)
            ones = jnp.ones((keys, dim), BF16)
            part = dot(powers.astype(BF16), jnp.concatenate([v_refs[j][:, cols], ones], axis=1))
            if at // BLOCK < block:
                part = jnp.where(keep_ref[block, at // BLOCK] == 1, part, 0.0)
            total = part if total is None else total + part
            at += keys
        out_ref[:, cols] = (total[:, :dim] / total[:, dim:]).astype(BF16)


def attention(first, keep, scale, q, ks, vs, heads, dim):
    rows = q.shape[0]
    return pl.pallas_call(
        functools.partial(attention_kernel, first, heads, dim),
        in_specs=[SMEM, SMEM] + [VMEM] * (1 + len(ks) + len(vs)),
        out_specs=VMEM,
        out_shape=struct(q.shape),
        compiler_params=params(),
        cost_estimate=cost(
            heads * 8 * rows * (first + rows) * dim, 0, heads * rows * (first + rows)
        ),
        name="attention",
    )(keep, scale, q, *ks, *vs)


def body_and_decay(ref, h, dim):
    size = ref.shape[0] - TAIL
    high = ref[size + h : size + h + 1, :].astype(F32)
    low = ref[size + TAIL // 2 + h : size + TAIL // 2 + h + 1, :].astype(F32)
    return ref[h * dim : (h + 1) * dim, :].astype(F32), high + low


def scanned(place, refs, h, dim):
    count = len(refs)
    loaded = [body_and_decay(ref, h, dim) for ref in refs]
    state, since = jnp.zeros((dim, refs[0].shape[1]), F32), jnp.ones((1, refs[0].shape[1]), F32)
    before, before_decay = state, since
    for j in range(count):
        before = jnp.where(place == j, state, before)
        before_decay = jnp.where(place == j, since, before_decay)
        body, decay = loaded[0]
        for k in range(1, count):
            here = place == (j ^ k)
            body = jnp.where(here, loaded[k][0], body)
            decay = jnp.where(here, loaded[k][1], decay)
        state = decay * state + body
        since = since * decay
    return before, before_decay, state, since


def quad_kernel(heads, dim, place_ref, *refs):
    refs, (before_ref, decay_ref, total_ref) = refs[:-3], refs[-3:]
    size = heads * dim
    total_ref[size:, :] = jnp.zeros((TAIL, total_ref.shape[1]), BF16)
    for h in range(heads):
        rows = slice(h * dim, (h + 1) * dim)
        before, before_decay, state, since = scanned(place_ref[0], refs, h, dim)
        before_ref[rows, :] = before
        decay_ref[h : h + 1, :] = before_decay
        total_ref[rows, :] = state.astype(BF16)
        high = since.astype(BF16)
        total_ref[size + h : size + h + 1, :] = high
        low = (since - high.astype(F32)).astype(BF16)
        total_ref[size + TAIL // 2 + h : size + TAIL // 2 + h + 1, :] = low


def quad(place, loads, heads, dim):
    shape = loads[0].shape
    return pl.pallas_call(
        functools.partial(quad_kernel, heads, dim),
        in_specs=[SMEM] + [VMEM] * len(loads),
        out_specs=[VMEM] * 3,
        out_shape=[
            struct((heads * dim, shape[1]), F32),
            struct((TAIL // 2, shape[1]), F32),
            struct(shape),
        ],
        compiler_params=params(),
        cost_estimate=cost(loads[0].size * 40, 0),
        name="quad",
    )(place, *loads)


def entering_kernel(heads, dim, place_ref, before_ref, decay_ref, *refs):
    refs, out_ref = refs[:-1], refs[-1]
    for h in range(heads):
        rows = slice(h * dim, (h + 1) * dim)
        earlier = scanned(place_ref[0], refs, h, dim)[0]
        out_ref[rows, :] = (before_ref[rows, :] + decay_ref[h : h + 1, :] * earlier).astype(BF16)


def entering(place, before, decay, totals, heads, dim):
    return pl.pallas_call(
        functools.partial(entering_kernel, heads, dim),
        in_specs=[SMEM] + [VMEM] * (2 + len(totals)),
        out_specs=VMEM,
        out_shape=struct(before.shape),
        compiler_params=params(),
        cost_estimate=cost(before.size * 20, 0),
        name="entering",
    )(place, before, decay, *totals)


def recall_kernel(heads, dim, reading_ref, q_ref, local_ref, state_ref, out_ref):
    for h in range(heads):
        cols = slice(h * dim, (h + 1) * dim)
        recalled = dot(q_ref[:, cols], state_ref[cols, :]) * reading_ref[:, h : h + 1]
        out_ref[:, cols] = (local_ref[:, cols].astype(F32) + recalled).astype(BF16)


def recall(reading, q, local, state, heads, dim):
    return pl.pallas_call(
        functools.partial(recall_kernel, heads, dim),
        in_specs=[VMEM] * 4,
        out_specs=VMEM,
        out_shape=struct(q.shape),
        compiler_params=params(),
        cost_estimate=cost(4 * q.size * dim, 0),
        name="recall",
    )(reading, q, local, state)


def project_kernel(shards, me_ref, own_ref, side_ref, own_w_ref, side_w_ref, *out_refs):
    width = out_refs[0].shape[1]
    own, side = own_ref[...], side_ref[...]
    for k in reversed(range(shards)):
        owner = lax.rem(me_ref[0] + k, shards)
        cols = pl.ds(pl.multiple_of(owner * width, width), width)
        out = dot(own, own_w_ref[:, cols]) + dot(side, side_w_ref[:, cols])
        out_refs[k][...] = out.astype(out_refs[k].dtype)


def project(me, own, side, own_w, side_w, shards):
    rows = own.shape[0]
    width = own_w.shape[1] // shards
    return pl.pallas_call(
        functools.partial(project_kernel, shards),
        in_specs=[SMEM] + [VMEM] * 4,
        out_specs=[VMEM] * shards,
        out_shape=[struct((rows, width))] * shards,
        compiler_params=params(),
        cost_estimate=cost(4 * rows * own_w.size, 0),
        name="project",
    )(me, own, side, own_w, side_w)


def finish_kernel(count, *refs):
    total = refs[0][...].astype(F32)
    for ref in refs[1:count]:
        total += ref[...].astype(F32)
    refs[-1][...] = total.astype(BF16)


def finish(parts, result, first, length):
    rows, width = parts[0].shape
    chunk = first // rows
    whole = pl.BlockSpec((rows, width), lambda i: (0, 0))
    more = [] if result is None else [result]
    return pl.pallas_call(
        functools.partial(finish_kernel, len(parts)),
        grid=(1,),
        in_specs=[whole] * len(parts) + [pl.BlockSpec(memory_space=pl.ANY)] * len(more),
        out_specs=pl.BlockSpec((rows, width), lambda i: (chunk, 0)),
        out_shape=struct((length, width)),
        input_output_aliases={len(parts): 0} if more else {},
        compiler_params=params(),
        cost_estimate=cost(rows * width * 2, rows * width * 6),
        name="finish",
    )(*parts, *more)


def per_device(
    residual_signal,
    prescale_amplifier,
    triple_projector,
    score_scaler,
    recall_retained_logshare,
    tile_retain_grid,
    recall_store_flags,
    emission_projector,
    sideways_coupling_coef,
):
    x = residual_signal[0]
    length = x.shape[0]
    sizes = [CHUNK] * (length // CHUNK - 1) + [LAST] * (CHUNK // LAST)
    firsts = [sum(sizes[:c]) for c in range(len(sizes))]
    chunks = len(sizes)
    shards = lax.axis_size("head")
    blocks = lax.axis_size("tm")
    heads = triple_projector.shape[2]
    dim = emission_projector.shape[2]
    me = lax.axis_index("head").astype(jnp.int32).reshape(1)
    place = lax.axis_index("tm").astype(jnp.int32).reshape(1)
    swap_streams = [(0, 1), (1, 0)]
    tied = lambda *arrays: lax.optimization_barrier(arrays)

    own_w = emission_projector[0].reshape(heads * dim, -1)
    side_w = lax.ppermute(
        sideways_coupling_coef[0].reshape(heads * dim, -1), "stream", swap_streams
    )
    fade, tail, *readings = prepare(
        recall_retained_logshare[0],
        recall_store_flags,
        dim,
        1.0 / math.sqrt(dim * length * blocks),
        sizes,
    )
    received = []
    for first, size in zip(firsts, sizes):
        piece = x[first : first + size]
        if size < CHUNK:
            piece, fade = tied(piece, fade)
        xs = [piece]
        for k in range(1, shards):
            xs.append(lax.ppermute(piece, "head", [((d + k) % shards, d) for d in range(shards)]))
        received.append(xs)
    gain = prescale_amplifier
    w = triple_projector[0].reshape(-1, 3 * heads * dim)

    qs, ks, vs, locals_ = [], [], [], []
    summary = None
    for c, first in enumerate(firsts[:-1]):
        q, k, v, summary = qkv(me, gain, w, fade, summary, received[c], heads, dim, first)
        qs.append(q)
        ks.append(k)
        vs.append(v)
        locals_.append(attention(first, tile_retain_grid, score_scaler, q, ks, vs, heads, dim))
    summary, *locals_ = tied(summary, *locals_)
    k, v, sent = last_keys_values(
        me, gain, w, fade, summary, tail, received[-1], heads, dim, firsts[-1]
    )
    ks.append(k)
    vs.append(v)

    quad_size = min(4, blocks)
    loads = [sent] + [
        lax.ppermute(sent, "tm", [(d, d ^ k) for d in range(blocks)]) for k in range(1, quad_size)
    ]
    qs.append(last_queries(me, gain, w, received[-1], heads, dim))
    locals_.append(attention(firsts[-1], tile_retain_grid, score_scaler, qs[-1], ks, vs, heads, dim))
    *loads, locals_[-1] = tied(*loads, locals_[-1])
    before, decay, total = quad(lax.rem(place, quad_size), loads, heads, dim)
    totals = [total] + [
        lax.ppermute(total, "tm", [(d, d ^ (quad_size * k)) for d in range(blocks)])
        for k in range(1, blocks // quad_size)
    ]
    state = entering(lax.div(place, quad_size), before, decay, totals, heads, dim)

    result = None
    for c in [chunks - 2, *range(chunks - 2), chunks - 1]:
        head_out = recall(readings[c], qs[c], locals_[c], state, heads, dim)
        side = lax.ppermute(head_out, "stream", swap_streams)
        outs = project(me, head_out, side, own_w, side_w, shards)
        parts = [outs[0]]
        for k in range(1, shards):
            parts.append(
                lax.ppermute(outs[k], "head", [(d, (d + k) % shards) for d in range(shards)])
            )
        if result is None:
            state, parts[0] = tied(state, parts[0])
        result = finish(parts, result, firsts[c], length)
    return result[None]


def solution(mesh):
    placed = (
        P("stream", "tm", "head"),
        P("stream", None),
        P("stream", None, "head", None),
        P("stream", "head"),
        P("stream", "head", "tm"),
        P("tm", None),
        P("tm"),
        P("stream", "head", None, None),
        P("stream", "head", None, None),
    )
    return jax.shard_map(
        per_device, mesh=mesh, in_specs=placed, out_specs=P("stream", "tm", "head"), check_vma=False
    )
```

```python
import functools
import math

import jax
import jax.numpy as jnp
from jax import lax
from jax.experimental import pallas as pl
from jax.experimental.pallas import tpu as pltpu
from jax.sharding import PartitionSpec as P

BLOCK = 512
CHUNK = 256
LAST = 128
TAIL = 16
EPSILON = 1e-06
F32 = jnp.float32
BF16 = jnp.bfloat16
SMEM = pl.BlockSpec(memory_space=pltpu.SMEM)
VMEM = pl.BlockSpec(memory_space=pltpu.VMEM)


def params():
    return pltpu.CompilerParams(vmem_limit_bytes=16 * 1024 * 1024)


def cost(flops, bytes_accessed, transcendentals=0):
    return pl.CostEstimate(
        flops=int(flops), bytes_accessed=int(bytes_accessed), transcendentals=int(transcendentals)
    )


def struct(shape, dtype=BF16):
    return jax.ShapeDtypeStruct(shape, dtype)


def dot(a, b):
    return lax.dot_general(a, b, (((1,), (0,)), ((), ())), preferred_element_type=F32)


def dot_nt(a, b):
    return lax.dot_general(a, b, (((1,), (1,)), ((), ())), preferred_element_type=F32)


def dot_tn(a, b):
    return lax.dot_general(a, b, (((0,), (0,)), ((), ())), preferred_element_type=F32)


def unit(values):
    return values * lax.rsqrt(jnp.mean(values * values, axis=-1, keepdims=True) + EPSILON)


def prepare_kernel(heads, factor, logs_ref, flags_ref, fade_ref, tail_ref, *refs):
    reading_refs, rows_ref = refs[:-1], refs[-1]
    length = logs_ref.shape[1]
    rows_ref[...] = jnp.zeros_like(rows_ref)
    rows_ref[:heads, :] = logs_ref[...]
    running = rows_ref[...]
    place = lax.broadcasted_iota(jnp.int32, running.shape, 1)
    step = 1
    while step < length:
        running += jnp.where(place >= step, pltpu.roll(running, step, 1), 0.0)
        step *= 2
    last = running[:, length - 1 :]
    chosen = jnp.zeros_like(running)
    for block in range(length // BLOCK):
        inside = (place >= block * BLOCK) & (place < (block + 1) * BLOCK)
        chosen = jnp.where(inside, flags_ref[block].astype(F32), chosen)
    fade_ref[...] = jnp.transpose(jnp.exp(last - running) * chosen)
    reading = jnp.transpose(jnp.exp(running) * factor)
    first = 0
    for ref in reading_refs:
        ref[...] = reading[first : first + ref.shape[0]]
        first += ref.shape[0]
    decay = jnp.exp(last)
    high = decay.astype(BF16).astype(F32)
    both = jnp.concatenate([high, decay - high], axis=0)
    tail_ref[...] = jnp.broadcast_to(both, tail_ref.shape).astype(BF16)


def prepare(logs, flags, dim, factor, sizes):
    heads, length = logs.shape
    lines = TAIL // 2
    return pl.pallas_call(
        functools.partial(prepare_kernel, heads, factor),
        in_specs=[VMEM, SMEM],
        out_specs=[VMEM] * (2 + len(sizes)),
        out_shape=[struct((length, lines), F32), struct((TAIL, dim))]
        + [struct((size, lines), F32) for size in sizes],
        scratch_shapes=[pltpu.VMEM((lines, length), F32)],
        compiler_params=params(),
        cost_estimate=cost(40 * lines * length, 0),
        name="prepare",
    )(logs, flags)


def normed_parts(gain_ref, x_refs):
    me = lax.axis_index("head")
    shards, width = len(x_refs), x_refs[0].shape[1]
    parts = [x[...].astype(F32) for x in x_refs]
    squares = sum(jnp.sum(p * p, axis=-1, keepdims=True) for p in parts)
    scale = lax.rsqrt(squares * (1.0 / (width * shards)) + EPSILON)
    out = []
    for k, part in enumerate(parts):
        owner = lax.rem(me + k, shards)
        rows = pl.ds(pl.multiple_of(owner * width, width), width)
        out.append(((part * scale * gain_ref[:, rows]).astype(BF16), rows))
    return out


def projected(parts, w_ref, cols):
    total = None
    for part, rows in parts:
        term = dot(part, w_ref[rows, cols])
        total = term if total is None else total + term
    return total


def add_summary(sum_ref, h, key, value, fade_ref, first):
    fade = fade_ref[first : first + key.shape[0], h : h + 1]
    sum_ref[h] += dot_tn((key.astype(F32) * fade).astype(BF16), value)


def qkv_kernel(heads, dim, first, gain_ref, w_ref, fade_ref, *refs):
    refs, (q_ref, k_ref, v_ref, sum_ref) = refs[:-4], refs[-4:]
    if first == 0:
        sum_ref[...] = jnp.zeros_like(sum_ref)
        x_refs = refs
    else:
        sum_ref[...] = refs[0][...]
        x_refs = refs[1:]
    parts = normed_parts(gain_ref, x_refs)
    wide = heads * dim
    thirds = [projected(parts, w_ref, slice(i * wide, (i + 1) * wide)) for i in range(3)]
    taken = lambda at: thirds[at * dim // wide][:, at * dim % wide : at * dim % wide + dim]
    for h in range(heads):
        cols = slice(h * dim, (h + 1) * dim)
        q_ref[:, cols] = unit(taken(3 * h)).astype(BF16)
        key = unit(taken(3 * h + 1)).astype(BF16)
        value = taken(3 * h + 2).astype(BF16)
        k_ref[:, cols] = key
        v_ref[:, cols] = value
        add_summary(sum_ref, h, key, value, fade_ref, first)


def qkv(gain, w, fade, prev, xs, heads, dim, first):
    rows = xs[0].shape[0]
    before = [prev] if first else []
    return pl.pallas_call(
        functools.partial(qkv_kernel, heads, dim, first),
        in_specs=[VMEM] * (3 + len(before) + len(xs)),
        out_specs=[VMEM] * 4,
        out_shape=[struct((rows, heads * dim))] * 3 + [struct((heads, dim, dim), F32)],
        compiler_params=params(),
        cost_estimate=cost(4 * rows * w.size, 0),
        name="qkv",
    )(gain, w, fade, *before, *xs)


def last_kernel(heads, dim, first, gain_ref, w_ref, fade_ref, prev_ref, tail_ref, *refs):
    x_refs, (k_ref, v_ref, send_ref, sum_ref) = refs[:-4], refs[-4:]
    sum_ref[...] = prev_ref[...]
    parts = normed_parts(gain_ref, x_refs)
    pairs = [
        projected(parts, w_ref, slice((3 * h + 1) * dim, (3 * h + 3) * dim)) for h in range(heads)
    ]
    for h in range(heads):
        cols = slice(h * dim, (h + 1) * dim)
        key = unit(pairs[h][:, :dim]).astype(BF16)
        value = pairs[h][:, dim:].astype(BF16)
        k_ref[:, cols] = key
        v_ref[:, cols] = value
        add_summary(sum_ref, h, key, value, fade_ref, first)
        send_ref[cols, :] = sum_ref[h].astype(BF16)
    send_ref[heads * dim :, :] = tail_ref[...]


def last_keys_values(gain, w, fade, prev, tail, xs, heads, dim, first):
    rows = xs[0].shape[0]
    return pl.pallas_call(
        functools.partial(last_kernel, heads, dim, first),
        in_specs=[VMEM] * (5 + len(xs)),
        out_specs=[VMEM] * 3,
        out_shape=[struct((rows, heads * dim))] * 2 + [struct((heads * dim + TAIL, dim))],
        scratch_shapes=[pltpu.VMEM((heads, dim, dim), F32)],
        compiler_params=params(),
        cost_estimate=cost(3 * rows * w.size, 0),
        name="last_keys_values",
    )(gain, w, fade, prev, tail, *xs)


def queries_kernel(heads, dim, gain_ref, w_ref, *refs):
    q_ref = refs[-1]
    parts = normed_parts(gain_ref, refs[:-1])
    for h in range(heads):
        base = 3 * h * dim
        cols = slice(h * dim, (h + 1) * dim)
        q_ref[:, cols] = unit(projected(parts, w_ref, slice(base, base + dim))).astype(BF16)


def last_queries(gain, w, xs, heads, dim):
    rows = xs[0].shape[0]
    return pl.pallas_call(
        functools.partial(queries_kernel, heads, dim),
        in_specs=[VMEM] * (2 + len(xs)),
        out_specs=VMEM,
        out_shape=struct((rows, heads * dim)),
        compiler_params=params(),
        cost_estimate=cost(2 * rows * w.size, 0),
        name="last_queries",
    )(gain, w, *xs)


def attention_kernel(first, heads, dim, keep_ref, scale_ref, q_ref, *refs):
    count = len(refs) // 2
    k_refs, v_refs, out_ref = refs[:count], refs[count:-1], refs[-1]
    rows = q_ref.shape[0]
    block = first // BLOCK
    causal = lax.broadcasted_iota(jnp.int32, (rows, rows), 1) <= lax.broadcasted_iota(
        jnp.int32, (rows, rows), 0
    )
    for h in range(heads):
        cols = slice(h * dim, (h + 1) * dim)
        query = q_ref[:, cols]
        scale = scale_ref[0, h] * (1.0 / math.sqrt(dim))
        total, at = None, 0
        for j in range(count):
            keys = k_refs[j].shape[0]
            powers = jnp.exp(dot_nt(query, k_refs[j][:, cols]) * scale)
            if at == first:
                powers = jnp.where(causal, powers, 0.0)
            ones = jnp.ones((keys, dim), BF16)
            part = dot(powers.astype(BF16), jnp.concatenate([v_refs[j][:, cols], ones], axis=1))
            if at // BLOCK < block:
                part = jnp.where(keep_ref[block, at // BLOCK] == 1, part, 0.0)
            total = part if total is None else total + part
            at += keys
        out_ref[:, cols] = (total[:, :dim] / total[:, dim:]).astype(BF16)


def attention(first, keep, scale, q, ks, vs, heads, dim):
    rows = q.shape[0]
    return pl.pallas_call(
        functools.partial(attention_kernel, first, heads, dim),
        in_specs=[SMEM, SMEM] + [VMEM] * (1 + len(ks) + len(vs)),
        out_specs=VMEM,
        out_shape=struct(q.shape),
        compiler_params=params(),
        cost_estimate=cost(
            heads * 8 * rows * (first + rows) * dim, 0, heads * rows * (first + rows)
        ),
        name="attention",
    )(keep, scale, q, *ks, *vs)


def body_and_decay(ref, h, dim):
    size = ref.shape[0] - TAIL
    high = ref[size + h : size + h + 1, :].astype(F32)
    low = ref[size + TAIL // 2 + h : size + TAIL // 2 + h + 1, :].astype(F32)
    return ref[h * dim : (h + 1) * dim, :].astype(F32), high + low


def scanned(place, refs, h, dim):
    count = len(refs)
    loaded = [body_and_decay(ref, h, dim) for ref in refs]
    state, since = jnp.zeros((dim, refs[0].shape[1]), F32), jnp.ones((1, refs[0].shape[1]), F32)
    before, before_decay = state, since
    for j in range(count):
        before = jnp.where(place == j, state, before)
        before_decay = jnp.where(place == j, since, before_decay)
        body, decay = loaded[0]
        for k in range(1, count):
            here = place == (j ^ k)
            body = jnp.where(here, loaded[k][0], body)
            decay = jnp.where(here, loaded[k][1], decay)
        state = decay * state + body
        since = since * decay
    return before, before_decay, state, since


def quad_kernel(heads, dim, *refs):
    place = lax.rem(lax.axis_index("tm"), len(refs) - 3)
    refs, (before_ref, decay_ref, total_ref) = refs[:-3], refs[-3:]
    size = heads * dim
    total_ref[size:, :] = jnp.zeros((TAIL, total_ref.shape[1]), BF16)
    for h in range(heads):
        rows = slice(h * dim, (h + 1) * dim)
        before, before_decay, state, since = scanned(place, refs, h, dim)
        before_ref[rows, :] = before
        decay_ref[h : h + 1, :] = before_decay
        total_ref[rows, :] = state.astype(BF16)
        high = since.astype(BF16)
        total_ref[size + h : size + h + 1, :] = high
        low = (since - high.astype(F32)).astype(BF16)
        total_ref[size + TAIL // 2 + h : size + TAIL // 2 + h + 1, :] = low


def quad(loads, heads, dim):
    shape = loads[0].shape
    return pl.pallas_call(
        functools.partial(quad_kernel, heads, dim),
        in_specs=[VMEM] * len(loads),
        out_specs=[VMEM] * 3,
        out_shape=[
            struct((heads * dim, shape[1]), F32),
            struct((TAIL // 2, shape[1]), F32),
            struct(shape),
        ],
        compiler_params=params(),
        cost_estimate=cost(loads[0].size * 40, 0),
        name="quad",
    )(*loads)


def entering_kernel(heads, dim, quad_size, before_ref, decay_ref, *refs):
    refs, out_ref = refs[:-1], refs[-1]
    place = lax.div(lax.axis_index("tm"), quad_size)
    for h in range(heads):
        rows = slice(h * dim, (h + 1) * dim)
        earlier = scanned(place, refs, h, dim)[0]
        out_ref[rows, :] = (before_ref[rows, :] + decay_ref[h : h + 1, :] * earlier).astype(BF16)


def entering(quad_size, before, decay, totals, heads, dim):
    return pl.pallas_call(
        functools.partial(entering_kernel, heads, dim, quad_size),
        in_specs=[VMEM] * (2 + len(totals)),
        out_specs=VMEM,
        out_shape=struct(before.shape),
        compiler_params=params(),
        cost_estimate=cost(before.size * 20, 0),
        name="entering",
    )(before, decay, *totals)


def recall_kernel(heads, dim, reading_ref, q_ref, local_ref, state_ref, out_ref):
    for h in range(heads):
        cols = slice(h * dim, (h + 1) * dim)
        recalled = dot(q_ref[:, cols], state_ref[cols, :]) * reading_ref[:, h : h + 1]
        out_ref[:, cols] = (local_ref[:, cols].astype(F32) + recalled).astype(BF16)


def recall(reading, q, local, state, heads, dim):
    return pl.pallas_call(
        functools.partial(recall_kernel, heads, dim),
        in_specs=[VMEM] * 4,
        out_specs=VMEM,
        out_shape=struct(q.shape),
        compiler_params=params(),
        cost_estimate=cost(4 * q.size * dim, 0),
        name="recall",
    )(reading, q, local, state)


def project_kernel(shards, own_ref, side_ref, own_w_ref, side_w_ref, *out_refs):
    width = out_refs[0].shape[1]
    own, side = own_ref[...], side_ref[...]
    for k in reversed(range(shards)):
        owner = lax.rem(lax.axis_index("head") + k, shards)
        cols = pl.ds(pl.multiple_of(owner * width, width), width)
        out = dot(own, own_w_ref[:, cols]) + dot(side, side_w_ref[:, cols])
        out_refs[k][...] = out.astype(out_refs[k].dtype)


def project(own, side, own_w, side_w, shards):
    rows = own.shape[0]
    width = own_w.shape[1] // shards
    return pl.pallas_call(
        functools.partial(project_kernel, shards),
        in_specs=[VMEM] * 4,
        out_specs=[VMEM] * shards,
        out_shape=[struct((rows, width))] * shards,
        compiler_params=params(),
        cost_estimate=cost(4 * rows * own_w.size, 0),
        name="project",
    )(own, side, own_w, side_w)


def finish_kernel(count, *refs):
    total = refs[0][...].astype(F32)
    for ref in refs[1:count]:
        total += ref[...].astype(F32)
    refs[-1][...] = total.astype(BF16)


def finish(parts, result, first, length):
    rows, width = parts[0].shape
    chunk = first // rows
    whole = pl.BlockSpec((rows, width), lambda i: (0, 0))
    more = [] if result is None else [result]
    return pl.pallas_call(
        functools.partial(finish_kernel, len(parts)),
        grid=(1,),
        in_specs=[whole] * len(parts) + [pl.BlockSpec(memory_space=pl.ANY)] * len(more),
        out_specs=pl.BlockSpec((rows, width), lambda i: (chunk, 0)),
        out_shape=struct((length, width)),
        input_output_aliases={len(parts): 0} if more else {},
        compiler_params=params(),
        cost_estimate=cost(rows * width * 2, rows * width * 6),
        name="finish",
    )(*parts, *more)


def per_device(
    residual_signal,
    prescale_amplifier,
    triple_projector,
    score_scaler,
    recall_retained_logshare,
    tile_retain_grid,
    recall_store_flags,
    emission_projector,
    sideways_coupling_coef,
):
    x = residual_signal[0]
    length = x.shape[0]
    sizes = [CHUNK] * (length // CHUNK - 1) + [LAST] * (CHUNK // LAST)
    firsts = [sum(sizes[:c]) for c in range(len(sizes))]
    chunks = len(sizes)
    shards = lax.axis_size("head")
    blocks = lax.axis_size("tm")
    heads = triple_projector.shape[2]
    dim = emission_projector.shape[2]
    swap_streams = [(0, 1), (1, 0)]
    tied = lambda *arrays: lax.optimization_barrier(arrays)

    own_w = emission_projector[0].reshape(heads * dim, -1)
    side_w = lax.ppermute(
        sideways_coupling_coef[0].reshape(heads * dim, -1), "stream", swap_streams
    )
    fade, tail, *readings = prepare(
        recall_retained_logshare[0],
        recall_store_flags,
        dim,
        1.0 / math.sqrt(dim * length * blocks),
        sizes,
    )
    pieces = [x[first : first + size] for first, size in zip(firsts, sizes)]
    received = []
    for c in range(chunks):
        if c == chunks - 2:
            pieces[c], pieces[c + 1], received[0] = tied(pieces[c], pieces[c + 1], received[0])
        xs = [pieces[c]]
        for k in range(1, shards):
            xs.append(
                lax.ppermute(pieces[c], "head", [((d + k) % shards, d) for d in range(shards)])
            )
        received.append(xs)
    gain = prescale_amplifier
    w = triple_projector[0].reshape(-1, 3 * heads * dim)

    qs, ks, vs, locals_ = [], [], [], []
    summary = None
    for c, first in enumerate(firsts[:-1]):
        q, k, v, summary = qkv(gain, w, fade, summary, received[c], heads, dim, first)
        qs.append(q)
        ks.append(k)
        vs.append(v)
        locals_.append(attention(first, tile_retain_grid, score_scaler, q, ks, vs, heads, dim))
    summary, *locals_ = tied(summary, *locals_)
    k, v, sent = last_keys_values(
        gain, w, fade, summary, tail, received[-1], heads, dim, firsts[-1]
    )
    ks.append(k)
    vs.append(v)

    quad_size = min(4, blocks)
    loads = [sent] + [
        lax.ppermute(sent, "tm", [(d, d ^ k) for d in range(blocks)]) for k in range(1, quad_size)
    ]
    qs.append(last_queries(gain, w, received[-1], heads, dim))
    locals_.append(attention(firsts[-1], tile_retain_grid, score_scaler, qs[-1], ks, vs, heads, dim))
    *loads, locals_[-1] = tied(*loads, locals_[-1])
    before, decay, total = quad(loads, heads, dim)
    totals = [total] + [
        lax.ppermute(total, "tm", [(d, d ^ (quad_size * k)) for d in range(blocks)])
        for k in range(1, blocks // quad_size)
    ]
    state = entering(quad_size, before, decay, totals, heads, dim)

    result = None
    for c in [chunks - 2, *range(chunks - 2), chunks - 1]:
        head_out = recall(readings[c], qs[c], locals_[c], state, heads, dim)
        side = lax.ppermute(head_out, "stream", swap_streams)
        outs = project(head_out, side, own_w, side_w, shards)
        parts = [outs[0]]
        for k in range(1, shards):
            parts.append(
                lax.ppermute(outs[k], "head", [(d, (d + k) % shards) for d in range(shards)])
            )
        if result is None:
            state, parts[0] = tied(state, parts[0])
        result = finish(parts, result, firsts[c], length)
    return result[None]


def solution(mesh):
    placed = (
        P("stream", "tm", "head"),
        P("stream", None),
        P("stream", None, "head", None),
        P("stream", "head"),
        P("stream", "head", "tm"),
        P("tm", None),
        P("tm"),
        P("stream", "head", None, None),
        P("stream", "head", None, None),
    )
    return jax.shard_map(
        per_device, mesh=mesh, in_specs=placed, out_specs=P("stream", "tm", "head"), check_vma=False
    )
```

```python
import functools
import math

import jax
import jax.numpy as jnp
from jax import lax
from jax.experimental import pallas as pl
from jax.experimental.pallas import tpu as pltpu
from jax.sharding import PartitionSpec as P

BLOCK = 512
CHUNK = 256
LAST = 128
TAIL = 16
EPSILON = 1e-06
F32 = jnp.float32
BF16 = jnp.bfloat16
SMEM = pl.BlockSpec(memory_space=pltpu.SMEM)
VMEM = pl.BlockSpec(memory_space=pltpu.VMEM)


def params():
    return pltpu.CompilerParams(vmem_limit_bytes=16 * 1024 * 1024)


def cost(flops, bytes_accessed, transcendentals=0):
    return pl.CostEstimate(
        flops=int(flops), bytes_accessed=int(bytes_accessed), transcendentals=int(transcendentals)
    )


def struct(shape, dtype=BF16):
    return jax.ShapeDtypeStruct(shape, dtype)


def dot(a, b):
    return lax.dot_general(a, b, (((1,), (0,)), ((), ())), preferred_element_type=F32)


def dot_nt(a, b):
    return lax.dot_general(a, b, (((1,), (1,)), ((), ())), preferred_element_type=F32)


def dot_tn(a, b):
    return lax.dot_general(a, b, (((0,), (0,)), ((), ())), preferred_element_type=F32)


def unit(values):
    return values * lax.rsqrt(jnp.mean(values * values, axis=-1, keepdims=True) + EPSILON)


def prepare_kernel(heads, factor, logs_ref, flags_ref, fade_ref, tail_ref, *refs):
    reading_refs, rows_ref = refs[:-1], refs[-1]
    length = logs_ref.shape[1]
    rows_ref[...] = jnp.zeros_like(rows_ref)
    rows_ref[:heads, :] = logs_ref[...]
    running = rows_ref[...]
    place = lax.broadcasted_iota(jnp.int32, running.shape, 1)
    step = 1
    while step < length:
        running += jnp.where(place >= step, pltpu.roll(running, step, 1), 0.0)
        step *= 2
    last = running[:, length - 1 :]
    chosen = jnp.zeros_like(running)
    for block in range(length // BLOCK):
        inside = (place >= block * BLOCK) & (place < (block + 1) * BLOCK)
        chosen = jnp.where(inside, flags_ref[block].astype(F32), chosen)
    fade_ref[...] = jnp.transpose(jnp.exp(last - running) * chosen)
    reading = jnp.transpose(jnp.exp(running) * factor)
    first = 0
    for ref in reading_refs:
        ref[...] = reading[first : first + ref.shape[0]]
        first += ref.shape[0]
    decay = jnp.exp(last)
    high = decay.astype(BF16).astype(F32)
    both = jnp.concatenate([high, decay - high], axis=0)
    tail_ref[...] = jnp.broadcast_to(both, tail_ref.shape).astype(BF16)


def prepare(logs, flags, dim, factor, sizes):
    heads, length = logs.shape
    lines = TAIL // 2
    return pl.pallas_call(
        functools.partial(prepare_kernel, heads, factor),
        in_specs=[VMEM, SMEM],
        out_specs=[VMEM] * (2 + len(sizes)),
        out_shape=[struct((length, lines), F32), struct((TAIL, dim))]
        + [struct((size, lines), F32) for size in sizes],
        scratch_shapes=[pltpu.VMEM((lines, length), F32)],
        compiler_params=params(),
        cost_estimate=cost(40 * lines * length, 0),
        name="prepare",
    )(logs, flags)


def normed_parts(gain_ref, x_refs):
    me = lax.axis_index("head")
    shards, width = len(x_refs), x_refs[0].shape[1]
    parts = [x[...].astype(F32) for x in x_refs]
    squares = sum(jnp.sum(p * p, axis=-1, keepdims=True) for p in parts)
    scale = lax.rsqrt(squares * (1.0 / (width * shards)) + EPSILON)
    out = []
    for k, part in enumerate(parts):
        owner = lax.rem(me + k, shards)
        rows = pl.ds(pl.multiple_of(owner * width, width), width)
        out.append(((part * scale * gain_ref[:, rows]).astype(BF16), rows))
    return out


def projected(parts, w_ref, cols):
    total = None
    for part, rows in parts:
        term = dot(part, w_ref[rows, cols])
        total = term if total is None else total + term
    return total


def add_summary(sum_ref, h, key, value, fade_ref, first):
    fade = fade_ref[first : first + key.shape[0], h : h + 1]
    sum_ref[h] += dot_tn((key.astype(F32) * fade).astype(BF16), value)


def qkv_kernel(heads, dim, first, gain_ref, w_ref, fade_ref, *refs):
    refs, (q_ref, k_ref, v_ref, sum_ref) = refs[:-4], refs[-4:]
    if first == 0:
        sum_ref[...] = jnp.zeros_like(sum_ref)
        x_refs = refs
    else:
        sum_ref[...] = refs[0][...]
        x_refs = refs[1:]
    parts = normed_parts(gain_ref, x_refs)
    wide = heads * dim
    thirds = [projected(parts, w_ref, slice(i * wide, (i + 1) * wide)) for i in range(3)]
    taken = lambda at: thirds[at * dim // wide][:, at * dim % wide : at * dim % wide + dim]
    for h in range(heads):
        cols = slice(h * dim, (h + 1) * dim)
        q_ref[:, cols] = unit(taken(3 * h)).astype(BF16)
        key = unit(taken(3 * h + 1)).astype(BF16)
        value = taken(3 * h + 2).astype(BF16)
        k_ref[:, cols] = key
        v_ref[:, cols] = value
        add_summary(sum_ref, h, key, value, fade_ref, first)


def qkv(gain, w, fade, prev, xs, heads, dim, first):
    rows = xs[0].shape[0]
    before = [prev] if first else []
    return pl.pallas_call(
        functools.partial(qkv_kernel, heads, dim, first),
        in_specs=[VMEM] * (3 + len(before) + len(xs)),
        out_specs=[VMEM] * 4,
        out_shape=[struct((rows, heads * dim))] * 3 + [struct((heads, dim, dim), F32)],
        compiler_params=params(),
        cost_estimate=cost(4 * rows * w.size, 0),
        name="qkv",
    )(gain, w, fade, *before, *xs)


def last_kernel(heads, dim, first, gain_ref, w_ref, fade_ref, prev_ref, tail_ref, *refs):
    x_refs, (k_ref, v_ref, send_ref, sum_ref) = refs[:-4], refs[-4:]
    sum_ref[...] = prev_ref[...]
    parts = normed_parts(gain_ref, x_refs)
    pairs = [
        projected(parts, w_ref, slice((3 * h + 1) * dim, (3 * h + 3) * dim)) for h in range(heads)
    ]
    for h in range(heads):
        cols = slice(h * dim, (h + 1) * dim)
        key = unit(pairs[h][:, :dim]).astype(BF16)
        value = pairs[h][:, dim:].astype(BF16)
        k_ref[:, cols] = key
        v_ref[:, cols] = value
        add_summary(sum_ref, h, key, value, fade_ref, first)
        send_ref[cols, :] = sum_ref[h].astype(BF16)
    send_ref[heads * dim :, :] = tail_ref[...]


def last_keys_values(gain, w, fade, prev, tail, xs, heads, dim, first):
    rows = xs[0].shape[0]
    return pl.pallas_call(
        functools.partial(last_kernel, heads, dim, first),
        in_specs=[VMEM] * (5 + len(xs)),
        out_specs=[VMEM] * 3,
        out_shape=[struct((rows, heads * dim))] * 2 + [struct((heads * dim + TAIL, dim))],
        scratch_shapes=[pltpu.VMEM((heads, dim, dim), F32)],
        compiler_params=params(),
        cost_estimate=cost(3 * rows * w.size, 0),
        name="last_keys_values",
    )(gain, w, fade, prev, tail, *xs)


def queries_kernel(heads, dim, gain_ref, w_ref, *refs):
    q_ref = refs[-1]
    parts = normed_parts(gain_ref, refs[:-1])
    for h in range(heads):
        base = 3 * h * dim
        cols = slice(h * dim, (h + 1) * dim)
        q_ref[:, cols] = unit(projected(parts, w_ref, slice(base, base + dim))).astype(BF16)


def last_queries(gain, w, xs, heads, dim):
    rows = xs[0].shape[0]
    return pl.pallas_call(
        functools.partial(queries_kernel, heads, dim),
        in_specs=[VMEM] * (2 + len(xs)),
        out_specs=VMEM,
        out_shape=struct((rows, heads * dim)),
        compiler_params=params(),
        cost_estimate=cost(2 * rows * w.size, 0),
        name="last_queries",
    )(gain, w, *xs)


def attention_kernel(first, heads, dim, keep_ref, scale_ref, q_ref, *refs):
    count = len(refs) // 2
    k_refs, v_refs, out_ref = refs[:count], refs[count:-1], refs[-1]
    rows = q_ref.shape[0]
    block = first // BLOCK
    causal = lax.broadcasted_iota(jnp.int32, (rows, rows), 1) <= lax.broadcasted_iota(
        jnp.int32, (rows, rows), 0
    )
    for h in range(heads):
        cols = slice(h * dim, (h + 1) * dim)
        query = q_ref[:, cols]
        scale = scale_ref[0, h] * (1.0 / math.sqrt(dim))
        total, at = None, 0
        for j in range(count):
            keys = k_refs[j].shape[0]
            powers = jnp.exp(dot_nt(query, k_refs[j][:, cols]) * scale)
            if at == first:
                powers = jnp.where(causal, powers, 0.0)
            ones = jnp.ones((keys, dim), BF16)
            part = dot(powers.astype(BF16), jnp.concatenate([v_refs[j][:, cols], ones], axis=1))
            if at // BLOCK < block:
                part = jnp.where(keep_ref[block, at // BLOCK] == 1, part, 0.0)
            total = part if total is None else total + part
            at += keys
        out_ref[:, cols] = (total[:, :dim] / total[:, dim:]).astype(BF16)


def attention(first, keep, scale, q, ks, vs, heads, dim):
    rows = q.shape[0]
    return pl.pallas_call(
        functools.partial(attention_kernel, first, heads, dim),
        in_specs=[SMEM, SMEM] + [VMEM] * (1 + len(ks) + len(vs)),
        out_specs=VMEM,
        out_shape=struct(q.shape),
        compiler_params=params(),
        cost_estimate=cost(
            heads * 8 * rows * (first + rows) * dim, 0, heads * rows * (first + rows)
        ),
        name="attention",
    )(keep, scale, q, *ks, *vs)


def body_and_decay(ref, h, dim):
    size = ref.shape[0] - TAIL
    high = ref[size + h : size + h + 1, :].astype(F32)
    low = ref[size + TAIL // 2 + h : size + TAIL // 2 + h + 1, :].astype(F32)
    return ref[h * dim : (h + 1) * dim, :].astype(F32), high + low


def scanned(place, refs, h, dim):
    count = len(refs)
    loaded = [body_and_decay(ref, h, dim) for ref in refs]
    state, since = jnp.zeros((dim, refs[0].shape[1]), F32), jnp.ones((1, refs[0].shape[1]), F32)
    before, before_decay = state, since
    for j in range(count):
        before = jnp.where(place == j, state, before)
        before_decay = jnp.where(place == j, since, before_decay)
        body, decay = loaded[0]
        for k in range(1, count):
            here = place == (j ^ k)
            body = jnp.where(here, loaded[k][0], body)
            decay = jnp.where(here, loaded[k][1], decay)
        state = decay * state + body
        since = since * decay
    return before, before_decay, state, since


def quad_kernel(heads, dim, *refs):
    place = lax.rem(lax.axis_index("tm"), len(refs) - 3)
    refs, (before_ref, decay_ref, total_ref) = refs[:-3], refs[-3:]
    size = heads * dim
    total_ref[size:, :] = jnp.zeros((TAIL, total_ref.shape[1]), BF16)
    for h in range(heads):
        rows = slice(h * dim, (h + 1) * dim)
        before, before_decay, state, since = scanned(place, refs, h, dim)
        before_ref[rows, :] = before
        decay_ref[h : h + 1, :] = before_decay
        total_ref[rows, :] = state.astype(BF16)
        high = since.astype(BF16)
        total_ref[size + h : size + h + 1, :] = high
        low = (since - high.astype(F32)).astype(BF16)
        total_ref[size + TAIL // 2 + h : size + TAIL // 2 + h + 1, :] = low


def quad(loads, heads, dim):
    shape = loads[0].shape
    return pl.pallas_call(
        functools.partial(quad_kernel, heads, dim),
        in_specs=[VMEM] * len(loads),
        out_specs=[VMEM] * 3,
        out_shape=[
            struct((heads * dim, shape[1]), F32),
            struct((TAIL // 2, shape[1]), F32),
            struct(shape),
        ],
        compiler_params=params(),
        cost_estimate=cost(loads[0].size * 40, 0),
        name="quad",
    )(*loads)


def entering_kernel(heads, dim, quad_size, before_ref, decay_ref, *refs):
    refs, out_ref = refs[:-1], refs[-1]
    place = lax.div(lax.axis_index("tm"), quad_size)
    for h in range(heads):
        rows = slice(h * dim, (h + 1) * dim)
        earlier = scanned(place, refs, h, dim)[0]
        out_ref[rows, :] = (before_ref[rows, :] + decay_ref[h : h + 1, :] * earlier).astype(BF16)


def entering(quad_size, before, decay, totals, heads, dim):
    return pl.pallas_call(
        functools.partial(entering_kernel, heads, dim, quad_size),
        in_specs=[VMEM] * (2 + len(totals)),
        out_specs=VMEM,
        out_shape=struct(before.shape),
        compiler_params=params(),
        cost_estimate=cost(before.size * 20, 0),
        name="entering",
    )(before, decay, *totals)


def recall_kernel(heads, dim, reading_ref, q_ref, local_ref, state_ref, out_ref):
    for h in range(heads):
        cols = slice(h * dim, (h + 1) * dim)
        recalled = dot(q_ref[:, cols], state_ref[cols, :]) * reading_ref[:, h : h + 1]
        out_ref[:, cols] = (local_ref[:, cols].astype(F32) + recalled).astype(BF16)


def recall(reading, q, local, state, heads, dim):
    return pl.pallas_call(
        functools.partial(recall_kernel, heads, dim),
        in_specs=[VMEM] * 4,
        out_specs=VMEM,
        out_shape=struct(q.shape),
        compiler_params=params(),
        cost_estimate=cost(4 * q.size * dim, 0),
        name="recall",
    )(reading, q, local, state)


def project_kernel(shards, own_ref, side_ref, own_w_ref, side_w_ref, *out_refs):
    width = out_refs[0].shape[1]
    own, side = own_ref[...], side_ref[...]
    for k in reversed(range(shards)):
        owner = lax.rem(lax.axis_index("head") + k, shards)
        cols = pl.ds(pl.multiple_of(owner * width, width), width)
        out = dot(own, own_w_ref[:, cols]) + dot(side, side_w_ref[:, cols])
        out_refs[k][...] = out.astype(out_refs[k].dtype)


def project(own, side, own_w, side_w, shards):
    rows = own.shape[0]
    width = own_w.shape[1] // shards
    return pl.pallas_call(
        functools.partial(project_kernel, shards),
        in_specs=[VMEM] * 4,
        out_specs=[VMEM] * shards,
        out_shape=[struct((rows, width))] * shards,
        compiler_params=params(),
        cost_estimate=cost(4 * rows * own_w.size, 0),
        name="project",
    )(own, side, own_w, side_w)


def finish_kernel(count, *refs):
    total = refs[0][...].astype(F32)
    for ref in refs[1:count]:
        total += ref[...].astype(F32)
    refs[-1][...] = total.astype(BF16)


def finish(parts, result, first, length):
    rows, width = parts[0].shape
    chunk = first // rows
    whole = pl.BlockSpec((rows, width), lambda i: (0, 0))
    more = [] if result is None else [result]
    return pl.pallas_call(
        functools.partial(finish_kernel, len(parts)),
        grid=(1,),
        in_specs=[whole] * len(parts) + [pl.BlockSpec(memory_space=pl.ANY)] * len(more),
        out_specs=pl.BlockSpec((rows, width), lambda i: (chunk, 0)),
        out_shape=struct((length, width)),
        input_output_aliases={len(parts): 0} if more else {},
        compiler_params=params(),
        cost_estimate=cost(rows * width * 2, rows * width * 6),
        name="finish",
    )(*parts, *more)


def per_device(
    residual_signal,
    prescale_amplifier,
    triple_projector,
    score_scaler,
    recall_retained_logshare,
    tile_retain_grid,
    recall_store_flags,
    emission_projector,
    sideways_coupling_coef,
):
    x = residual_signal[0]
    length = x.shape[0]
    sizes = [CHUNK] * (length // CHUNK - 1) + [LAST] * (CHUNK // LAST)
    firsts = [sum(sizes[:c]) for c in range(len(sizes))]
    chunks = len(sizes)
    shards = lax.axis_size("head")
    blocks = lax.axis_size("tm")
    heads = triple_projector.shape[2]
    dim = emission_projector.shape[2]
    swap_streams = [(0, 1), (1, 0)]
    tied = lambda *arrays: lax.optimization_barrier(arrays)

    own_w = emission_projector[0].reshape(heads * dim, -1)
    side_w = lax.ppermute(
        sideways_coupling_coef[0].reshape(heads * dim, -1), "stream", swap_streams
    )
    fade, tail, *readings = prepare(
        recall_retained_logshare[0],
        recall_store_flags,
        dim,
        1.0 / math.sqrt(dim * length * blocks),
        sizes,
    )
    pieces = [x[first : first + size] for first, size in zip(firsts, sizes)]
    received = []
    for c in range(chunks):
        if c == chunks - 2:
            pieces[c], pieces[c + 1], received[0] = tied(pieces[c], pieces[c + 1], received[0])
        xs = [pieces[c]]
        for k in range(1, shards):
            xs.append(
                lax.ppermute(pieces[c], "head", [((d + k) % shards, d) for d in range(shards)])
            )
        received.append(xs)
    gain = prescale_amplifier
    w = triple_projector[0].reshape(-1, 3 * heads * dim)

    qs, ks, vs, locals_ = [], [], [], []
    summary = None
    for c, first in enumerate(firsts[:-1]):
        q, k, v, summary = qkv(gain, w, fade, summary, received[c], heads, dim, first)
        qs.append(q)
        ks.append(k)
        vs.append(v)
        local = attention(first, tile_retain_grid, score_scaler, q, ks, vs, heads, dim)
        summary, local = tied(summary, local)
        locals_.append(local)
    k, v, sent = last_keys_values(
        gain, w, fade, summary, tail, received[-1], heads, dim, firsts[-1]
    )
    ks.append(k)
    vs.append(v)

    quad_size = min(4, blocks)
    loads = [sent] + [
        lax.ppermute(sent, "tm", [(d, d ^ k) for d in range(blocks)]) for k in range(1, quad_size)
    ]
    qs.append(last_queries(gain, w, received[-1], heads, dim))
    locals_.append(attention(firsts[-1], tile_retain_grid, score_scaler, qs[-1], ks, vs, heads, dim))
    *loads, locals_[-1] = tied(*loads, locals_[-1])
    before, decay, total = quad(loads, heads, dim)
    totals = [total] + [
        lax.ppermute(total, "tm", [(d, d ^ (quad_size * k)) for d in range(blocks)])
        for k in range(1, blocks // quad_size)
    ]
    state = entering(quad_size, before, decay, totals, heads, dim)

    result = None
    for c in range(chunks):
        head_out = recall(readings[c], qs[c], locals_[c], state, heads, dim)
        side = lax.ppermute(head_out, "stream", swap_streams)
        outs = project(head_out, side, own_w, side_w, shards)
        parts = [outs[0]]
        for k in range(1, shards):
            parts.append(
                lax.ppermute(outs[k], "head", [(d, (d + k) % shards) for d in range(shards)])
            )
        result = finish(parts, result, firsts[c], length)
    return result[None]


def solution(mesh):
    placed = (
        P("stream", "tm", "head"),
        P("stream", None),
        P("stream", None, "head", None),
        P("stream", "head"),
        P("stream", "head", "tm"),
        P("tm", None),
        P("tm"),
        P("stream", "head", None, None),
        P("stream", "head", None, None),
    )
    return jax.shard_map(
        per_device, mesh=mesh, in_specs=placed, out_specs=P("stream", "tm", "head"), check_vma=False
    )
```

```python
import functools
import math

import jax
import jax.numpy as jnp
from jax import lax
from jax.experimental import pallas as pl
from jax.experimental.pallas import tpu as pltpu
from jax.sharding import PartitionSpec as P

BLOCK = 512
CHUNK = 256
LAST = 128
TAIL = 16
EPSILON = 1e-06
F32 = jnp.float32
BF16 = jnp.bfloat16
SMEM = pl.BlockSpec(memory_space=pltpu.SMEM)
VMEM = pl.BlockSpec(memory_space=pltpu.VMEM)


def params():
    return pltpu.CompilerParams(vmem_limit_bytes=16 * 1024 * 1024)


def cost(flops, bytes_accessed, transcendentals=0):
    return pl.CostEstimate(
        flops=int(flops), bytes_accessed=int(bytes_accessed), transcendentals=int(transcendentals)
    )


def struct(shape, dtype=BF16):
    return jax.ShapeDtypeStruct(shape, dtype)


def dot(a, b):
    return lax.dot_general(a, b, (((1,), (0,)), ((), ())), preferred_element_type=F32)


def dot_nt(a, b):
    return lax.dot_general(a, b, (((1,), (1,)), ((), ())), preferred_element_type=F32)


def dot_tn(a, b):
    return lax.dot_general(a, b, (((0,), (0,)), ((), ())), preferred_element_type=F32)


def unit(values):
    return values * lax.rsqrt(jnp.mean(values * values, axis=-1, keepdims=True) + EPSILON)


def prepare_kernel(heads, factor, logs_ref, flags_ref, fade_ref, tail_ref, *refs):
    reading_refs, rows_ref = refs[:-1], refs[-1]
    length = logs_ref.shape[1]
    rows_ref[...] = jnp.zeros_like(rows_ref)
    rows_ref[:heads, :] = logs_ref[...]
    running = rows_ref[...]
    place = lax.broadcasted_iota(jnp.int32, running.shape, 1)
    step = 1
    while step < length:
        running += jnp.where(place >= step, pltpu.roll(running, step, 1), 0.0)
        step *= 2
    last = running[:, length - 1 :]
    chosen = jnp.zeros_like(running)
    for block in range(length // BLOCK):
        inside = (place >= block * BLOCK) & (place < (block + 1) * BLOCK)
        chosen = jnp.where(inside, flags_ref[block].astype(F32), chosen)
    fade_ref[...] = jnp.transpose(jnp.exp(last - running) * chosen)
    reading = jnp.transpose(jnp.exp(running) * factor)
    first = 0
    for ref in reading_refs:
        ref[...] = reading[first : first + ref.shape[0]]
        first += ref.shape[0]
    decay = jnp.exp(last)
    high = decay.astype(BF16).astype(F32)
    both = jnp.concatenate([high, decay - high], axis=0)
    tail_ref[...] = jnp.broadcast_to(both, tail_ref.shape).astype(BF16)


def prepare(logs, flags, dim, factor, sizes):
    heads, length = logs.shape
    lines = TAIL // 2
    return pl.pallas_call(
        functools.partial(prepare_kernel, heads, factor),
        in_specs=[VMEM, SMEM],
        out_specs=[VMEM] * (2 + len(sizes)),
        out_shape=[struct((length, lines), F32), struct((TAIL, dim))]
        + [struct((size, lines), F32) for size in sizes],
        scratch_shapes=[pltpu.VMEM((lines, length), F32)],
        compiler_params=params(),
        cost_estimate=cost(40 * lines * length, 0),
        name="prepare",
    )(logs, flags)


def normed_parts(gain_ref, x_refs):
    me = lax.axis_index("head")
    shards, width = len(x_refs), x_refs[0].shape[1]
    parts = [x[...].astype(F32) for x in x_refs]
    squares = sum(jnp.sum(p * p, axis=-1, keepdims=True) for p in parts)
    scale = lax.rsqrt(squares * (1.0 / (width * shards)) + EPSILON)
    out = []
    for k, part in enumerate(parts):
        owner = lax.rem(me + k, shards)
        rows = pl.ds(pl.multiple_of(owner * width, width), width)
        out.append(((part * scale * gain_ref[:, rows]).astype(BF16), rows))
    return out


def projected(parts, w_ref, cols):
    total = None
    for part, rows in parts:
        term = dot(part, w_ref[rows, cols])
        total = term if total is None else total + term
    return total


def add_summary(sum_ref, h, key, value, fade_ref, first):
    fade = fade_ref[first : first + key.shape[0], h : h + 1]
    sum_ref[h] += dot_tn((key.astype(F32) * fade).astype(BF16), value)


def qkv_kernel(heads, dim, first, gain_ref, w_ref, fade_ref, *refs):
    refs, (q_ref, k_ref, v_ref, sum_ref) = refs[:-4], refs[-4:]
    if first == 0:
        sum_ref[...] = jnp.zeros_like(sum_ref)
        x_refs = refs
    else:
        sum_ref[...] = refs[0][...]
        x_refs = refs[1:]
    parts = normed_parts(gain_ref, x_refs)
    wide = heads * dim
    thirds = [projected(parts, w_ref, slice(i * wide, (i + 1) * wide)) for i in range(3)]
    taken = lambda at: thirds[at * dim // wide][:, at * dim % wide : at * dim % wide + dim]
    for h in range(heads):
        cols = slice(h * dim, (h + 1) * dim)
        q_ref[:, cols] = unit(taken(3 * h)).astype(BF16)
        key = unit(taken(3 * h + 1)).astype(BF16)
        value = taken(3 * h + 2).astype(BF16)
        k_ref[:, cols] = key
        v_ref[:, cols] = value
        add_summary(sum_ref, h, key, value, fade_ref, first)


def qkv(gain, w, fade, prev, xs, heads, dim, first):
    rows = xs[0].shape[0]
    before = [prev] if first else []
    return pl.pallas_call(
        functools.partial(qkv_kernel, heads, dim, first),
        in_specs=[VMEM] * (3 + len(before) + len(xs)),
        out_specs=[VMEM] * 4,
        out_shape=[struct((rows, heads * dim))] * 3 + [struct((heads, dim, dim), F32)],
        compiler_params=params(),
        cost_estimate=cost(4 * rows * w.size, 0),
        name="qkv",
    )(gain, w, fade, *before, *xs)


def last_kernel(heads, dim, first, gain_ref, w_ref, fade_ref, prev_ref, tail_ref, *refs):
    x_refs, (k_ref, v_ref, send_ref, sum_ref) = refs[:-4], refs[-4:]
    sum_ref[...] = prev_ref[...]
    parts = normed_parts(gain_ref, x_refs)
    pairs = [
        projected(parts, w_ref, slice((3 * h + 1) * dim, (3 * h + 3) * dim)) for h in range(heads)
    ]
    for h in range(heads):
        cols = slice(h * dim, (h + 1) * dim)
        key = unit(pairs[h][:, :dim]).astype(BF16)
        value = pairs[h][:, dim:].astype(BF16)
        k_ref[:, cols] = key
        v_ref[:, cols] = value
        add_summary(sum_ref, h, key, value, fade_ref, first)
        send_ref[cols, :] = sum_ref[h].astype(BF16)
    send_ref[heads * dim :, :] = tail_ref[...]


def last_keys_values(gain, w, fade, prev, tail, xs, heads, dim, first):
    rows = xs[0].shape[0]
    return pl.pallas_call(
        functools.partial(last_kernel, heads, dim, first),
        in_specs=[VMEM] * (5 + len(xs)),
        out_specs=[VMEM] * 3,
        out_shape=[struct((rows, heads * dim))] * 2 + [struct((heads * dim + TAIL, dim))],
        scratch_shapes=[pltpu.VMEM((heads, dim, dim), F32)],
        compiler_params=params(),
        cost_estimate=cost(3 * rows * w.size, 0),
        name="last_keys_values",
    )(gain, w, fade, prev, tail, *xs)


def queries_kernel(heads, dim, gain_ref, w_ref, *refs):
    q_ref = refs[-1]
    parts = normed_parts(gain_ref, refs[:-1])
    for h in range(heads):
        base = 3 * h * dim
        cols = slice(h * dim, (h + 1) * dim)
        q_ref[:, cols] = unit(projected(parts, w_ref, slice(base, base + dim))).astype(BF16)


def last_queries(gain, w, xs, heads, dim):
    rows = xs[0].shape[0]
    return pl.pallas_call(
        functools.partial(queries_kernel, heads, dim),
        in_specs=[VMEM] * (2 + len(xs)),
        out_specs=VMEM,
        out_shape=struct((rows, heads * dim)),
        compiler_params=params(),
        cost_estimate=cost(2 * rows * w.size, 0),
        name="last_queries",
    )(gain, w, *xs)


def attention_kernel(first, heads, dim, keep_ref, scale_ref, q_ref, *refs):
    count = len(refs) // 2
    k_refs, v_refs, out_ref = refs[:count], refs[count:-1], refs[-1]
    rows = q_ref.shape[0]
    block = first // BLOCK
    causal = lax.broadcasted_iota(jnp.int32, (rows, rows), 1) <= lax.broadcasted_iota(
        jnp.int32, (rows, rows), 0
    )
    for h in range(heads):
        cols = slice(h * dim, (h + 1) * dim)
        query = q_ref[:, cols]
        scale = scale_ref[0, h] * (1.0 / math.sqrt(dim))
        total, at = None, 0
        for j in range(count):
            keys = k_refs[j].shape[0]
            powers = jnp.exp(dot_nt(query, k_refs[j][:, cols]) * scale)
            if at == first:
                powers = jnp.where(causal, powers, 0.0)
            ones = jnp.ones((keys, dim), BF16)
            part = dot(powers.astype(BF16), jnp.concatenate([v_refs[j][:, cols], ones], axis=1))
            if at // BLOCK < block:
                part = jnp.where(keep_ref[block, at // BLOCK] == 1, part, 0.0)
            total = part if total is None else total + part
            at += keys
        out_ref[:, cols] = (total[:, :dim] / total[:, dim:]).astype(BF16)


def attention(first, keep, scale, q, ks, vs, heads, dim):
    rows = q.shape[0]
    return pl.pallas_call(
        functools.partial(attention_kernel, first, heads, dim),
        in_specs=[SMEM, SMEM] + [VMEM] * (1 + len(ks) + len(vs)),
        out_specs=VMEM,
        out_shape=struct(q.shape),
        compiler_params=params(),
        cost_estimate=cost(
            heads * 8 * rows * (first + rows) * dim, 0, heads * rows * (first + rows)
        ),
        name="attention",
    )(keep, scale, q, *ks, *vs)


def body_and_decay(ref, h, dim):
    size = ref.shape[0] - TAIL
    high = ref[size + h : size + h + 1, :].astype(F32)
    low = ref[size + TAIL // 2 + h : size + TAIL // 2 + h + 1, :].astype(F32)
    return ref[h * dim : (h + 1) * dim, :].astype(F32), high + low


def scanned(place, refs, h, dim):
    count = len(refs)
    loaded = [body_and_decay(ref, h, dim) for ref in refs]
    state, since = jnp.zeros((dim, refs[0].shape[1]), F32), jnp.ones((1, refs[0].shape[1]), F32)
    before, before_decay = state, since
    for j in range(count):
        before = jnp.where(place == j, state, before)
        before_decay = jnp.where(place == j, since, before_decay)
        body, decay = loaded[0]
        for k in range(1, count):
            here = place == (j ^ k)
            body = jnp.where(here, loaded[k][0], body)
            decay = jnp.where(here, loaded[k][1], decay)
        state = decay * state + body
        since = since * decay
    return before, before_decay, state, since


def quad_kernel(heads, dim, *refs):
    place = lax.rem(lax.axis_index("tm"), len(refs) - 3)
    refs, (before_ref, decay_ref, total_ref) = refs[:-3], refs[-3:]
    size = heads * dim
    total_ref[size:, :] = jnp.zeros((TAIL, total_ref.shape[1]), BF16)
    for h in range(heads):
        rows = slice(h * dim, (h + 1) * dim)
        before, before_decay, state, since = scanned(place, refs, h, dim)
        before_ref[rows, :] = before
        decay_ref[h : h + 1, :] = before_decay
        total_ref[rows, :] = state.astype(BF16)
        high = since.astype(BF16)
        total_ref[size + h : size + h + 1, :] = high
        low = (since - high.astype(F32)).astype(BF16)
        total_ref[size + TAIL // 2 + h : size + TAIL // 2 + h + 1, :] = low


def quad(loads, heads, dim):
    shape = loads[0].shape
    return pl.pallas_call(
        functools.partial(quad_kernel, heads, dim),
        in_specs=[VMEM] * len(loads),
        out_specs=[VMEM] * 3,
        out_shape=[
            struct((heads * dim, shape[1]), F32),
            struct((TAIL // 2, shape[1]), F32),
            struct(shape),
        ],
        compiler_params=params(),
        cost_estimate=cost(loads[0].size * 40, 0),
        name="quad",
    )(*loads)


def entering_kernel(heads, dim, quad_size, before_ref, decay_ref, *refs):
    refs, out_ref = refs[:-1], refs[-1]
    place = lax.div(lax.axis_index("tm"), quad_size)
    for h in range(heads):
        rows = slice(h * dim, (h + 1) * dim)
        earlier = scanned(place, refs, h, dim)[0]
        out_ref[rows, :] = (before_ref[rows, :] + decay_ref[h : h + 1, :] * earlier).astype(BF16)


def entering(quad_size, before, decay, totals, heads, dim):
    return pl.pallas_call(
        functools.partial(entering_kernel, heads, dim, quad_size),
        in_specs=[VMEM] * (2 + len(totals)),
        out_specs=VMEM,
        out_shape=struct(before.shape),
        compiler_params=params(),
        cost_estimate=cost(before.size * 20, 0),
        name="entering",
    )(before, decay, *totals)


def recall_kernel(heads, dim, reading_ref, q_ref, local_ref, state_ref, out_ref):
    for h in range(heads):
        cols = slice(h * dim, (h + 1) * dim)
        recalled = dot(q_ref[:, cols], state_ref[cols, :]) * reading_ref[:, h : h + 1]
        out_ref[:, cols] = (local_ref[:, cols].astype(F32) + recalled).astype(BF16)


def recall(reading, q, local, state, heads, dim):
    return pl.pallas_call(
        functools.partial(recall_kernel, heads, dim),
        in_specs=[VMEM] * 4,
        out_specs=VMEM,
        out_shape=struct(q.shape),
        compiler_params=params(),
        cost_estimate=cost(4 * q.size * dim, 0),
        name="recall",
    )(reading, q, local, state)


def project_kernel(shards, own_ref, side_ref, own_w_ref, side_w_ref, *out_refs):
    width = out_refs[0].shape[1]
    own, side = own_ref[...], side_ref[...]
    for k in reversed(range(shards)):
        owner = lax.rem(lax.axis_index("head") + k, shards)
        cols = pl.ds(pl.multiple_of(owner * width, width), width)
        out = dot(own, own_w_ref[:, cols]) + dot(side, side_w_ref[:, cols])
        out_refs[k][...] = out.astype(out_refs[k].dtype)


def project(own, side, own_w, side_w, shards):
    rows = own.shape[0]
    width = own_w.shape[1] // shards
    return pl.pallas_call(
        functools.partial(project_kernel, shards),
        in_specs=[VMEM] * 4,
        out_specs=[VMEM] * shards,
        out_shape=[struct((rows, width))] * shards,
        compiler_params=params(),
        cost_estimate=cost(4 * rows * own_w.size, 0),
        name="project",
    )(own, side, own_w, side_w)


def finish_kernel(count, *refs):
    total = refs[0][...].astype(F32)
    for ref in refs[1:count]:
        total += ref[...].astype(F32)
    refs[-1][...] = total.astype(BF16)


def finish(parts, result, first, length):
    rows, width = parts[0].shape
    chunk = first // rows
    whole = pl.BlockSpec((rows, width), lambda i: (0, 0))
    more = [] if result is None else [result]
    return pl.pallas_call(
        functools.partial(finish_kernel, len(parts)),
        grid=(1,),
        in_specs=[whole] * len(parts) + [pl.BlockSpec(memory_space=pl.ANY)] * len(more),
        out_specs=pl.BlockSpec((rows, width), lambda i: (chunk, 0)),
        out_shape=struct((length, width)),
        input_output_aliases={len(parts): 0} if more else {},
        compiler_params=params(),
        cost_estimate=cost(rows * width * 2, rows * width * 6),
        name="finish",
    )(*parts, *more)


def per_device(
    residual_signal,
    prescale_amplifier,
    triple_projector,
    score_scaler,
    recall_retained_logshare,
    tile_retain_grid,
    recall_store_flags,
    emission_projector,
    sideways_coupling_coef,
):
    x = residual_signal[0]
    length = x.shape[0]
    sizes = [CHUNK] * (length // CHUNK - 1) + [LAST] * (CHUNK // LAST)
    firsts = [sum(sizes[:c]) for c in range(len(sizes))]
    chunks = len(sizes)
    shards = lax.axis_size("head")
    blocks = lax.axis_size("tm")
    heads = triple_projector.shape[2]
    dim = emission_projector.shape[2]
    swap_streams = [(0, 1), (1, 0)]
    tied = lambda *arrays: lax.optimization_barrier(arrays)

    own_w = emission_projector[0].reshape(heads * dim, -1)
    side_w = lax.ppermute(
        sideways_coupling_coef[0].reshape(heads * dim, -1), "stream", swap_streams
    )
    fade, tail, *readings = prepare(
        recall_retained_logshare[0],
        recall_store_flags,
        dim,
        1.0 / math.sqrt(dim * length * blocks),
        sizes,
    )
    pieces = [x[first : first + size] for first, size in zip(firsts, sizes)]
    received = []
    for c in range(chunks):
        if c == chunks - 2:
            pieces[c], pieces[c + 1], tail = tied(pieces[c], pieces[c + 1], tail)
        xs = [pieces[c]]
        for k in range(1, shards):
            xs.append(
                lax.ppermute(pieces[c], "head", [((d + k) % shards, d) for d in range(shards)])
            )
        received.append(xs)
    gain = prescale_amplifier
    w = triple_projector[0].reshape(-1, 3 * heads * dim)

    qs, ks, vs, locals_ = [], [], [], []
    summary = None
    for c, first in enumerate(firsts[:-1]):
        q, k, v, summary = qkv(gain, w, fade, summary, received[c], heads, dim, first)
        qs.append(q)
        ks.append(k)
        vs.append(v)
        if c < chunks - 2:
            local = attention(first, tile_retain_grid, score_scaler, q, ks, vs, heads, dim)
            summary, local = tied(summary, local)
            locals_.append(local)
    k, v, sent = last_keys_values(
        gain, w, fade, summary, tail, received[-1], heads, dim, firsts[-1]
    )
    ks.append(k)
    vs.append(v)

    quad_size = min(4, blocks)
    loads = [sent] + [
        lax.ppermute(sent, "tm", [(d, d ^ k) for d in range(blocks)]) for k in range(1, quad_size)
    ]
    qs.append(last_queries(gain, w, received[-1], heads, dim))
    for c in range(chunks - 2, chunks):
        locals_.append(
            attention(
                firsts[c], tile_retain_grid, score_scaler, qs[c], ks[: c + 1], vs[: c + 1], heads, dim
            )
        )
    *loads, locals_[-2] = tied(*loads, locals_[-2])
    before, decay, total = quad(loads, heads, dim)
    totals = [total] + [
        lax.ppermute(total, "tm", [(d, d ^ (quad_size * k)) for d in range(blocks)])
        for k in range(1, blocks // quad_size)
    ]
    *totals, locals_[-1] = tied(*totals, locals_[-1])
    state = entering(quad_size, before, decay, totals, heads, dim)

    result = None
    for c in range(chunks):
        head_out = recall(readings[c], qs[c], locals_[c], state, heads, dim)
        side = lax.ppermute(head_out, "stream", swap_streams)
        outs = project(head_out, side, own_w, side_w, shards)
        parts = [outs[0]]
        for k in range(1, shards):
            parts.append(
                lax.ppermute(outs[k], "head", [(d, (d + k) % shards) for d in range(shards)])
            )
        result = finish(parts, result, firsts[c], length)
    return result[None]


def solution(mesh):
    placed = (
        P("stream", "tm", "head"),
        P("stream", None),
        P("stream", None, "head", None),
        P("stream", "head"),
        P("stream", "head", "tm"),
        P("tm", None),
        P("tm"),
        P("stream", "head", None, None),
        P("stream", "head", None, None),
    )
    return jax.shard_map(
        per_device, mesh=mesh, in_specs=placed, out_specs=P("stream", "tm", "head"), check_vma=False
    )
```

```python
import functools
import math

import jax
import jax.numpy as jnp
from jax import lax
from jax.experimental import pallas as pl
from jax.experimental.pallas import tpu as pltpu
from jax.sharding import PartitionSpec as P

BLOCK = 512
CHUNK = 256
LAST = 128
TAIL = 16
EPSILON = 1e-06
F32 = jnp.float32
BF16 = jnp.bfloat16
SMEM = pl.BlockSpec(memory_space=pltpu.SMEM)
VMEM = pl.BlockSpec(memory_space=pltpu.VMEM)


def params():
    return pltpu.CompilerParams(vmem_limit_bytes=16 * 1024 * 1024)


def cost(flops, bytes_accessed, transcendentals=0):
    return pl.CostEstimate(
        flops=int(flops), bytes_accessed=int(bytes_accessed), transcendentals=int(transcendentals)
    )


def struct(shape, dtype=BF16):
    return jax.ShapeDtypeStruct(shape, dtype)


def dot(a, b):
    return lax.dot_general(a, b, (((1,), (0,)), ((), ())), preferred_element_type=F32)


def dot_nt(a, b):
    return lax.dot_general(a, b, (((1,), (1,)), ((), ())), preferred_element_type=F32)


def dot_tn(a, b):
    return lax.dot_general(a, b, (((0,), (0,)), ((), ())), preferred_element_type=F32)


def unit(values):
    return values * lax.rsqrt(jnp.mean(values * values, axis=-1, keepdims=True) + EPSILON)


def prepare_kernel(heads, factor, logs_ref, flags_ref, fade_ref, tail_ref, *refs):
    reading_refs, rows_ref = refs[:-1], refs[-1]
    length = logs_ref.shape[1]
    rows_ref[...] = jnp.zeros_like(rows_ref)
    rows_ref[:heads, :] = logs_ref[...]
    running = rows_ref[...]
    place = lax.broadcasted_iota(jnp.int32, running.shape, 1)
    step = 1
    while step < length:
        running += jnp.where(place >= step, pltpu.roll(running, step, 1), 0.0)
        step *= 2
    last = running[:, length - 1 :]
    chosen = jnp.zeros_like(running)
    for block in range(length // BLOCK):
        inside = (place >= block * BLOCK) & (place < (block + 1) * BLOCK)
        chosen = jnp.where(inside, flags_ref[block].astype(F32), chosen)
    fade_ref[...] = jnp.transpose(jnp.exp(last - running) * chosen)
    reading = jnp.transpose(jnp.exp(running) * factor)
    first = 0
    for ref in reading_refs:
        ref[...] = reading[first : first + ref.shape[0]]
        first += ref.shape[0]
    decay = jnp.exp(last)
    high = decay.astype(BF16).astype(F32)
    both = jnp.concatenate([high, decay - high], axis=0)
    tail_ref[...] = jnp.broadcast_to(both, tail_ref.shape).astype(BF16)


def prepare(logs, flags, dim, factor, sizes):
    heads, length = logs.shape
    lines = TAIL // 2
    return pl.pallas_call(
        functools.partial(prepare_kernel, heads, factor),
        in_specs=[VMEM, SMEM],
        out_specs=[VMEM] * (2 + len(sizes)),
        out_shape=[struct((length, lines), F32), struct((TAIL, dim))]
        + [struct((size, lines), F32) for size in sizes],
        scratch_shapes=[pltpu.VMEM((lines, length), F32)],
        compiler_params=params(),
        cost_estimate=cost(40 * lines * length, 0),
        name="prepare",
    )(logs, flags)


def normed_parts(gain_ref, x_refs):
    me = lax.axis_index("head")
    shards, width = len(x_refs), x_refs[0].shape[1]
    parts = [x[...].astype(F32) for x in x_refs]
    squares = sum(jnp.sum(p * p, axis=-1, keepdims=True) for p in parts)
    scale = lax.rsqrt(squares * (1.0 / (width * shards)) + EPSILON)
    out = []
    for k, part in enumerate(parts):
        owner = lax.rem(me + k, shards)
        rows = pl.ds(pl.multiple_of(owner * width, width), width)
        out.append(((part * scale * gain_ref[:, rows]).astype(BF16), rows))
    return out


def projected(parts, w_ref, cols):
    total = None
    for part, rows in parts:
        term = dot(part, w_ref[rows, cols])
        total = term if total is None else total + term
    return total


def add_summary(sum_ref, h, key, value, fade_ref, first):
    fade = fade_ref[first : first + key.shape[0], h : h + 1]
    sum_ref[h] += dot_tn((key.astype(F32) * fade).astype(BF16), value)


def qkv_kernel(heads, dim, first, gain_ref, w_ref, fade_ref, *refs):
    refs, (q_ref, k_ref, v_ref, sum_ref) = refs[:-4], refs[-4:]
    if first == 0:
        sum_ref[...] = jnp.zeros_like(sum_ref)
        x_refs = refs
    else:
        sum_ref[...] = refs[0][...]
        x_refs = refs[1:]
    parts = normed_parts(gain_ref, x_refs)
    wide = heads * dim
    thirds = [projected(parts, w_ref, slice(i * wide, (i + 1) * wide)) for i in range(3)]
    taken = lambda at: thirds[at * dim // wide][:, at * dim % wide : at * dim % wide + dim]
    for h in range(heads):
        cols = slice(h * dim, (h + 1) * dim)
        q_ref[:, cols] = unit(taken(3 * h)).astype(BF16)
        key = unit(taken(3 * h + 1)).astype(BF16)
        value = taken(3 * h + 2).astype(BF16)
        k_ref[:, cols] = key
        v_ref[:, cols] = value
        add_summary(sum_ref, h, key, value, fade_ref, first)


def qkv(gain, w, fade, prev, xs, heads, dim, first):
    rows = xs[0].shape[0]
    before = [prev] if first else []
    return pl.pallas_call(
        functools.partial(qkv_kernel, heads, dim, first),
        in_specs=[VMEM] * (3 + len(before) + len(xs)),
        out_specs=[VMEM] * 4,
        out_shape=[struct((rows, heads * dim))] * 3 + [struct((heads, dim, dim), F32)],
        compiler_params=params(),
        cost_estimate=cost(4 * rows * w.size, 0),
        name="qkv",
    )(gain, w, fade, *before, *xs)


def last_kernel(heads, dim, first, gain_ref, w_ref, fade_ref, prev_ref, tail_ref, *refs):
    x_refs, (k_ref, v_ref, send_ref, sum_ref) = refs[:-4], refs[-4:]
    sum_ref[...] = prev_ref[...]
    parts = normed_parts(gain_ref, x_refs)
    pairs = [
        projected(parts, w_ref, slice((3 * h + 1) * dim, (3 * h + 3) * dim)) for h in range(heads)
    ]
    for h in range(heads):
        cols = slice(h * dim, (h + 1) * dim)
        key = unit(pairs[h][:, :dim]).astype(BF16)
        value = pairs[h][:, dim:].astype(BF16)
        k_ref[:, cols] = key
        v_ref[:, cols] = value
        add_summary(sum_ref, h, key, value, fade_ref, first)
        send_ref[cols, :] = sum_ref[h].astype(BF16)
    send_ref[heads * dim :, :] = tail_ref[...]


def last_keys_values(gain, w, fade, prev, tail, xs, heads, dim, first):
    rows = xs[0].shape[0]
    return pl.pallas_call(
        functools.partial(last_kernel, heads, dim, first),
        in_specs=[VMEM] * (5 + len(xs)),
        out_specs=[VMEM] * 3,
        out_shape=[struct((rows, heads * dim))] * 2 + [struct((heads * dim + TAIL, dim))],
        scratch_shapes=[pltpu.VMEM((heads, dim, dim), F32)],
        compiler_params=params(),
        cost_estimate=cost(3 * rows * w.size, 0),
        name="last_keys_values",
    )(gain, w, fade, prev, tail, *xs)


def queries_kernel(heads, dim, gain_ref, w_ref, *refs):
    q_ref = refs[-1]
    parts = normed_parts(gain_ref, refs[:-1])
    for h in range(heads):
        base = 3 * h * dim
        cols = slice(h * dim, (h + 1) * dim)
        q_ref[:, cols] = unit(projected(parts, w_ref, slice(base, base + dim))).astype(BF16)


def last_queries(gain, w, xs, heads, dim):
    rows = xs[0].shape[0]
    return pl.pallas_call(
        functools.partial(queries_kernel, heads, dim),
        in_specs=[VMEM] * (2 + len(xs)),
        out_specs=VMEM,
        out_shape=struct((rows, heads * dim)),
        compiler_params=params(),
        cost_estimate=cost(2 * rows * w.size, 0),
        name="last_queries",
    )(gain, w, *xs)


def attention_kernel(first, heads, dim, keep_ref, scale_ref, reading_ref, q_ref, *refs):
    count = len(refs) // 2
    k_refs, v_refs, out_ref = refs[:count], refs[count:-1], refs[-1]
    rows = q_ref.shape[0]
    block = first // BLOCK
    causal = lax.broadcasted_iota(jnp.int32, (rows, rows), 1) <= lax.broadcasted_iota(
        jnp.int32, (rows, rows), 0
    )
    for h in range(heads):
        cols = slice(h * dim, (h + 1) * dim)
        query = q_ref[:, cols]
        scale = scale_ref[0, h] * (1.0 / math.sqrt(dim))
        total, at = None, 0
        for j in range(count):
            keys = k_refs[j].shape[0]
            powers = jnp.exp(dot_nt(query, k_refs[j][:, cols]) * scale)
            if at == first:
                powers = jnp.where(causal, powers, 0.0)
            ones = jnp.ones((keys, dim), BF16)
            part = dot(powers.astype(BF16), jnp.concatenate([v_refs[j][:, cols], ones], axis=1))
            if at // BLOCK < block:
                part = jnp.where(keep_ref[block, at // BLOCK] == 1, part, 0.0)
            total = part if total is None else total + part
            at += keys
        out_ref[:rows, cols] = (query.astype(F32) * reading_ref[:, h : h + 1]).astype(BF16)
        out_ref[rows:, cols] = (total[:, :dim] / total[:, dim:]).astype(BF16)


def attention(first, keep, scale, reading, q, ks, vs, heads, dim):
    rows = q.shape[0]
    return pl.pallas_call(
        functools.partial(attention_kernel, first, heads, dim),
        in_specs=[SMEM, SMEM] + [VMEM] * (2 + len(ks) + len(vs)),
        out_specs=VMEM,
        out_shape=struct((2 * rows, heads * dim)),
        compiler_params=params(),
        cost_estimate=cost(
            heads * 8 * rows * (first + rows) * dim, 0, heads * rows * (first + rows)
        ),
        name="attention",
    )(keep, scale, reading, q, *ks, *vs)


def body_and_decay(ref, h, dim):
    size = ref.shape[0] - TAIL
    high = ref[size + h : size + h + 1, :].astype(F32)
    low = ref[size + TAIL // 2 + h : size + TAIL // 2 + h + 1, :].astype(F32)
    return ref[h * dim : (h + 1) * dim, :].astype(F32), high + low


def scanned(place, refs, h, dim):
    count = len(refs)
    loaded = [body_and_decay(ref, h, dim) for ref in refs]
    state, since = jnp.zeros((dim, refs[0].shape[1]), F32), jnp.ones((1, refs[0].shape[1]), F32)
    before, before_decay = state, since
    for j in range(count):
        before = jnp.where(place == j, state, before)
        before_decay = jnp.where(place == j, since, before_decay)
        body, decay = loaded[0]
        for k in range(1, count):
            here = place == (j ^ k)
            body = jnp.where(here, loaded[k][0], body)
            decay = jnp.where(here, loaded[k][1], decay)
        state = decay * state + body
        since = since * decay
    return before, before_decay, state, since


def quad_kernel(heads, dim, *refs):
    place = lax.rem(lax.axis_index("tm"), len(refs) - 3)
    refs, (before_ref, decay_ref, total_ref) = refs[:-3], refs[-3:]
    size = heads * dim
    total_ref[size:, :] = jnp.zeros((TAIL, total_ref.shape[1]), BF16)
    for h in range(heads):
        rows = slice(h * dim, (h + 1) * dim)
        before, before_decay, state, since = scanned(place, refs, h, dim)
        before_ref[rows, :] = before
        decay_ref[h : h + 1, :] = before_decay
        total_ref[rows, :] = state.astype(BF16)
        high = since.astype(BF16)
        total_ref[size + h : size + h + 1, :] = high
        low = (since - high.astype(F32)).astype(BF16)
        total_ref[size + TAIL // 2 + h : size + TAIL // 2 + h + 1, :] = low


def quad(loads, heads, dim):
    shape = loads[0].shape
    return pl.pallas_call(
        functools.partial(quad_kernel, heads, dim),
        in_specs=[VMEM] * len(loads),
        out_specs=[VMEM] * 3,
        out_shape=[
            struct((heads * dim, shape[1]), F32),
            struct((TAIL // 2, shape[1]), F32),
            struct(shape),
        ],
        compiler_params=params(),
        cost_estimate=cost(loads[0].size * 40, 0),
        name="quad",
    )(*loads)


def entering_kernel(heads, dim, quad_size, before_ref, decay_ref, *refs):
    refs, out_ref = refs[:-1], refs[-1]
    place = lax.div(lax.axis_index("tm"), quad_size)
    for h in range(heads):
        rows = slice(h * dim, (h + 1) * dim)
        earlier = scanned(place, refs, h, dim)[0]
        out_ref[rows, :] = (before_ref[rows, :] + decay_ref[h : h + 1, :] * earlier).astype(BF16)


def entering(quad_size, before, decay, totals, heads, dim):
    return pl.pallas_call(
        functools.partial(entering_kernel, heads, dim, quad_size),
        in_specs=[VMEM] * (2 + len(totals)),
        out_specs=VMEM,
        out_shape=struct(before.shape),
        compiler_params=params(),
        cost_estimate=cost(before.size * 20, 0),
        name="entering",
    )(before, decay, *totals)


def respond_kernel(shards, heads, dim, own_ref, side_ref, own_state_ref, side_state_ref, *refs):
    own_w_ref, side_w_ref, *out_refs = refs
    rows, width = out_refs[0].shape
    head_outs = []
    for pack_ref, state_ref in ((own_ref, own_state_ref), (side_ref, side_state_ref)):
        parts = []
        for h in range(heads):
            cols = slice(h * dim, (h + 1) * dim)
            recalled = dot(pack_ref[:rows, cols], state_ref[cols, :])
            parts.append((pack_ref[rows:, cols].astype(F32) + recalled).astype(BF16))
        head_outs.append(jnp.concatenate(parts, axis=1))
    own, side = head_outs
    for k in reversed(range(shards)):
        owner = lax.rem(lax.axis_index("head") + k, shards)
        cols = pl.ds(pl.multiple_of(owner * width, width), width)
        out = dot(own, own_w_ref[:, cols]) + dot(side, side_w_ref[:, cols])
        out_refs[k][...] = out.astype(out_refs[k].dtype)


def respond(own, side, own_state, side_state, own_w, side_w, shards, heads, dim):
    rows = own.shape[0] // 2
    width = own_w.shape[1] // shards
    return pl.pallas_call(
        functools.partial(respond_kernel, shards, heads, dim),
        in_specs=[VMEM] * 6,
        out_specs=[VMEM] * shards,
        out_shape=[struct((rows, width))] * shards,
        compiler_params=params(),
        cost_estimate=cost(4 * rows * own_w.size, 0),
        name="respond",
    )(own, side, own_state, side_state, own_w, side_w)


def finish_kernel(count, *refs):
    total = refs[0][...].astype(F32)
    for ref in refs[1:count]:
        total += ref[...].astype(F32)
    refs[-1][...] = total.astype(BF16)


def finish(parts, result, first, length):
    rows, width = parts[0].shape
    chunk = first // rows
    whole = pl.BlockSpec((rows, width), lambda i: (0, 0))
    more = [] if result is None else [result]
    return pl.pallas_call(
        functools.partial(finish_kernel, len(parts)),
        grid=(1,),
        in_specs=[whole] * len(parts) + [pl.BlockSpec(memory_space=pl.ANY)] * len(more),
        out_specs=pl.BlockSpec((rows, width), lambda i: (chunk, 0)),
        out_shape=struct((length, width)),
        input_output_aliases={len(parts): 0} if more else {},
        compiler_params=params(),
        cost_estimate=cost(rows * width * 2, rows * width * 6),
        name="finish",
    )(*parts, *more)


def per_device(
    residual_signal,
    prescale_amplifier,
    triple_projector,
    score_scaler,
    recall_retained_logshare,
    tile_retain_grid,
    recall_store_flags,
    emission_projector,
    sideways_coupling_coef,
):
    x = residual_signal[0]
    length = x.shape[0]
    sizes = [CHUNK] * (length // CHUNK - 1) + [LAST] * (CHUNK // LAST)
    firsts = [sum(sizes[:c]) for c in range(len(sizes))]
    chunks = len(sizes)
    shards = lax.axis_size("head")
    blocks = lax.axis_size("tm")
    heads = triple_projector.shape[2]
    dim = emission_projector.shape[2]
    swap_streams = [(0, 1), (1, 0)]
    tied = lambda *arrays: lax.optimization_barrier(arrays)

    own_w = emission_projector[0].reshape(heads * dim, -1)
    side_w = lax.ppermute(
        sideways_coupling_coef[0].reshape(heads * dim, -1), "stream", swap_streams
    )
    fade, tail, *readings = prepare(
        recall_retained_logshare[0],
        recall_store_flags,
        dim,
        1.0 / math.sqrt(dim * length * blocks),
        sizes,
    )
    pieces = [x[first : first + size] for first, size in zip(firsts, sizes)]
    received = []
    for c in range(chunks):
        if c == chunks - 2:
            pieces[c], pieces[c + 1], tail = tied(pieces[c], pieces[c + 1], tail)
        xs = [pieces[c]]
        for k in range(1, shards):
            xs.append(
                lax.ppermute(pieces[c], "head", [((d + k) % shards, d) for d in range(shards)])
            )
        received.append(xs)
    gain = prescale_amplifier
    w = triple_projector[0].reshape(-1, 3 * heads * dim)

    qs, ks, vs, packs, sides = [], [], [], [], []
    summary = None
    for c, first in enumerate(firsts[:-1]):
        q, k, v, summary = qkv(gain, w, fade, summary, received[c], heads, dim, first)
        qs.append(q)
        ks.append(k)
        vs.append(v)
        if c < chunks - 2:
            pack = attention(
                first, tile_retain_grid, score_scaler, readings[c], q, ks, vs, heads, dim
            )
            if c == 0:
                pack, side_w = tied(pack, side_w)
            summary, pack = tied(summary, pack)
            packs.append(pack)
            if c < 2:
                sides.append(lax.ppermute(pack, "stream", swap_streams))
    k, v, sent = last_keys_values(
        gain, w, fade, summary, tail, received[-1], heads, dim, firsts[-1]
    )
    ks.append(k)
    vs.append(v)

    quad_size = min(4, blocks)
    loads = [sent] + [
        lax.ppermute(sent, "tm", [(d, d ^ k) for d in range(blocks)]) for k in range(1, quad_size)
    ]
    qs.append(last_queries(gain, w, received[-1], heads, dim))
    for c in range(chunks - 2, chunks):
        packs.append(
            attention(
                firsts[c],
                tile_retain_grid,
                score_scaler,
                readings[c],
                qs[c],
                ks[: c + 1],
                vs[: c + 1],
                heads,
                dim,
            )
        )
    *loads, packs[-2] = tied(*loads, packs[-2])
    before, decay, total = quad(loads, heads, dim)
    totals = [total] + [
        lax.ppermute(total, "tm", [(d, d ^ (quad_size * k)) for d in range(blocks)])
        for k in range(1, blocks // quad_size)
    ]
    sides += [lax.ppermute(pack, "stream", swap_streams) for pack in packs[2:]]
    *totals, sides[2], sides[3], packs[-1] = tied(*totals, sides[2], sides[3], packs[-1])
    state = entering(quad_size, before, decay, totals, heads, dim)

    side_state = lax.ppermute(state, "stream", swap_streams)
    result = None
    for c in range(chunks):
        outs = respond(
            packs[c], sides[c], state, side_state, own_w, side_w, shards, heads, dim
        )
        parts = [outs[0]]
        for k in range(1, shards):
            parts.append(
                lax.ppermute(outs[k], "head", [(d, (d + k) % shards) for d in range(shards)])
            )
        result = finish(parts, result, firsts[c], length)
    return result[None]


def solution(mesh):
    placed = (
        P("stream", "tm", "head"),
        P("stream", None),
        P("stream", None, "head", None),
        P("stream", "head"),
        P("stream", "head", "tm"),
        P("tm", None),
        P("tm"),
        P("stream", "head", None, None),
        P("stream", "head", None, None),
    )
    return jax.shard_map(
        per_device, mesh=mesh, in_specs=placed, out_specs=P("stream", "tm", "head"), check_vma=False
    )
```

```python
import functools
import math

import jax
import jax.numpy as jnp
from jax import lax
from jax.experimental import pallas as pl
from jax.experimental.pallas import tpu as pltpu
from jax.sharding import PartitionSpec as P

BLOCK = 512
CHUNK = 256
LAST = 128
TAIL = 16
EPSILON = 1e-06
F32 = jnp.float32
BF16 = jnp.bfloat16
SMEM = pl.BlockSpec(memory_space=pltpu.SMEM)
VMEM = pl.BlockSpec(memory_space=pltpu.VMEM)


def params():
    return pltpu.CompilerParams(vmem_limit_bytes=16 * 1024 * 1024)


def cost(flops, bytes_accessed, transcendentals=0):
    return pl.CostEstimate(
        flops=int(flops), bytes_accessed=int(bytes_accessed), transcendentals=int(transcendentals)
    )


def struct(shape, dtype=BF16):
    return jax.ShapeDtypeStruct(shape, dtype)


def dot(a, b):
    return lax.dot_general(a, b, (((1,), (0,)), ((), ())), preferred_element_type=F32)


def dot_nt(a, b):
    return lax.dot_general(a, b, (((1,), (1,)), ((), ())), preferred_element_type=F32)


def dot_tn(a, b):
    return lax.dot_general(a, b, (((0,), (0,)), ((), ())), preferred_element_type=F32)


def unit(values):
    return values * lax.rsqrt(jnp.mean(values * values, axis=-1, keepdims=True) + EPSILON)


def prepare_kernel(heads, factor, logs_ref, flags_ref, fade_ref, tail_ref, *refs):
    reading_refs, rows_ref = refs[:-1], refs[-1]
    length = logs_ref.shape[1]
    rows_ref[...] = jnp.zeros_like(rows_ref)
    rows_ref[:heads, :] = logs_ref[...]
    running = rows_ref[...]
    place = lax.broadcasted_iota(jnp.int32, running.shape, 1)
    step = 1
    while step < length:
        running += jnp.where(place >= step, pltpu.roll(running, step, 1), 0.0)
        step *= 2
    last = running[:, length - 1 :]
    chosen = jnp.zeros_like(running)
    for block in range(length // BLOCK):
        inside = (place >= block * BLOCK) & (place < (block + 1) * BLOCK)
        chosen = jnp.where(inside, flags_ref[block].astype(F32), chosen)
    fade_ref[...] = jnp.transpose(jnp.exp(last - running) * chosen)
    reading = jnp.transpose(jnp.exp(running) * factor)
    first = 0
    for ref in reading_refs:
        ref[...] = reading[first : first + ref.shape[0]]
        first += ref.shape[0]
    decay = jnp.exp(last)
    high = decay.astype(BF16).astype(F32)
    both = jnp.concatenate([high, decay - high], axis=0)
    tail_ref[...] = jnp.broadcast_to(both, tail_ref.shape).astype(BF16)


def prepare(logs, flags, dim, factor, sizes):
    heads, length = logs.shape
    lines = TAIL // 2
    return pl.pallas_call(
        functools.partial(prepare_kernel, heads, factor),
        in_specs=[VMEM, SMEM],
        out_specs=[VMEM] * (2 + len(sizes)),
        out_shape=[struct((length, lines), F32), struct((TAIL, dim))]
        + [struct((size, lines), F32) for size in sizes],
        scratch_shapes=[pltpu.VMEM((lines, length), F32)],
        compiler_params=params(),
        cost_estimate=cost(40 * lines * length, 0),
        name="prepare",
    )(logs, flags)


def normed_parts(gain_ref, x_refs):
    me = lax.axis_index("head")
    shards, width = len(x_refs), x_refs[0].shape[1]
    parts = [x[...].astype(F32) for x in x_refs]
    squares = sum(jnp.sum(p * p, axis=-1, keepdims=True) for p in parts)
    scale = lax.rsqrt(squares * (1.0 / (width * shards)) + EPSILON)
    out = []
    for k, part in enumerate(parts):
        owner = lax.rem(me + k, shards)
        rows = pl.ds(pl.multiple_of(owner * width, width), width)
        out.append(((part * scale * gain_ref[:, rows]).astype(BF16), rows))
    return out


def projected(parts, w_ref, cols):
    total = None
    for part, rows in parts:
        term = dot(part, w_ref[rows, cols])
        total = term if total is None else total + term
    return total


def add_summary(sum_ref, h, key, value, fade_ref, first):
    fade = fade_ref[first : first + key.shape[0], h : h + 1]
    sum_ref[h] += dot_tn((key.astype(F32) * fade).astype(BF16), value)


def qkv_kernel(heads, dim, first, gain_ref, w_ref, fade_ref, *refs):
    refs, (q_ref, k_ref, v_ref, sum_ref) = refs[:-4], refs[-4:]
    if first == 0:
        sum_ref[...] = jnp.zeros_like(sum_ref)
        x_refs = refs
    else:
        sum_ref[...] = refs[0][...]
        x_refs = refs[1:]
    parts = normed_parts(gain_ref, x_refs)
    wide = heads * dim
    thirds = [projected(parts, w_ref, slice(i * wide, (i + 1) * wide)) for i in range(3)]
    taken = lambda at: thirds[at * dim // wide][:, at * dim % wide : at * dim % wide + dim]
    for h in range(heads):
        cols = slice(h * dim, (h + 1) * dim)
        q_ref[:, cols] = unit(taken(3 * h)).astype(BF16)
        key = unit(taken(3 * h + 1)).astype(BF16)
        value = taken(3 * h + 2).astype(BF16)
        k_ref[:, cols] = key
        v_ref[:, cols] = value
        add_summary(sum_ref, h, key, value, fade_ref, first)


def qkv(gain, w, fade, prev, xs, heads, dim, first):
    rows = xs[0].shape[0]
    before = [prev] if first else []
    return pl.pallas_call(
        functools.partial(qkv_kernel, heads, dim, first),
        in_specs=[VMEM] * (3 + len(before) + len(xs)),
        out_specs=[VMEM] * 4,
        out_shape=[struct((rows, heads * dim))] * 3 + [struct((heads, dim, dim), F32)],
        compiler_params=params(),
        cost_estimate=cost(4 * rows * w.size, 0),
        name="qkv",
    )(gain, w, fade, *before, *xs)


def last_kernel(heads, dim, first, gain_ref, w_ref, fade_ref, prev_ref, tail_ref, *refs):
    x_refs, (k_ref, v_ref, send_ref, sum_ref) = refs[:-4], refs[-4:]
    sum_ref[...] = prev_ref[...]
    parts = normed_parts(gain_ref, x_refs)
    pairs = [
        projected(parts, w_ref, slice((3 * h + 1) * dim, (3 * h + 3) * dim)) for h in range(heads)
    ]
    for h in range(heads):
        cols = slice(h * dim, (h + 1) * dim)
        key = unit(pairs[h][:, :dim]).astype(BF16)
        value = pairs[h][:, dim:].astype(BF16)
        k_ref[:, cols] = key
        v_ref[:, cols] = value
        add_summary(sum_ref, h, key, value, fade_ref, first)
        send_ref[cols, :] = sum_ref[h].astype(BF16)
    send_ref[heads * dim :, :] = tail_ref[...]


def last_keys_values(gain, w, fade, prev, tail, xs, heads, dim, first):
    rows = xs[0].shape[0]
    return pl.pallas_call(
        functools.partial(last_kernel, heads, dim, first),
        in_specs=[VMEM] * (5 + len(xs)),
        out_specs=[VMEM] * 3,
        out_shape=[struct((rows, heads * dim))] * 2 + [struct((heads * dim + TAIL, dim))],
        scratch_shapes=[pltpu.VMEM((heads, dim, dim), F32)],
        compiler_params=params(),
        cost_estimate=cost(3 * rows * w.size, 0),
        name="last_keys_values",
    )(gain, w, fade, prev, tail, *xs)


def queries_kernel(heads, dim, gain_ref, w_ref, *refs):
    q_ref = refs[-1]
    parts = normed_parts(gain_ref, refs[:-1])
    for h in range(heads):
        base = 3 * h * dim
        cols = slice(h * dim, (h + 1) * dim)
        q_ref[:, cols] = unit(projected(parts, w_ref, slice(base, base + dim))).astype(BF16)


def last_queries(gain, w, xs, heads, dim):
    rows = xs[0].shape[0]
    return pl.pallas_call(
        functools.partial(queries_kernel, heads, dim),
        in_specs=[VMEM] * (2 + len(xs)),
        out_specs=VMEM,
        out_shape=struct((rows, heads * dim)),
        compiler_params=params(),
        cost_estimate=cost(2 * rows * w.size, 0),
        name="last_queries",
    )(gain, w, *xs)


def attention_kernel(first, heads, dim, keep_ref, scale_ref, q_ref, *refs):
    count = len(refs) // 2
    k_refs, v_refs, out_ref = refs[:count], refs[count:-1], refs[-1]
    rows = q_ref.shape[0]
    block = first // BLOCK
    causal = lax.broadcasted_iota(jnp.int32, (rows, rows), 1) <= lax.broadcasted_iota(
        jnp.int32, (rows, rows), 0
    )
    for h in range(heads):
        cols = slice(h * dim, (h + 1) * dim)
        query = q_ref[:, cols]
        scale = scale_ref[0, h] * (1.0 / math.sqrt(dim))
        total, at = None, 0
        for j in range(count):
            keys = k_refs[j].shape[0]
            powers = jnp.exp(dot_nt(query, k_refs[j][:, cols]) * scale)
            if at == first:
                powers = jnp.where(causal, powers, 0.0)
            ones = jnp.ones((keys, dim), BF16)
            part = dot(powers.astype(BF16), jnp.concatenate([v_refs[j][:, cols], ones], axis=1))
            if at // BLOCK < block:
                part = jnp.where(keep_ref[block, at // BLOCK] == 1, part, 0.0)
            total = part if total is None else total + part
            at += keys
        out_ref[:, cols] = (total[:, :dim] / total[:, dim:]).astype(BF16)


def attention(first, keep, scale, q, ks, vs, heads, dim):
    rows = q.shape[0]
    return pl.pallas_call(
        functools.partial(attention_kernel, first, heads, dim),
        in_specs=[SMEM, SMEM] + [VMEM] * (1 + len(ks) + len(vs)),
        out_specs=VMEM,
        out_shape=struct(q.shape),
        compiler_params=params(),
        cost_estimate=cost(
            heads * 8 * rows * (first + rows) * dim, 0, heads * rows * (first + rows)
        ),
        name="attention",
    )(keep, scale, q, *ks, *vs)


def body_and_decay(ref, h, dim):
    size = ref.shape[0] - TAIL
    high = ref[size + h : size + h + 1, :].astype(F32)
    low = ref[size + TAIL // 2 + h : size + TAIL // 2 + h + 1, :].astype(F32)
    return ref[h * dim : (h + 1) * dim, :].astype(F32), high + low


def scanned(place, refs, h, dim):
    count = len(refs)
    loaded = [body_and_decay(ref, h, dim) for ref in refs]
    state, since = jnp.zeros((dim, refs[0].shape[1]), F32), jnp.ones((1, refs[0].shape[1]), F32)
    before, before_decay = state, since
    for j in range(count):
        before = jnp.where(place == j, state, before)
        before_decay = jnp.where(place == j, since, before_decay)
        body, decay = loaded[0]
        for k in range(1, count):
            here = place == (j ^ k)
            body = jnp.where(here, loaded[k][0], body)
            decay = jnp.where(here, loaded[k][1], decay)
        state = decay * state + body
        since = since * decay
    return before, before_decay, state, since


def quad_kernel(heads, dim, *refs):
    place = lax.rem(lax.axis_index("tm"), len(refs) - 3)
    refs, (before_ref, decay_ref, total_ref) = refs[:-3], refs[-3:]
    size = heads * dim
    total_ref[size:, :] = jnp.zeros((TAIL, total_ref.shape[1]), BF16)
    for h in range(heads):
        rows = slice(h * dim, (h + 1) * dim)
        before, before_decay, state, since = scanned(place, refs, h, dim)
        before_ref[rows, :] = before
        decay_ref[h : h + 1, :] = before_decay
        total_ref[rows, :] = state.astype(BF16)
        high = since.astype(BF16)
        total_ref[size + h : size + h + 1, :] = high
        low = (since - high.astype(F32)).astype(BF16)
        total_ref[size + TAIL // 2 + h : size + TAIL // 2 + h + 1, :] = low


def quad(loads, heads, dim):
    shape = loads[0].shape
    return pl.pallas_call(
        functools.partial(quad_kernel, heads, dim),
        in_specs=[VMEM] * len(loads),
        out_specs=[VMEM] * 3,
        out_shape=[
            struct((heads * dim, shape[1]), F32),
            struct((TAIL // 2, shape[1]), F32),
            struct(shape),
        ],
        compiler_params=params(),
        cost_estimate=cost(loads[0].size * 40, 0),
        name="quad",
    )(*loads)


def entering_kernel(heads, dim, before_ref, decay_ref, *refs):
    refs, out_ref = refs[:-1], refs[-1]
    for h in range(heads):
        rows = slice(h * dim, (h + 1) * dim)
        earlier = jnp.zeros((dim, out_ref.shape[1]), F32)
        for ref in reversed(refs):
            body, decay = body_and_decay(ref, h, dim)
            earlier = body + decay * earlier
        out_ref[rows, :] = (before_ref[rows, :] + decay_ref[h : h + 1, :] * earlier).astype(BF16)


def entering(before, decay, totals, heads, dim):
    return pl.pallas_call(
        functools.partial(entering_kernel, heads, dim),
        in_specs=[VMEM] * (2 + len(totals)),
        out_specs=VMEM,
        out_shape=struct(before.shape),
        compiler_params=params(),
        cost_estimate=cost(before.size * 20, 0),
        name="entering",
    )(before, decay, *totals)


def recall_kernel(heads, dim, reading_ref, q_ref, local_ref, state_ref, out_ref):
    for h in range(heads):
        cols = slice(h * dim, (h + 1) * dim)
        recalled = dot(q_ref[:, cols], state_ref[cols, :]) * reading_ref[:, h : h + 1]
        out_ref[:, cols] = (local_ref[:, cols].astype(F32) + recalled).astype(BF16)


def recall(reading, q, local, state, heads, dim):
    return pl.pallas_call(
        functools.partial(recall_kernel, heads, dim),
        in_specs=[VMEM] * 4,
        out_specs=VMEM,
        out_shape=struct(q.shape),
        compiler_params=params(),
        cost_estimate=cost(4 * q.size * dim, 0),
        name="recall",
    )(reading, q, local, state)


def project_kernel(shards, own_ref, side_ref, own_w_ref, side_w_ref, *out_refs):
    width = out_refs[0].shape[1]
    own, side = own_ref[...], side_ref[...]
    for k in reversed(range(shards)):
        owner = lax.rem(lax.axis_index("head") + k, shards)
        cols = pl.ds(pl.multiple_of(owner * width, width), width)
        out = dot(own, own_w_ref[:, cols]) + dot(side, side_w_ref[:, cols])
        out_refs[k][...] = out.astype(out_refs[k].dtype)


def project(own, side, own_w, side_w, shards):
    rows = own.shape[0]
    width = own_w.shape[1] // shards
    return pl.pallas_call(
        functools.partial(project_kernel, shards),
        in_specs=[VMEM] * 4,
        out_specs=[VMEM] * shards,
        out_shape=[struct((rows, width))] * shards,
        compiler_params=params(),
        cost_estimate=cost(4 * rows * own_w.size, 0),
        name="project",
    )(own, side, own_w, side_w)


def finish_kernel(count, *refs):
    total = refs[0][...].astype(F32)
    for ref in refs[1:count]:
        total += ref[...].astype(F32)
    refs[-1][...] = total.astype(BF16)


def finish(parts, result, first, length):
    rows, width = parts[0].shape
    chunk = first // rows
    whole = pl.BlockSpec((rows, width), lambda i: (0, 0))
    more = [] if result is None else [result]
    return pl.pallas_call(
        functools.partial(finish_kernel, len(parts)),
        grid=(1,),
        in_specs=[whole] * len(parts) + [pl.BlockSpec(memory_space=pl.ANY)] * len(more),
        out_specs=pl.BlockSpec((rows, width), lambda i: (chunk, 0)),
        out_shape=struct((length, width)),
        input_output_aliases={len(parts): 0} if more else {},
        compiler_params=params(),
        cost_estimate=cost(rows * width * 2, rows * width * 6),
        name="finish",
    )(*parts, *more)


def per_device(
    residual_signal,
    prescale_amplifier,
    triple_projector,
    score_scaler,
    recall_retained_logshare,
    tile_retain_grid,
    recall_store_flags,
    emission_projector,
    sideways_coupling_coef,
):
    x = residual_signal[0]
    length = x.shape[0]
    sizes = [CHUNK] * (length // CHUNK - 1) + [LAST] * (CHUNK // LAST)
    firsts = [sum(sizes[:c]) for c in range(len(sizes))]
    chunks = len(sizes)
    shards = lax.axis_size("head")
    blocks = lax.axis_size("tm")
    heads = triple_projector.shape[2]
    dim = emission_projector.shape[2]
    swap_streams = [(0, 1), (1, 0)]
    tied = lambda *arrays: lax.optimization_barrier(arrays)

    own_w = emission_projector[0].reshape(heads * dim, -1)
    side_w = lax.ppermute(
        sideways_coupling_coef[0].reshape(heads * dim, -1), "stream", swap_streams
    )
    fade, tail, *readings = prepare(
        recall_retained_logshare[0],
        recall_store_flags,
        dim,
        1.0 / math.sqrt(dim * length * blocks),
        sizes,
    )
    pieces = [x[first : first + size] for first, size in zip(firsts, sizes)]
    received = []
    for c in range(chunks):
        if c == chunks - 2:
            pieces[c], pieces[c + 1], tail = tied(pieces[c], pieces[c + 1], tail)
        xs = [pieces[c]]
        for k in range(1, shards):
            xs.append(
                lax.ppermute(pieces[c], "head", [((d + k) % shards, d) for d in range(shards)])
            )
        received.append(xs)
    gain = prescale_amplifier
    w = triple_projector[0].reshape(-1, 3 * heads * dim)

    qs, ks, vs, locals_ = [], [], [], []
    summary = None
    for c, first in enumerate(firsts[:-1]):
        q, k, v, summary = qkv(gain, w, fade, summary, received[c], heads, dim, first)
        qs.append(q)
        ks.append(k)
        vs.append(v)
        if c < chunks - 2:
            local = attention(first, tile_retain_grid, score_scaler, q, ks, vs, heads, dim)
            summary, local = tied(summary, local)
            locals_.append(local)
    k, v, sent = last_keys_values(
        gain, w, fade, summary, tail, received[-1], heads, dim, firsts[-1]
    )
    ks.append(k)
    vs.append(v)

    quad_size = min(4, blocks)
    loads = [sent] + [
        lax.ppermute(sent, "tm", [(d, d ^ k) for d in range(blocks)]) for k in range(1, quad_size)
    ]
    qs.append(last_queries(gain, w, received[-1], heads, dim))
    for c in range(chunks - 2, chunks):
        locals_.append(
            attention(
                firsts[c], tile_retain_grid, score_scaler, qs[c], ks[: c + 1], vs[: c + 1], heads, dim
            )
        )
    *loads, locals_[-2] = tied(*loads, locals_[-2])
    before, decay, total = quad(loads, heads, dim)
    totals = [
        lax.ppermute(total, "tm", [(d, d + quad_size * k) for d in range(blocks - quad_size * k)])
        for k in range(1, blocks // quad_size)
    ]
    *totals, locals_[-1] = tied(*totals, locals_[-1])
    state = entering(before, decay, totals, heads, dim)

    result = None
    for c in range(chunks):
        head_out = recall(readings[c], qs[c], locals_[c], state, heads, dim)
        side = lax.ppermute(head_out, "stream", swap_streams)
        outs = project(head_out, side, own_w, side_w, shards)
        parts = [outs[0]]
        for k in range(1, shards):
            parts.append(
                lax.ppermute(outs[k], "head", [(d, (d + k) % shards) for d in range(shards)])
            )
        result = finish(parts, result, firsts[c], length)
    return result[None]


def solution(mesh):
    placed = (
        P("stream", "tm", "head"),
        P("stream", None),
        P("stream", None, "head", None),
        P("stream", "head"),
        P("stream", "head", "tm"),
        P("tm", None),
        P("tm"),
        P("stream", "head", None, None),
        P("stream", "head", None, None),
    )
    return jax.shard_map(
        per_device, mesh=mesh, in_specs=placed, out_specs=P("stream", "tm", "head"), check_vma=False
    )
```

```python
import functools
import math

import jax
import jax.numpy as jnp
from jax import lax
from jax.experimental import pallas as pl
from jax.experimental.pallas import tpu as pltpu
from jax.sharding import PartitionSpec as P

BLOCK = 512
CHUNK = 256
LAST = 128
TAIL = 16
EPSILON = 1e-06
F32 = jnp.float32
BF16 = jnp.bfloat16
SMEM = pl.BlockSpec(memory_space=pltpu.SMEM)
VMEM = pl.BlockSpec(memory_space=pltpu.VMEM)


def params():
    return pltpu.CompilerParams(vmem_limit_bytes=16 * 1024 * 1024)


def cost(flops, bytes_accessed, transcendentals=0):
    return pl.CostEstimate(
        flops=int(flops), bytes_accessed=int(bytes_accessed), transcendentals=int(transcendentals)
    )


def struct(shape, dtype=BF16):
    return jax.ShapeDtypeStruct(shape, dtype)


def dot(a, b):
    return lax.dot_general(a, b, (((1,), (0,)), ((), ())), preferred_element_type=F32)


def dot_nt(a, b):
    return lax.dot_general(a, b, (((1,), (1,)), ((), ())), preferred_element_type=F32)


def dot_tn(a, b):
    return lax.dot_general(a, b, (((0,), (0,)), ((), ())), preferred_element_type=F32)


def unit(values):
    return values * lax.rsqrt(jnp.mean(values * values, axis=-1, keepdims=True) + EPSILON)


def prepare_kernel(heads, factor, logs_ref, flags_ref, fade_ref, tail_ref, *refs):
    reading_refs, rows_ref = refs[:-1], refs[-1]
    length = logs_ref.shape[1]
    rows_ref[...] = jnp.zeros_like(rows_ref)
    rows_ref[:heads, :] = logs_ref[...]
    running = rows_ref[...]
    place = lax.broadcasted_iota(jnp.int32, running.shape, 1)
    step = 1
    while step < length:
        running += jnp.where(place >= step, pltpu.roll(running, step, 1), 0.0)
        step *= 2
    last = running[:, length - 1 :]
    chosen = jnp.zeros_like(running)
    for block in range(length // BLOCK):
        inside = (place >= block * BLOCK) & (place < (block + 1) * BLOCK)
        chosen = jnp.where(inside, flags_ref[block].astype(F32), chosen)
    fade_ref[...] = jnp.transpose(jnp.exp(last - running) * chosen)
    reading = jnp.transpose(jnp.exp(running) * factor)
    first = 0
    for ref in reading_refs:
        ref[...] = reading[first : first + ref.shape[0]]
        first += ref.shape[0]
    decay = jnp.exp(last)
    high = decay.astype(BF16).astype(F32)
    both = jnp.concatenate([high, decay - high], axis=0)
    tail_ref[...] = jnp.broadcast_to(both, tail_ref.shape).astype(BF16)


def prepare(logs, flags, dim, factor, sizes):
    heads, length = logs.shape
    lines = TAIL // 2
    return pl.pallas_call(
        functools.partial(prepare_kernel, heads, factor),
        in_specs=[VMEM, SMEM],
        out_specs=[VMEM] * (2 + len(sizes)),
        out_shape=[struct((length, lines), F32), struct((TAIL, dim))]
        + [struct((size, lines), F32) for size in sizes],
        scratch_shapes=[pltpu.VMEM((lines, length), F32)],
        compiler_params=params(),
        cost_estimate=cost(40 * lines * length, 0),
        name="prepare",
    )(logs, flags)


def normed_parts(gain_ref, x_refs):
    me = lax.axis_index("head")
    shards, width = len(x_refs), x_refs[0].shape[1]
    parts = [x[...].astype(F32) for x in x_refs]
    squares = sum(jnp.sum(p * p, axis=-1, keepdims=True) for p in parts)
    scale = lax.rsqrt(squares * (1.0 / (width * shards)) + EPSILON)
    out = []
    for k, part in enumerate(parts):
        owner = lax.rem(me + k, shards)
        rows = pl.ds(pl.multiple_of(owner * width, width), width)
        out.append(((part * scale * gain_ref[:, rows]).astype(BF16), rows))
    return out


def projected(parts, w_ref, cols):
    total = None
    for part, rows in parts:
        term = dot(part, w_ref[rows, cols])
        total = term if total is None else total + term
    return total


def add_summary(sum_ref, h, key, value, fade_ref, first):
    fade = fade_ref[first : first + key.shape[0], h : h + 1]
    sum_ref[h] += dot_tn((key.astype(F32) * fade).astype(BF16), value)


def qkv_kernel(heads, dim, first, gain_ref, w_ref, fade_ref, *refs):
    refs, (q_ref, k_ref, v_ref, sum_ref) = refs[:-4], refs[-4:]
    if first == 0:
        sum_ref[...] = jnp.zeros_like(sum_ref)
        x_refs = refs
    else:
        sum_ref[...] = refs[0][...]
        x_refs = refs[1:]
    parts = normed_parts(gain_ref, x_refs)
    wide = heads * dim
    thirds = [projected(parts, w_ref, slice(i * wide, (i + 1) * wide)) for i in range(3)]
    taken = lambda at: thirds[at * dim // wide][:, at * dim % wide : at * dim % wide + dim]
    for h in range(heads):
        cols = slice(h * dim, (h + 1) * dim)
        q_ref[:, cols] = unit(taken(3 * h)).astype(BF16)
        key = unit(taken(3 * h + 1)).astype(BF16)
        value = taken(3 * h + 2).astype(BF16)
        k_ref[:, cols] = key
        v_ref[:, cols] = value
        add_summary(sum_ref, h, key, value, fade_ref, first)


def qkv(gain, w, fade, prev, xs, heads, dim, first):
    rows = xs[0].shape[0]
    before = [prev] if first else []
    return pl.pallas_call(
        functools.partial(qkv_kernel, heads, dim, first),
        in_specs=[VMEM] * (3 + len(before) + len(xs)),
        out_specs=[VMEM] * 4,
        out_shape=[struct((rows, heads * dim))] * 3 + [struct((heads, dim, dim), F32)],
        compiler_params=params(),
        cost_estimate=cost(4 * rows * w.size, 0),
        name="qkv",
    )(gain, w, fade, *before, *xs)


def last_kernel(heads, dim, first, gain_ref, w_ref, fade_ref, prev_ref, tail_ref, *refs):
    x_refs, (k_ref, v_ref, send_ref, sum_ref) = refs[:-4], refs[-4:]
    sum_ref[...] = prev_ref[...]
    parts = normed_parts(gain_ref, x_refs)
    pairs = [
        projected(parts, w_ref, slice((3 * h + 1) * dim, (3 * h + 3) * dim)) for h in range(heads)
    ]
    for h in range(heads):
        cols = slice(h * dim, (h + 1) * dim)
        key = unit(pairs[h][:, :dim]).astype(BF16)
        value = pairs[h][:, dim:].astype(BF16)
        k_ref[:, cols] = key
        v_ref[:, cols] = value
        add_summary(sum_ref, h, key, value, fade_ref, first)
        send_ref[cols, :] = sum_ref[h].astype(BF16)
    send_ref[heads * dim :, :] = tail_ref[...]


def last_keys_values(gain, w, fade, prev, tail, xs, heads, dim, first):
    rows = xs[0].shape[0]
    return pl.pallas_call(
        functools.partial(last_kernel, heads, dim, first),
        in_specs=[VMEM] * (5 + len(xs)),
        out_specs=[VMEM] * 3,
        out_shape=[struct((rows, heads * dim))] * 2 + [struct((heads * dim + TAIL, dim))],
        scratch_shapes=[pltpu.VMEM((heads, dim, dim), F32)],
        compiler_params=params(),
        cost_estimate=cost(3 * rows * w.size, 0),
        name="last_keys_values",
    )(gain, w, fade, prev, tail, *xs)


def queries_kernel(heads, dim, gain_ref, w_ref, *refs):
    q_ref = refs[-1]
    parts = normed_parts(gain_ref, refs[:-1])
    for h in range(heads):
        base = 3 * h * dim
        cols = slice(h * dim, (h + 1) * dim)
        q_ref[:, cols] = unit(projected(parts, w_ref, slice(base, base + dim))).astype(BF16)


def last_queries(gain, w, xs, heads, dim):
    rows = xs[0].shape[0]
    return pl.pallas_call(
        functools.partial(queries_kernel, heads, dim),
        in_specs=[VMEM] * (2 + len(xs)),
        out_specs=VMEM,
        out_shape=struct((rows, heads * dim)),
        compiler_params=params(),
        cost_estimate=cost(2 * rows * w.size, 0),
        name="last_queries",
    )(gain, w, *xs)


def attention_kernel(first, heads, dim, keep_ref, scale_ref, q_ref, *refs):
    count = len(refs) // 2
    k_refs, v_refs, out_ref = refs[:count], refs[count:-1], refs[-1]
    rows = q_ref.shape[0]
    block = first // BLOCK
    causal = lax.broadcasted_iota(jnp.int32, (rows, rows), 1) <= lax.broadcasted_iota(
        jnp.int32, (rows, rows), 0
    )
    for h in range(heads):
        cols = slice(h * dim, (h + 1) * dim)
        query = q_ref[:, cols]
        scale = scale_ref[0, h] * (1.0 / math.sqrt(dim))
        total, at = None, 0
        for j in range(count):
            keys = k_refs[j].shape[0]
            powers = jnp.exp(dot_nt(query, k_refs[j][:, cols]) * scale)
            if at == first:
                powers = jnp.where(causal, powers, 0.0)
            ones = jnp.ones((keys, dim), BF16)
            part = dot(powers.astype(BF16), jnp.concatenate([v_refs[j][:, cols], ones], axis=1))
            if at // BLOCK < block:
                part = jnp.where(keep_ref[block, at // BLOCK] == 1, part, 0.0)
            total = part if total is None else total + part
            at += keys
        out_ref[:, cols] = (total[:, :dim] / total[:, dim:]).astype(BF16)


def attention(first, keep, scale, q, ks, vs, heads, dim):
    rows = q.shape[0]
    return pl.pallas_call(
        functools.partial(attention_kernel, first, heads, dim),
        in_specs=[SMEM, SMEM] + [VMEM] * (1 + len(ks) + len(vs)),
        out_specs=VMEM,
        out_shape=struct(q.shape),
        compiler_params=params(),
        cost_estimate=cost(
            heads * 8 * rows * (first + rows) * dim, 0, heads * rows * (first + rows)
        ),
        name="attention",
    )(keep, scale, q, *ks, *vs)


def body_and_decay(ref, h, dim):
    size = ref.shape[0] - TAIL
    high = ref[size + h : size + h + 1, :].astype(F32)
    low = ref[size + TAIL // 2 + h : size + TAIL // 2 + h + 1, :].astype(F32)
    return ref[h * dim : (h + 1) * dim, :].astype(F32), high + low


def scanned(place, loaded):
    state, since = jnp.zeros_like(loaded[0][0]), jnp.ones_like(loaded[0][1])
    before, before_decay = state, since
    for j in range(len(loaded)):
        before = jnp.where(place == j, state, before)
        before_decay = jnp.where(place == j, since, before_decay)
        body, decay = loaded[0]
        for k in range(1, len(loaded)):
            here = place == (j ^ k)
            body = jnp.where(here, loaded[k][0], body)
            decay = jnp.where(here, loaded[k][1], decay)
        state = decay * state + body
        since = since * decay
    return before, before_decay, state, since


def quad_kernel(heads, dim, *refs):
    place = lax.rem(lax.axis_index("tm"), len(refs) - 3)
    refs, (before_ref, decay_ref, total_ref) = refs[:-3], refs[-3:]
    size = heads * dim
    total_ref[size:, :] = jnp.zeros((TAIL, total_ref.shape[1]), BF16)
    for h in range(heads):
        rows = slice(h * dim, (h + 1) * dim)
        loaded = [body_and_decay(ref, h, dim) for ref in refs]
        before, before_decay, state, since = scanned(place, loaded)
        before_ref[rows, :] = before
        decay_ref[h : h + 1, :] = before_decay
        total_ref[rows, :] = state.astype(BF16)
        high = since.astype(BF16)
        total_ref[size + h : size + h + 1, :] = high
        low = (since - high.astype(F32)).astype(BF16)
        total_ref[size + TAIL // 2 + h : size + TAIL // 2 + h + 1, :] = low


def quad(loads, heads, dim):
    shape = loads[0].shape
    return pl.pallas_call(
        functools.partial(quad_kernel, heads, dim),
        in_specs=[VMEM] * len(loads),
        out_specs=[VMEM] * 3,
        out_shape=[
            struct((heads * dim, shape[1]), F32),
            struct((TAIL // 2, shape[1]), F32),
            struct(shape),
        ],
        compiler_params=params(),
        cost_estimate=cost(loads[0].size * 40, 0),
        name="quad",
    )(*loads)


def entering_kernel(heads, dim, quad_size, before_ref, decay_ref, total_ref, *refs):
    refs, out_ref = refs[:-1], refs[-1]
    place = lax.div(lax.axis_index("tm"), quad_size)
    near = lax.rem(lax.axis_index("tm"), quad_size) < quad_size // 2
    near_refs, far_refs = refs[: len(refs) // 2], refs[len(refs) // 2 :]
    for h in range(heads):
        rows = slice(h * dim, (h + 1) * dim)
        loaded = [body_and_decay(total_ref, h, dim)]
        for near_ref, far_ref in zip(near_refs, far_refs):
            pair = zip(body_and_decay(near_ref, h, dim), body_and_decay(far_ref, h, dim))
            loaded.append([jnp.where(near, a, b) for a, b in pair])
        earlier = scanned(place, loaded)[0]
        out_ref[rows, :] = (before_ref[rows, :] + decay_ref[h : h + 1, :] * earlier).astype(BF16)


def entering(quad_size, before, decay, totals, heads, dim):
    return pl.pallas_call(
        functools.partial(entering_kernel, heads, dim, quad_size),
        in_specs=[VMEM] * (2 + len(totals)),
        out_specs=VMEM,
        out_shape=struct(before.shape),
        compiler_params=params(),
        cost_estimate=cost(before.size * 20, 0),
        name="entering",
    )(before, decay, *totals)


def recall_kernel(heads, dim, reading_ref, q_ref, local_ref, state_ref, out_ref):
    for h in range(heads):
        cols = slice(h * dim, (h + 1) * dim)
        recalled = dot(q_ref[:, cols], state_ref[cols, :]) * reading_ref[:, h : h + 1]
        out_ref[:, cols] = (local_ref[:, cols].astype(F32) + recalled).astype(BF16)


def recall(reading, q, local, state, heads, dim):
    return pl.pallas_call(
        functools.partial(recall_kernel, heads, dim),
        in_specs=[VMEM] * 4,
        out_specs=VMEM,
        out_shape=struct(q.shape),
        compiler_params=params(),
        cost_estimate=cost(4 * q.size * dim, 0),
        name="recall",
    )(reading, q, local, state)


def project_kernel(shards, own_ref, side_ref, own_w_ref, side_w_ref, *out_refs):
    width = out_refs[0].shape[1]
    own, side = own_ref[...], side_ref[...]
    for k in reversed(range(shards)):
        owner = lax.rem(lax.axis_index("head") + k, shards)
        cols = pl.ds(pl.multiple_of(owner * width, width), width)
        out = dot(own, own_w_ref[:, cols]) + dot(side, side_w_ref[:, cols])
        out_refs[k][...] = out.astype(out_refs[k].dtype)


def project(own, side, own_w, side_w, shards):
    rows = own.shape[0]
    width = own_w.shape[1] // shards
    return pl.pallas_call(
        functools.partial(project_kernel, shards),
        in_specs=[VMEM] * 4,
        out_specs=[VMEM] * shards,
        out_shape=[struct((rows, width))] * shards,
        compiler_params=params(),
        cost_estimate=cost(4 * rows * own_w.size, 0),
        name="project",
    )(own, side, own_w, side_w)


def finish_kernel(count, *refs):
    total = refs[0][...].astype(F32)
    for ref in refs[1:count]:
        total += ref[...].astype(F32)
    refs[-1][...] = total.astype(BF16)


def finish(parts, result, first, length):
    rows, width = parts[0].shape
    chunk = first // rows
    whole = pl.BlockSpec((rows, width), lambda i: (0, 0))
    more = [] if result is None else [result]
    return pl.pallas_call(
        functools.partial(finish_kernel, len(parts)),
        grid=(1,),
        in_specs=[whole] * len(parts) + [pl.BlockSpec(memory_space=pl.ANY)] * len(more),
        out_specs=pl.BlockSpec((rows, width), lambda i: (chunk, 0)),
        out_shape=struct((length, width)),
        input_output_aliases={len(parts): 0} if more else {},
        compiler_params=params(),
        cost_estimate=cost(rows * width * 2, rows * width * 6),
        name="finish",
    )(*parts, *more)


def per_device(
    residual_signal,
    prescale_amplifier,
    triple_projector,
    score_scaler,
    recall_retained_logshare,
    tile_retain_grid,
    recall_store_flags,
    emission_projector,
    sideways_coupling_coef,
):
    x = residual_signal[0]
    length = x.shape[0]
    sizes = [CHUNK] * (length // CHUNK - 1) + [LAST] * (CHUNK // LAST)
    firsts = [sum(sizes[:c]) for c in range(len(sizes))]
    chunks = len(sizes)
    shards = lax.axis_size("head")
    blocks = lax.axis_size("tm")
    heads = triple_projector.shape[2]
    dim = emission_projector.shape[2]
    swap_streams = [(0, 1), (1, 0)]
    tied = lambda *arrays: lax.optimization_barrier(arrays)

    own_w = emission_projector[0].reshape(heads * dim, -1)
    side_w = lax.ppermute(
        sideways_coupling_coef[0].reshape(heads * dim, -1), "stream", swap_streams
    )
    fade, tail, *readings = prepare(
        recall_retained_logshare[0],
        recall_store_flags,
        dim,
        1.0 / math.sqrt(dim * length * blocks),
        sizes,
    )
    pieces = [x[first : first + size] for first, size in zip(firsts, sizes)]
    received = []
    for c in range(chunks):
        if c == chunks - 2:
            pieces[c], pieces[c + 1], tail = tied(pieces[c], pieces[c + 1], tail)
        xs = [pieces[c]]
        for k in range(1, shards):
            xs.append(
                lax.ppermute(pieces[c], "head", [((d + k) % shards, d) for d in range(shards)])
            )
        received.append(xs)
    gain = prescale_amplifier
    w = triple_projector[0].reshape(-1, 3 * heads * dim)

    qs, ks, vs, locals_ = [], [], [], []
    summary = None
    for c, first in enumerate(firsts[:-1]):
        q, k, v, summary = qkv(gain, w, fade, summary, received[c], heads, dim, first)
        qs.append(q)
        ks.append(k)
        vs.append(v)
        if c < chunks - 2:
            local = attention(first, tile_retain_grid, score_scaler, q, ks, vs, heads, dim)
            summary, local = tied(summary, local)
            locals_.append(local)
    k, v, sent = last_keys_values(
        gain, w, fade, summary, tail, received[-1], heads, dim, firsts[-1]
    )
    ks.append(k)
    vs.append(v)

    quad_size = min(4, blocks)
    loads = [sent] + [
        lax.ppermute(sent, "tm", [(d, d ^ k) for d in range(blocks)]) for k in range(1, quad_size)
    ]
    qs.append(last_queries(gain, w, received[-1], heads, dim))
    for c in range(chunks - 2, chunks):
        locals_.append(
            attention(
                firsts[c], tile_retain_grid, score_scaler, qs[c], ks[: c + 1], vs[: c + 1], heads, dim
            )
        )
    *loads, locals_[-2] = tied(*loads, locals_[-2])
    before, decay, total = quad(loads, heads, dim)
    totals, half = [total], quad_size // 2
    for into in (0, half):
        for k in range(1, blocks // quad_size):
            pairs = {d: d for d in range(blocks)}
            for d in range(blocks):
                later = d ^ (quad_size * k)
                if d % quad_size >= half and later > d:
                    later += into - half
                    pairs[d], pairs[later] = later, d
            totals.append(lax.ppermute(total, "tm", list(pairs.items())))
    *totals, locals_[-1] = tied(*totals, locals_[-1])
    state = entering(quad_size, before, decay, totals, heads, dim)

    result = None
    for c in range(chunks):
        head_out = recall(readings[c], qs[c], locals_[c], state, heads, dim)
        side = lax.ppermute(head_out, "stream", swap_streams)
        outs = project(head_out, side, own_w, side_w, shards)
        parts = [outs[0]]
        for k in range(1, shards):
            parts.append(
                lax.ppermute(outs[k], "head", [(d, (d + k) % shards) for d in range(shards)])
            )
        result = finish(parts, result, firsts[c], length)
    return result[None]


def solution(mesh):
    placed = (
        P("stream", "tm", "head"),
        P("stream", None),
        P("stream", None, "head", None),
        P("stream", "head"),
        P("stream", "head", "tm"),
        P("tm", None),
        P("tm"),
        P("stream", "head", None, None),
        P("stream", "head", None, None),
    )
    return jax.shard_map(
        per_device, mesh=mesh, in_specs=placed, out_specs=P("stream", "tm", "head"), check_vma=False
    )
```

```python
import functools
import math

import jax
import jax.numpy as jnp
from jax import lax
from jax.experimental import pallas as pl
from jax.experimental.pallas import tpu as pltpu
from jax.sharding import PartitionSpec as P

BLOCK = 512
CHUNK = 256
LAST = 64
TAIL = 16
EPSILON = 1e-06
F32 = jnp.float32
BF16 = jnp.bfloat16
SMEM = pl.BlockSpec(memory_space=pltpu.SMEM)
VMEM = pl.BlockSpec(memory_space=pltpu.VMEM)


def params():
    return pltpu.CompilerParams(vmem_limit_bytes=16 * 1024 * 1024)


def cost(flops, bytes_accessed, transcendentals=0):
    return pl.CostEstimate(
        flops=int(flops), bytes_accessed=int(bytes_accessed), transcendentals=int(transcendentals)
    )


def struct(shape, dtype=BF16):
    return jax.ShapeDtypeStruct(shape, dtype)


def dot(a, b):
    return lax.dot_general(a, b, (((1,), (0,)), ((), ())), preferred_element_type=F32)


def dot_nt(a, b):
    return lax.dot_general(a, b, (((1,), (1,)), ((), ())), preferred_element_type=F32)


def dot_tn(a, b):
    return lax.dot_general(a, b, (((0,), (0,)), ((), ())), preferred_element_type=F32)


def unit(values):
    return values * lax.rsqrt(jnp.mean(values * values, axis=-1, keepdims=True) + EPSILON)


def prepare_kernel(heads, factor, logs_ref, flags_ref, fade_ref, tail_ref, *refs):
    reading_refs, rows_ref = refs[:-1], refs[-1]
    length = logs_ref.shape[1]
    rows_ref[...] = jnp.zeros_like(rows_ref)
    rows_ref[:heads, :] = logs_ref[...]
    running = rows_ref[...]
    place = lax.broadcasted_iota(jnp.int32, running.shape, 1)
    step = 1
    while step < length:
        running += jnp.where(place >= step, pltpu.roll(running, step, 1), 0.0)
        step *= 2
    last = running[:, length - 1 :]
    chosen = jnp.zeros_like(running)
    for block in range(length // BLOCK):
        inside = (place >= block * BLOCK) & (place < (block + 1) * BLOCK)
        chosen = jnp.where(inside, flags_ref[block].astype(F32), chosen)
    fade_ref[...] = jnp.transpose(jnp.exp(last - running) * chosen)
    reading = jnp.transpose(jnp.exp(running) * factor)
    first = 0
    for ref in reading_refs:
        ref[...] = reading[first : first + ref.shape[0]]
        first += ref.shape[0]
    decay = jnp.exp(last)
    high = decay.astype(BF16).astype(F32)
    both = jnp.concatenate([high, decay - high], axis=0)
    tail_ref[...] = jnp.broadcast_to(both, tail_ref.shape).astype(BF16)


def prepare(logs, flags, dim, factor, sizes):
    heads, length = logs.shape
    lines = TAIL // 2
    return pl.pallas_call(
        functools.partial(prepare_kernel, heads, factor),
        in_specs=[VMEM, SMEM],
        out_specs=[VMEM] * (2 + len(sizes)),
        out_shape=[struct((length, lines), F32), struct((TAIL, dim))]
        + [struct((size, lines), F32) for size in sizes],
        scratch_shapes=[pltpu.VMEM((lines, length), F32)],
        compiler_params=params(),
        cost_estimate=cost(40 * lines * length, 0),
        name="prepare",
    )(logs, flags)


def normed_parts(gain_ref, x_refs):
    me = lax.axis_index("head")
    shards, width = len(x_refs), x_refs[0].shape[1]
    parts = [x[...].astype(F32) for x in x_refs]
    squares = sum(jnp.sum(p * p, axis=-1, keepdims=True) for p in parts)
    scale = lax.rsqrt(squares * (1.0 / (width * shards)) + EPSILON)
    out = []
    for k, part in enumerate(parts):
        owner = lax.rem(me + k, shards)
        rows = pl.ds(pl.multiple_of(owner * width, width), width)
        out.append(((part * scale * gain_ref[:, rows]).astype(BF16), rows))
    return out


def projected(parts, w_ref, cols):
    total = None
    for part, rows in parts:
        term = dot(part, w_ref[rows, cols])
        total = term if total is None else total + term
    return total


def add_summary(sum_ref, h, key, value, fade_ref, first):
    fade = fade_ref[first : first + key.shape[0], h : h + 1]
    sum_ref[h] += dot_tn((key.astype(F32) * fade).astype(BF16), value)


def qkv_kernel(heads, dim, first, gain_ref, w_ref, fade_ref, *refs):
    refs, (q_ref, k_ref, v_ref, sum_ref) = refs[:-4], refs[-4:]
    if first == 0:
        sum_ref[...] = jnp.zeros_like(sum_ref)
        x_refs = refs
    else:
        sum_ref[...] = refs[0][...]
        x_refs = refs[1:]
    parts = normed_parts(gain_ref, x_refs)
    wide = heads * dim
    thirds = [projected(parts, w_ref, slice(i * wide, (i + 1) * wide)) for i in range(3)]
    taken = lambda at: thirds[at * dim // wide][:, at * dim % wide : at * dim % wide + dim]
    for h in range(heads):
        cols = slice(h * dim, (h + 1) * dim)
        q_ref[:, cols] = unit(taken(3 * h)).astype(BF16)
        key = unit(taken(3 * h + 1)).astype(BF16)
        value = taken(3 * h + 2).astype(BF16)
        k_ref[:, cols] = key
        v_ref[:, cols] = value
        add_summary(sum_ref, h, key, value, fade_ref, first)


def qkv(gain, w, fade, prev, xs, heads, dim, first):
    rows = xs[0].shape[0]
    before = [prev] if first else []
    return pl.pallas_call(
        functools.partial(qkv_kernel, heads, dim, first),
        in_specs=[VMEM] * (3 + len(before) + len(xs)),
        out_specs=[VMEM] * 4,
        out_shape=[struct((rows, heads * dim))] * 3 + [struct((heads, dim, dim), F32)],
        compiler_params=params(),
        cost_estimate=cost(4 * rows * w.size, 0),
        name="qkv",
    )(gain, w, fade, *before, *xs)


def last_kernel(heads, dim, first, gain_ref, w_ref, fade_ref, prev_ref, tail_ref, *refs):
    x_refs, (k_ref, v_ref, send_ref, sum_ref) = refs[:-4], refs[-4:]
    sum_ref[...] = prev_ref[...]
    parts = normed_parts(gain_ref, x_refs)
    pairs = [
        projected(parts, w_ref, slice((3 * h + 1) * dim, (3 * h + 3) * dim)) for h in range(heads)
    ]
    for h in range(heads):
        cols = slice(h * dim, (h + 1) * dim)
        key = unit(pairs[h][:, :dim]).astype(BF16)
        value = pairs[h][:, dim:].astype(BF16)
        k_ref[:, cols] = key
        v_ref[:, cols] = value
        add_summary(sum_ref, h, key, value, fade_ref, first)
        send_ref[cols, :] = sum_ref[h].astype(BF16)
    send_ref[heads * dim :, :] = tail_ref[...]


def last_keys_values(gain, w, fade, prev, tail, xs, heads, dim, first):
    rows = xs[0].shape[0]
    return pl.pallas_call(
        functools.partial(last_kernel, heads, dim, first),
        in_specs=[VMEM] * (5 + len(xs)),
        out_specs=[VMEM] * 3,
        out_shape=[struct((rows, heads * dim))] * 2 + [struct((heads * dim + TAIL, dim))],
        scratch_shapes=[pltpu.VMEM((heads, dim, dim), F32)],
        compiler_params=params(),
        cost_estimate=cost(3 * rows * w.size, 0),
        name="last_keys_values",
    )(gain, w, fade, prev, tail, *xs)


def queries_kernel(heads, dim, gain_ref, w_ref, *refs):
    q_ref = refs[-1]
    parts = normed_parts(gain_ref, refs[:-1])
    for h in range(heads):
        base = 3 * h * dim
        cols = slice(h * dim, (h + 1) * dim)
        q_ref[:, cols] = unit(projected(parts, w_ref, slice(base, base + dim))).astype(BF16)


def last_queries(gain, w, xs, heads, dim):
    rows = xs[0].shape[0]
    return pl.pallas_call(
        functools.partial(queries_kernel, heads, dim),
        in_specs=[VMEM] * (2 + len(xs)),
        out_specs=VMEM,
        out_shape=struct((rows, heads * dim)),
        compiler_params=params(),
        cost_estimate=cost(2 * rows * w.size, 0),
        name="last_queries",
    )(gain, w, *xs)


def attention_kernel(first, heads, dim, keep_ref, scale_ref, q_ref, *refs):
    count = len(refs) // 2
    k_refs, v_refs, out_ref = refs[:count], refs[count:-1], refs[-1]
    rows = q_ref.shape[0]
    block = first // BLOCK
    causal = lax.broadcasted_iota(jnp.int32, (rows, rows), 1) <= lax.broadcasted_iota(
        jnp.int32, (rows, rows), 0
    )
    for h in range(heads):
        cols = slice(h * dim, (h + 1) * dim)
        query = q_ref[:, cols]
        scale = scale_ref[0, h] * (1.0 / math.sqrt(dim))
        total, at = None, 0
        for j in range(count):
            keys = k_refs[j].shape[0]
            powers = jnp.exp(dot_nt(query, k_refs[j][:, cols]) * scale)
            if at == first:
                powers = jnp.where(causal, powers, 0.0)
            ones = jnp.ones((keys, dim), BF16)
            part = dot(powers.astype(BF16), jnp.concatenate([v_refs[j][:, cols], ones], axis=1))
            if at // BLOCK < block:
                part = jnp.where(keep_ref[block, at // BLOCK] == 1, part, 0.0)
            total = part if total is None else total + part
            at += keys
        out_ref[:, cols] = (total[:, :dim] / total[:, dim:]).astype(BF16)


def attention(first, keep, scale, q, ks, vs, heads, dim):
    rows = q.shape[0]
    return pl.pallas_call(
        functools.partial(attention_kernel, first, heads, dim),
        in_specs=[SMEM, SMEM] + [VMEM] * (1 + len(ks) + len(vs)),
        out_specs=VMEM,
        out_shape=struct(q.shape),
        compiler_params=params(),
        cost_estimate=cost(
            heads * 8 * rows * (first + rows) * dim, 0, heads * rows * (first + rows)
        ),
        name="attention",
    )(keep, scale, q, *ks, *vs)


def body_and_decay(ref, h, dim):
    size = ref.shape[0] - TAIL
    high = ref[size + h : size + h + 1, :].astype(F32)
    low = ref[size + TAIL // 2 + h : size + TAIL // 2 + h + 1, :].astype(F32)
    return ref[h * dim : (h + 1) * dim, :].astype(F32), high + low


def scanned(place, refs, h, dim):
    count = len(refs)
    loaded = [body_and_decay(ref, h, dim) for ref in refs]
    state, since = jnp.zeros((dim, refs[0].shape[1]), F32), jnp.ones((1, refs[0].shape[1]), F32)
    before, before_decay = state, since
    for j in range(count):
        before = jnp.where(place == j, state, before)
        before_decay = jnp.where(place == j, since, before_decay)
        body, decay = loaded[0]
        for k in range(1, count):
            here = place == (j ^ k)
            body = jnp.where(here, loaded[k][0], body)
            decay = jnp.where(here, loaded[k][1], decay)
        state = decay * state + body
        since = since * decay
    return before, before_decay, state, since


def quad_kernel(heads, dim, *refs):
    place = lax.rem(lax.axis_index("tm"), len(refs) - 3)
    refs, (before_ref, decay_ref, total_ref) = refs[:-3], refs[-3:]
    size = heads * dim
    total_ref[size:, :] = jnp.zeros((TAIL, total_ref.shape[1]), BF16)
    for h in range(heads):
        rows = slice(h * dim, (h + 1) * dim)
        before, before_decay, state, since = scanned(place, refs, h, dim)
        before_ref[rows, :] = before
        decay_ref[h : h + 1, :] = before_decay
        total_ref[rows, :] = state.astype(BF16)
        high = since.astype(BF16)
        total_ref[size + h : size + h + 1, :] = high
        low = (since - high.astype(F32)).astype(BF16)
        total_ref[size + TAIL // 2 + h : size + TAIL // 2 + h + 1, :] = low


def quad(loads, heads, dim):
    shape = loads[0].shape
    return pl.pallas_call(
        functools.partial(quad_kernel, heads, dim),
        in_specs=[VMEM] * len(loads),
        out_specs=[VMEM] * 3,
        out_shape=[
            struct((heads * dim, shape[1]), F32),
            struct((TAIL // 2, shape[1]), F32),
            struct(shape),
        ],
        compiler_params=params(),
        cost_estimate=cost(loads[0].size * 40, 0),
        name="quad",
    )(*loads)


def entering_kernel(heads, dim, before_ref, decay_ref, *refs):
    refs, out_ref = refs[:-1], refs[-1]
    for h in range(heads):
        rows = slice(h * dim, (h + 1) * dim)
        earlier = jnp.zeros((dim, out_ref.shape[1]), F32)
        for ref in reversed(refs):
            body, decay = body_and_decay(ref, h, dim)
            earlier = body + decay * earlier
        out_ref[rows, :] = (before_ref[rows, :] + decay_ref[h : h + 1, :] * earlier).astype(BF16)


def entering(before, decay, totals, heads, dim):
    return pl.pallas_call(
        functools.partial(entering_kernel, heads, dim),
        in_specs=[VMEM] * (2 + len(totals)),
        out_specs=VMEM,
        out_shape=struct(before.shape),
        compiler_params=params(),
        cost_estimate=cost(before.size * 20, 0),
        name="entering",
    )(before, decay, *totals)


def recall_kernel(heads, dim, reading_ref, q_ref, local_ref, state_ref, out_ref):
    for h in range(heads):
        cols = slice(h * dim, (h + 1) * dim)
        recalled = dot(q_ref[:, cols], state_ref[cols, :]) * reading_ref[:, h : h + 1]
        out_ref[:, cols] = (local_ref[:, cols].astype(F32) + recalled).astype(BF16)


def recall(reading, q, local, state, heads, dim):
    return pl.pallas_call(
        functools.partial(recall_kernel, heads, dim),
        in_specs=[VMEM] * 4,
        out_specs=VMEM,
        out_shape=struct(q.shape),
        compiler_params=params(),
        cost_estimate=cost(4 * q.size * dim, 0),
        name="recall",
    )(reading, q, local, state)


def project_kernel(shards, own_ref, side_ref, own_w_ref, side_w_ref, *out_refs):
    width = out_refs[0].shape[1]
    own, side = own_ref[...], side_ref[...]
    for k in reversed(range(shards)):
        owner = lax.rem(lax.axis_index("head") + k, shards)
        cols = pl.ds(pl.multiple_of(owner * width, width), width)
        out = dot(own, own_w_ref[:, cols]) + dot(side, side_w_ref[:, cols])
        out_refs[k][...] = out.astype(out_refs[k].dtype)


def project(own, side, own_w, side_w, shards):
    rows = own.shape[0]
    width = own_w.shape[1] // shards
    return pl.pallas_call(
        functools.partial(project_kernel, shards),
        in_specs=[VMEM] * 4,
        out_specs=[VMEM] * shards,
        out_shape=[struct((rows, width))] * shards,
        compiler_params=params(),
        cost_estimate=cost(4 * rows * own_w.size, 0),
        name="project",
    )(own, side, own_w, side_w)


def finish_kernel(count, *refs):
    total = refs[0][...].astype(F32)
    for ref in refs[1:count]:
        total += ref[...].astype(F32)
    refs[-1][...] = total.astype(BF16)


def finish(parts, result, first, length):
    rows, width = parts[0].shape
    chunk = first // rows
    whole = pl.BlockSpec((rows, width), lambda i: (0, 0))
    more = [] if result is None else [result]
    return pl.pallas_call(
        functools.partial(finish_kernel, len(parts)),
        grid=(1,),
        in_specs=[whole] * len(parts) + [pl.BlockSpec(memory_space=pl.ANY)] * len(more),
        out_specs=pl.BlockSpec((rows, width), lambda i: (chunk, 0)),
        out_shape=struct((length, width)),
        input_output_aliases={len(parts): 0} if more else {},
        compiler_params=params(),
        cost_estimate=cost(rows * width * 2, rows * width * 6),
        name="finish",
    )(*parts, *more)


def per_device(
    residual_signal,
    prescale_amplifier,
    triple_projector,
    score_scaler,
    recall_retained_logshare,
    tile_retain_grid,
    recall_store_flags,
    emission_projector,
    sideways_coupling_coef,
):
    x = residual_signal[0]
    length = x.shape[0]
    sizes = [CHUNK] * (length // CHUNK - 1) + [CHUNK - LAST, LAST]
    firsts = [sum(sizes[:c]) for c in range(len(sizes))]
    chunks = len(sizes)
    shards = lax.axis_size("head")
    blocks = lax.axis_size("tm")
    heads = triple_projector.shape[2]
    dim = emission_projector.shape[2]
    swap_streams = [(0, 1), (1, 0)]
    tied = lambda *arrays: lax.optimization_barrier(arrays)

    own_w = emission_projector[0].reshape(heads * dim, -1)
    side_w = lax.ppermute(
        sideways_coupling_coef[0].reshape(heads * dim, -1), "stream", swap_streams
    )
    fade, tail, *readings = prepare(
        recall_retained_logshare[0],
        recall_store_flags,
        dim,
        1.0 / math.sqrt(dim * length * blocks),
        sizes,
    )
    pieces = [x[first : first + size] for first, size in zip(firsts, sizes)]
    received = []
    for c in range(chunks):
        if c == chunks - 2:
            pieces[c], pieces[c + 1], tail = tied(pieces[c], pieces[c + 1], tail)
        xs = [pieces[c]]
        for k in range(1, shards):
            xs.append(
                lax.ppermute(pieces[c], "head", [((d + k) % shards, d) for d in range(shards)])
            )
        received.append(xs)
    gain = prescale_amplifier
    w = triple_projector[0].reshape(-1, 3 * heads * dim)

    qs, ks, vs, locals_ = [], [], [], []
    summary = None
    for c, first in enumerate(firsts[:-1]):
        q, k, v, summary = qkv(gain, w, fade, summary, received[c], heads, dim, first)
        qs.append(q)
        ks.append(k)
        vs.append(v)
        if c < chunks - 2:
            local = attention(first, tile_retain_grid, score_scaler, q, ks, vs, heads, dim)
            summary, local = tied(summary, local)
            locals_.append(local)
    k, v, sent = last_keys_values(
        gain, w, fade, summary, tail, received[-1], heads, dim, firsts[-1]
    )
    ks.append(k)
    vs.append(v)

    quad_size = min(4, blocks)
    loads = [sent] + [
        lax.ppermute(sent, "tm", [(d, d ^ k) for d in range(blocks)]) for k in range(1, quad_size)
    ]
    qs.append(last_queries(gain, w, received[-1], heads, dim))
    for c in range(chunks - 2, chunks):
        locals_.append(
            attention(
                firsts[c], tile_retain_grid, score_scaler, qs[c], ks[: c + 1], vs[: c + 1], heads, dim
            )
        )
    *loads, locals_[-2] = tied(*loads, locals_[-2])
    before, decay, total = quad(loads, heads, dim)
    totals = [
        lax.ppermute(total, "tm", [(d, d + quad_size * k) for d in range(blocks - quad_size * k)])
        for k in range(1, blocks // quad_size)
    ]
    *totals, locals_[-1] = tied(*totals, locals_[-1])
    state = entering(before, decay, totals, heads, dim)

    result = None
    for c in range(chunks):
        head_out = recall(readings[c], qs[c], locals_[c], state, heads, dim)
        side = lax.ppermute(head_out, "stream", swap_streams)
        outs = project(head_out, side, own_w, side_w, shards)
        parts = [outs[0]]
        for k in range(1, shards):
            parts.append(
                lax.ppermute(outs[k], "head", [(d, (d + k) % shards) for d in range(shards)])
            )
        result = finish(parts, result, firsts[c], length)
    return result[None]


def solution(mesh):
    placed = (
        P("stream", "tm", "head"),
        P("stream", None),
        P("stream", None, "head", None),
        P("stream", "head"),
        P("stream", "head", "tm"),
        P("tm", None),
        P("tm"),
        P("stream", "head", None, None),
        P("stream", "head", None, None),
    )
    return jax.shard_map(
        per_device, mesh=mesh, in_specs=placed, out_specs=P("stream", "tm", "head"), check_vma=False
    )
```

```python
import functools
import math

import jax
import jax.numpy as jnp
from jax import lax
from jax.experimental import pallas as pl
from jax.experimental.pallas import tpu as pltpu
from jax.sharding import PartitionSpec as P

BLOCK = 512
CHUNK = 256
LAST = 64
TAIL = 16
EPSILON = 1e-06
F32 = jnp.float32
BF16 = jnp.bfloat16
SMEM = pl.BlockSpec(memory_space=pltpu.SMEM)
VMEM = pl.BlockSpec(memory_space=pltpu.VMEM)


def params():
    return pltpu.CompilerParams(vmem_limit_bytes=16 * 1024 * 1024)


def cost(flops, bytes_accessed, transcendentals=0):
    return pl.CostEstimate(
        flops=int(flops), bytes_accessed=int(bytes_accessed), transcendentals=int(transcendentals)
    )


def struct(shape, dtype=BF16):
    return jax.ShapeDtypeStruct(shape, dtype)


def dot(a, b):
    return lax.dot_general(a, b, (((1,), (0,)), ((), ())), preferred_element_type=F32)


def dot_nt(a, b):
    return lax.dot_general(a, b, (((1,), (1,)), ((), ())), preferred_element_type=F32)


def dot_tn(a, b):
    return lax.dot_general(a, b, (((0,), (0,)), ((), ())), preferred_element_type=F32)


def unit(values):
    return values * lax.rsqrt(jnp.mean(values * values, axis=-1, keepdims=True) + EPSILON)


def prepare_kernel(heads, factor, logs_ref, flags_ref, fade_ref, tail_ref, *refs):
    reading_refs, rows_ref = refs[:-1], refs[-1]
    length = logs_ref.shape[1]
    rows_ref[...] = jnp.zeros_like(rows_ref)
    rows_ref[:heads, :] = logs_ref[...]
    running = rows_ref[...]
    place = lax.broadcasted_iota(jnp.int32, running.shape, 1)
    step = 1
    while step < length:
        running += jnp.where(place >= step, pltpu.roll(running, step, 1), 0.0)
        step *= 2
    last = running[:, length - 1 :]
    chosen = jnp.zeros_like(running)
    for block in range(length // BLOCK):
        inside = (place >= block * BLOCK) & (place < (block + 1) * BLOCK)
        chosen = jnp.where(inside, flags_ref[block].astype(F32), chosen)
    fade_ref[...] = jnp.transpose(jnp.exp(last - running) * chosen)
    reading = jnp.transpose(jnp.exp(running) * factor)
    first = 0
    for ref in reading_refs:
        ref[...] = reading[first : first + ref.shape[0]]
        first += ref.shape[0]
    decay = jnp.exp(last)
    high = decay.astype(BF16).astype(F32)
    both = jnp.concatenate([high, decay - high], axis=0)
    tail_ref[...] = jnp.broadcast_to(both, tail_ref.shape).astype(BF16)


def prepare(logs, flags, dim, factor, sizes):
    heads, length = logs.shape
    lines = TAIL // 2
    return pl.pallas_call(
        functools.partial(prepare_kernel, heads, factor),
        in_specs=[VMEM, SMEM],
        out_specs=[VMEM] * (2 + len(sizes)),
        out_shape=[struct((length, lines), F32), struct((TAIL, dim))]
        + [struct((size, lines), F32) for size in sizes],
        scratch_shapes=[pltpu.VMEM((lines, length), F32)],
        compiler_params=params(),
        cost_estimate=cost(40 * lines * length, 0),
        name="prepare",
    )(logs, flags)


def normed_parts(gain_ref, x_refs):
    me = lax.axis_index("head")
    shards, width = len(x_refs), x_refs[0].shape[1]
    parts = [x[...].astype(F32) for x in x_refs]
    squares = sum(jnp.sum(p * p, axis=-1, keepdims=True) for p in parts)
    scale = lax.rsqrt(squares * (1.0 / (width * shards)) + EPSILON)
    out = []
    for k, part in enumerate(parts):
        owner = lax.rem(me + k, shards)
        rows = pl.ds(pl.multiple_of(owner * width, width), width)
        out.append(((part * scale * gain_ref[:, rows]).astype(BF16), rows))
    return out


def projected(parts, w_ref, cols):
    total = None
    for part, rows in parts:
        term = dot(part, w_ref[rows, cols])
        total = term if total is None else total + term
    return total


def add_summary(sum_ref, h, key, value, fade_ref, first):
    fade = fade_ref[first : first + key.shape[0], h : h + 1]
    sum_ref[h] += dot_tn((key.astype(F32) * fade).astype(BF16), value)


def qkv_kernel(heads, dim, first, gain_ref, w_ref, fade_ref, *refs):
    refs, (q_ref, k_ref, v_ref, sum_ref) = refs[:-4], refs[-4:]
    if first == 0:
        sum_ref[...] = jnp.zeros_like(sum_ref)
        x_refs = refs
    else:
        sum_ref[...] = refs[0][...]
        x_refs = refs[1:]
    parts = normed_parts(gain_ref, x_refs)
    wide = heads * dim
    thirds = [projected(parts, w_ref, slice(i * wide, (i + 1) * wide)) for i in range(3)]
    taken = lambda at: thirds[at * dim // wide][:, at * dim % wide : at * dim % wide + dim]
    for h in range(heads):
        cols = slice(h * dim, (h + 1) * dim)
        q_ref[:, cols] = unit(taken(3 * h)).astype(BF16)
        key = unit(taken(3 * h + 1)).astype(BF16)
        value = taken(3 * h + 2).astype(BF16)
        k_ref[:, cols] = key
        v_ref[:, cols] = value
        add_summary(sum_ref, h, key, value, fade_ref, first)


def qkv(gain, w, fade, prev, xs, heads, dim, first):
    rows = xs[0].shape[0]
    before = [prev] if first else []
    return pl.pallas_call(
        functools.partial(qkv_kernel, heads, dim, first),
        in_specs=[VMEM] * (3 + len(before) + len(xs)),
        out_specs=[VMEM] * 4,
        out_shape=[struct((rows, heads * dim))] * 3 + [struct((heads, dim, dim), F32)],
        compiler_params=params(),
        cost_estimate=cost(4 * rows * w.size, 0),
        name="qkv",
    )(gain, w, fade, *before, *xs)


def own_part_kernel(heads, dim, gain_ref, w_ref, x_ref, out_ref):
    width = x_ref.shape[1]
    rows = pl.ds(pl.multiple_of(lax.axis_index("head") * width, width), width)
    part = (x_ref[...].astype(F32) * gain_ref[:, rows]).astype(BF16)
    for h in range(heads):
        cols = slice((3 * h + 1) * dim, (3 * h + 3) * dim)
        out_ref[:, 2 * h * dim : 2 * (h + 1) * dim] = dot(part, w_ref[rows, cols])


def own_part(gain, w, x, heads, dim):
    return pl.pallas_call(
        functools.partial(own_part_kernel, heads, dim),
        in_specs=[VMEM] * 3,
        out_specs=VMEM,
        out_shape=struct((x.shape[0], 2 * heads * dim), F32),
        compiler_params=params(),
        cost_estimate=cost(x.shape[0] * w.size, 0),
        name="own_part",
    )(gain, w, x)


def last_kernel(heads, dim, first, acc_ref, gain_ref, w_ref, fade_ref, prev_ref, tail_ref, *refs):
    x_refs, (k_ref, v_ref, send_ref, sum_ref) = refs[:-4], refs[-4:]
    sum_ref[...] = prev_ref[...]
    shards, width = len(x_refs), x_refs[0].shape[1]
    xs = [x[...].astype(F32) for x in x_refs]
    squares = sum(jnp.sum(x * x, axis=-1, keepdims=True) for x in xs)
    scale = lax.rsqrt(squares * (1.0 / (width * shards)) + EPSILON)
    parts = []
    for k in range(1, shards):
        owner = lax.rem(lax.axis_index("head") + k, shards)
        span = pl.ds(pl.multiple_of(owner * width, width), width)
        parts.append(((xs[k] * gain_ref[:, span]).astype(BF16), span))
    pairs = []
    for h in range(heads):
        total = acc_ref[:, 2 * h * dim : 2 * (h + 1) * dim]
        if parts:
            total += projected(parts, w_ref, slice((3 * h + 1) * dim, (3 * h + 3) * dim))
        pairs.append(total * scale)
    for h in range(heads):
        cols = slice(h * dim, (h + 1) * dim)
        key = unit(pairs[h][:, :dim]).astype(BF16)
        value = pairs[h][:, dim:].astype(BF16)
        k_ref[:, cols] = key
        v_ref[:, cols] = value
        add_summary(sum_ref, h, key, value, fade_ref, first)
        send_ref[cols, :] = sum_ref[h].astype(BF16)
    send_ref[heads * dim :, :] = tail_ref[...]


def last_keys_values(acc, gain, w, fade, prev, tail, xs, heads, dim, first):
    rows = xs[0].shape[0]
    return pl.pallas_call(
        functools.partial(last_kernel, heads, dim, first),
        in_specs=[VMEM] * (6 + len(xs)),
        out_specs=[VMEM] * 3,
        out_shape=[struct((rows, heads * dim))] * 2 + [struct((heads * dim + TAIL, dim))],
        scratch_shapes=[pltpu.VMEM((heads, dim, dim), F32)],
        compiler_params=params(),
        cost_estimate=cost(3 * rows * w.size, 0),
        name="last_keys_values",
    )(acc, gain, w, fade, prev, tail, *xs)


def queries_kernel(heads, dim, gain_ref, w_ref, *refs):
    q_ref = refs[-1]
    parts = normed_parts(gain_ref, refs[:-1])
    for h in range(heads):
        base = 3 * h * dim
        cols = slice(h * dim, (h + 1) * dim)
        q_ref[:, cols] = unit(projected(parts, w_ref, slice(base, base + dim))).astype(BF16)


def last_queries(gain, w, xs, heads, dim):
    rows = xs[0].shape[0]
    return pl.pallas_call(
        functools.partial(queries_kernel, heads, dim),
        in_specs=[VMEM] * (2 + len(xs)),
        out_specs=VMEM,
        out_shape=struct((rows, heads * dim)),
        compiler_params=params(),
        cost_estimate=cost(2 * rows * w.size, 0),
        name="last_queries",
    )(gain, w, *xs)


def attention_kernel(first, heads, dim, keep_ref, scale_ref, q_ref, *refs):
    count = len(refs) // 2
    k_refs, v_refs, out_ref = refs[:count], refs[count:-1], refs[-1]
    rows = q_ref.shape[0]
    block = first // BLOCK
    causal = lax.broadcasted_iota(jnp.int32, (rows, rows), 1) <= lax.broadcasted_iota(
        jnp.int32, (rows, rows), 0
    )
    for h in range(heads):
        cols = slice(h * dim, (h + 1) * dim)
        query = q_ref[:, cols]
        scale = scale_ref[0, h] * (1.0 / math.sqrt(dim))
        total, at = None, 0
        for j in range(count):
            keys = k_refs[j].shape[0]
            powers = jnp.exp(dot_nt(query, k_refs[j][:, cols]) * scale)
            if at == first:
                powers = jnp.where(causal, powers, 0.0)
            ones = jnp.ones((keys, dim), BF16)
            part = dot(powers.astype(BF16), jnp.concatenate([v_refs[j][:, cols], ones], axis=1))
            if at // BLOCK < block:
                part = jnp.where(keep_ref[block, at // BLOCK] == 1, part, 0.0)
            total = part if total is None else total + part
            at += keys
        out_ref[:, cols] = (total[:, :dim] / total[:, dim:]).astype(BF16)


def attention(first, keep, scale, q, ks, vs, heads, dim):
    rows = q.shape[0]
    return pl.pallas_call(
        functools.partial(attention_kernel, first, heads, dim),
        in_specs=[SMEM, SMEM] + [VMEM] * (1 + len(ks) + len(vs)),
        out_specs=VMEM,
        out_shape=struct(q.shape),
        compiler_params=params(),
        cost_estimate=cost(
            heads * 8 * rows * (first + rows) * dim, 0, heads * rows * (first + rows)
        ),
        name="attention",
    )(keep, scale, q, *ks, *vs)


def body_and_decay(ref, h, dim):
    size = ref.shape[0] - TAIL
    high = ref[size + h : size + h + 1, :].astype(F32)
    low = ref[size + TAIL // 2 + h : size + TAIL // 2 + h + 1, :].astype(F32)
    return ref[h * dim : (h + 1) * dim, :].astype(F32), high + low


def scanned(place, refs, h, dim):
    count = len(refs)
    loaded = [body_and_decay(ref, h, dim) for ref in refs]
    state, since = jnp.zeros((dim, refs[0].shape[1]), F32), jnp.ones((1, refs[0].shape[1]), F32)
    before, before_decay = state, since
    for j in range(count):
        before = jnp.where(place == j, state, before)
        before_decay = jnp.where(place == j, since, before_decay)
        body, decay = loaded[0]
        for k in range(1, count):
            here = place == (j ^ k)
            body = jnp.where(here, loaded[k][0], body)
            decay = jnp.where(here, loaded[k][1], decay)
        state = decay * state + body
        since = since * decay
    return before, before_decay, state, since


def quad_kernel(heads, dim, *refs):
    place = lax.rem(lax.axis_index("tm"), len(refs) - 3)
    refs, (before_ref, decay_ref, total_ref) = refs[:-3], refs[-3:]
    size = heads * dim
    total_ref[size:, :] = jnp.zeros((TAIL, total_ref.shape[1]), BF16)
    for h in range(heads):
        rows = slice(h * dim, (h + 1) * dim)
        before, before_decay, state, since = scanned(place, refs, h, dim)
        before_ref[rows, :] = before
        decay_ref[h : h + 1, :] = before_decay
        total_ref[rows, :] = state.astype(BF16)
        high = since.astype(BF16)
        total_ref[size + h : size + h + 1, :] = high
        low = (since - high.astype(F32)).astype(BF16)
        total_ref[size + TAIL // 2 + h : size + TAIL // 2 + h + 1, :] = low


def quad(loads, heads, dim):
    shape = loads[0].shape
    return pl.pallas_call(
        functools.partial(quad_kernel, heads, dim),
        in_specs=[VMEM] * len(loads),
        out_specs=[VMEM] * 3,
        out_shape=[
            struct((heads * dim, shape[1]), F32),
            struct((TAIL // 2, shape[1]), F32),
            struct(shape),
        ],
        compiler_params=params(),
        cost_estimate=cost(loads[0].size * 40, 0),
        name="quad",
    )(*loads)


def entering_kernel(heads, dim, before_ref, decay_ref, *refs):
    refs, out_ref = refs[:-1], refs[-1]
    for h in range(heads):
        rows = slice(h * dim, (h + 1) * dim)
        earlier = jnp.zeros((dim, out_ref.shape[1]), F32)
        for ref in reversed(refs):
            body, decay = body_and_decay(ref, h, dim)
            earlier = body + decay * earlier
        out_ref[rows, :] = (before_ref[rows, :] + decay_ref[h : h + 1, :] * earlier).astype(BF16)


def entering(before, decay, totals, heads, dim):
    return pl.pallas_call(
        functools.partial(entering_kernel, heads, dim),
        in_specs=[VMEM] * (2 + len(totals)),
        out_specs=VMEM,
        out_shape=struct(before.shape),
        compiler_params=params(),
        cost_estimate=cost(before.size * 20, 0),
        name="entering",
    )(before, decay, *totals)


def recall_kernel(heads, dim, reading_ref, q_ref, local_ref, state_ref, out_ref):
    for h in range(heads):
        cols = slice(h * dim, (h + 1) * dim)
        recalled = dot(q_ref[:, cols], state_ref[cols, :]) * reading_ref[:, h : h + 1]
        out_ref[:, cols] = (local_ref[:, cols].astype(F32) + recalled).astype(BF16)


def recall(reading, q, local, state, heads, dim):
    return pl.pallas_call(
        functools.partial(recall_kernel, heads, dim),
        in_specs=[VMEM] * 4,
        out_specs=VMEM,
        out_shape=struct(q.shape),
        compiler_params=params(),
        cost_estimate=cost(4 * q.size * dim, 0),
        name="recall",
    )(reading, q, local, state)


def project_kernel(shards, own_ref, side_ref, own_w_ref, side_w_ref, *out_refs):
    width = out_refs[0].shape[1]
    own, side = own_ref[...], side_ref[...]
    for k in reversed(range(shards)):
        owner = lax.rem(lax.axis_index("head") + k, shards)
        cols = pl.ds(pl.multiple_of(owner * width, width), width)
        out = dot(own, own_w_ref[:, cols]) + dot(side, side_w_ref[:, cols])
        out_refs[k][...] = out.astype(out_refs[k].dtype)


def project(own, side, own_w, side_w, shards):
    rows = own.shape[0]
    width = own_w.shape[1] // shards
    return pl.pallas_call(
        functools.partial(project_kernel, shards),
        in_specs=[VMEM] * 4,
        out_specs=[VMEM] * shards,
        out_shape=[struct((rows, width))] * shards,
        compiler_params=params(),
        cost_estimate=cost(4 * rows * own_w.size, 0),
        name="project",
    )(own, side, own_w, side_w)


def finish_kernel(count, *refs):
    total = refs[0][...].astype(F32)
    for ref in refs[1:count]:
        total += ref[...].astype(F32)
    refs[-1][...] = total.astype(BF16)


def finish(parts, result, first, length):
    rows, width = parts[0].shape
    chunk = first // rows
    whole = pl.BlockSpec((rows, width), lambda i: (0, 0))
    more = [] if result is None else [result]
    return pl.pallas_call(
        functools.partial(finish_kernel, len(parts)),
        grid=(1,),
        in_specs=[whole] * len(parts) + [pl.BlockSpec(memory_space=pl.ANY)] * len(more),
        out_specs=pl.BlockSpec((rows, width), lambda i: (chunk, 0)),
        out_shape=struct((length, width)),
        input_output_aliases={len(parts): 0} if more else {},
        compiler_params=params(),
        cost_estimate=cost(rows * width * 2, rows * width * 6),
        name="finish",
    )(*parts, *more)


def per_device(
    residual_signal,
    prescale_amplifier,
    triple_projector,
    score_scaler,
    recall_retained_logshare,
    tile_retain_grid,
    recall_store_flags,
    emission_projector,
    sideways_coupling_coef,
):
    x = residual_signal[0]
    length = x.shape[0]
    sizes = [CHUNK] * (length // CHUNK - 1) + [CHUNK - LAST, LAST]
    firsts = [sum(sizes[:c]) for c in range(len(sizes))]
    chunks = len(sizes)
    shards = lax.axis_size("head")
    blocks = lax.axis_size("tm")
    heads = triple_projector.shape[2]
    dim = emission_projector.shape[2]
    swap_streams = [(0, 1), (1, 0)]
    tied = lambda *arrays: lax.optimization_barrier(arrays)

    own_w = emission_projector[0].reshape(heads * dim, -1)
    side_w = lax.ppermute(
        sideways_coupling_coef[0].reshape(heads * dim, -1), "stream", swap_streams
    )
    fade, tail, *readings = prepare(
        recall_retained_logshare[0],
        recall_store_flags,
        dim,
        1.0 / math.sqrt(dim * length * blocks),
        sizes,
    )
    pieces = [x[first : first + size] for first, size in zip(firsts, sizes)]
    received = []
    for c in range(chunks):
        if c == chunks - 2:
            pieces[c], pieces[c + 1], tail = tied(pieces[c], pieces[c + 1], tail)
        xs = [pieces[c]]
        for k in range(1, shards):
            xs.append(
                lax.ppermute(pieces[c], "head", [((d + k) % shards, d) for d in range(shards)])
            )
        received.append(xs)
    gain = prescale_amplifier
    w = triple_projector[0].reshape(-1, 3 * heads * dim)

    qs, ks, vs, locals_ = [], [], [], []
    summary = None
    for c, first in enumerate(firsts[:-1]):
        q, k, v, summary = qkv(gain, w, fade, summary, received[c], heads, dim, first)
        qs.append(q)
        ks.append(k)
        vs.append(v)
        if c < chunks - 2:
            local = attention(first, tile_retain_grid, score_scaler, q, ks, vs, heads, dim)
            summary, local = tied(summary, local)
            locals_.append(local)
    acc = own_part(gain, w, received[-1][0], heads, dim)
    summary, acc = tied(summary, acc)
    k, v, sent = last_keys_values(
        acc, gain, w, fade, summary, tail, received[-1], heads, dim, firsts[-1]
    )
    ks.append(k)
    vs.append(v)

    quad_size = min(4, blocks)
    loads = [sent] + [
        lax.ppermute(sent, "tm", [(d, d ^ k) for d in range(blocks)]) for k in range(1, quad_size)
    ]
    qs.append(last_queries(gain, w, received[-1], heads, dim))
    for c in range(chunks - 2, chunks):
        locals_.append(
            attention(
                firsts[c], tile_retain_grid, score_scaler, qs[c], ks[: c + 1], vs[: c + 1], heads, dim
            )
        )
    *loads, locals_[-2] = tied(*loads, locals_[-2])
    before, decay, total = quad(loads, heads, dim)
    totals = [
        lax.ppermute(total, "tm", [(d, d + quad_size * k) for d in range(blocks - quad_size * k)])
        for k in range(1, blocks // quad_size)
    ]
    *totals, locals_[-1] = tied(*totals, locals_[-1])
    state = entering(before, decay, totals, heads, dim)

    result = None
    for c in range(chunks):
        head_out = recall(readings[c], qs[c], locals_[c], state, heads, dim)
        side = lax.ppermute(head_out, "stream", swap_streams)
        outs = project(head_out, side, own_w, side_w, shards)
        parts = [outs[0]]
        for k in range(1, shards):
            parts.append(
                lax.ppermute(outs[k], "head", [(d, (d + k) % shards) for d in range(shards)])
            )
        result = finish(parts, result, firsts[c], length)
    return result[None]


def solution(mesh):
    placed = (
        P("stream", "tm", "head"),
        P("stream", None),
        P("stream", None, "head", None),
        P("stream", "head"),
        P("stream", "head", "tm"),
        P("tm", None),
        P("tm"),
        P("stream", "head", None, None),
        P("stream", "head", None, None),
    )
    return jax.shard_map(
        per_device, mesh=mesh, in_specs=placed, out_specs=P("stream", "tm", "head"), check_vma=False
    )
```
